128 devices in a mesh: phase: 2 (over core), dp: 16 (over y, x), mp: 4 (over z).
Axes of the slice: x: 4, y: 4, z: 4, core: 2. Of those that a mesh axis runs over, the one named last changes fastest.
Arguments:
- queries: bfloat16 [16384, 2048], P(('phase', 'dp'), 'mp'), may hold values from -150 to 150
- grad_out: bfloat16 [16384, 2048], P(('phase', 'dp'), 'mp'), may hold values from -6 to 6
- encoded: bfloat16 [256, 128, 4096], P(('phase', 'dp'), None, 'mp'), may hold values from -6 to 6
- key_weight: bfloat16 [4096, 2048], P(None, 'mp'), may hold values from -0.09375 to 0.09375
- value_weight: bfloat16 [4096, 2048], P(None, 'mp'), may hold values from -0.09375 to 0.09375
- send_rows: int32 [32, 32, 1], P(('phase', 'dp')), may hold values from 0 to 7, as said below
- read_slots: int32 [256, 2], P(('phase', 'dp')), may hold values from 0 to 31, as said below
Outputs:
- attended: bfloat16 [16384, 2048], P(('phase', 'dp'), 'mp')
- grad_q: bfloat16 [16384, 2048], P(('phase', 'dp'), 'mp')
- grad_e: bfloat16 [256, 128, 4096], P(('phase', 'dp'), None, 'mp')
The draws below stay inside these ranges and needn't reach their ends.
Inputs may be any that keep to these rules, and one draw needn't show every extreme that they name: send_rows[o, r, c] is a local row (below 8) of owner o's neighbours; one row may be sent to several readers and in several slots; slots that no span of reader r reads hold 0. `read_slots`: all 16 entries of one reader's spans name different slots; every reader fills all 1 slots of at least one owner.
All inputs are finite; a program needn't handle non-finite values.
Results may differ from the reference program's by a relative error of at most 0.013.
Values may be sent and summed in bfloat16 or wider, within the bound.
A program may use at most 128 MiB of HBM per device.

```python
import jax
import jax.numpy as jnp
from jax import lax

D = 4096
HEADS = 16
HS = 128
CLEN = 64
NLEN = 128
SPAN_DEV = 8
NB_DEV = 8
STEP_REPLICA_SETS = 32
CAP = 1
CONSUMER_PLACES = 32
TOKENS = 16384
NEIGH = 256


def plan_reads(key):
    reads = 2 * SPAN_DEV
    key_reorder, key_forcing, lookup_added_merit, key_row_list, key_ranking = jax.random.split(key, 5)
    shuffled_orderings = jax.vmap(lambda sub: jax.random.permutation(sub, CONSUMER_PLACES))(jax.random.split(key_reorder, STEP_REPLICA_SETS)).astype(jnp.int32)
    forced_owner = jax.random.randint(key_forcing, (STEP_REPLICA_SETS,), 0, STEP_REPLICA_SETS)
    position_occupant = jnp.arange(CONSUMER_PLACES, dtype=jnp.int32) // CAP
    mandated_pick = (position_occupant[None, :] == forced_owner[:, None]).astype(jnp.int32)
    merit_increment = jax.random.randint(lookup_added_merit, (STEP_REPLICA_SETS,), 0, 2)
    merit_grid = mandated_pick * (4 * CONSUMER_PLACES * CONSUMER_PLACES) + merit_increment[position_occupant][None, :] * (CONSUMER_PLACES // 2 + 1) * CONSUMER_PLACES + shuffled_orderings
    live_slots = jax.lax.top_k(merit_grid, reads)[1].astype(jnp.int32)
    local_rows = jax.random.randint(key_row_list, (STEP_REPLICA_SETS, reads), 0, NB_DEV)
    table = jnp.zeros((STEP_REPLICA_SETS, CONSUMER_PLACES), jnp.int32)
    table = table.at[jnp.arange(STEP_REPLICA_SETS)[:, None], live_slots].set(local_rows)
    send_table = jnp.transpose(table.reshape(STEP_REPLICA_SETS, STEP_REPLICA_SETS, CAP), (1, 0, 2))
    orders = jax.vmap(lambda sub: jax.random.permutation(sub, reads))(jax.random.split(key_ranking, STEP_REPLICA_SETS))
    slot_table = jnp.take_along_axis(live_slots, orders, 1).reshape(STEP_REPLICA_SETS * SPAN_DEV, 2)
    return (send_table.astype(jnp.int32), slot_table.astype(jnp.int32))


def draw_send_rows(key, part):
    return plan_reads(key)[0]


def draw_read_slots(key, part):
    return plan_reads(key)[1]


def draw_queries(key, part):
    key = jax.random.fold_in(key, 7)
    key_base = jax.random.fold_in(key, 0)
    values_out = jnp.clip(jax.random.normal(key_base, (TOKENS, HEADS * HS), jnp.float32), -6.0, 6.0)
    return values_out.astype(jnp.bfloat16)


def shard_levels(own_key, dims, shards, least, largest):
    loudness = 1.0
    for position, blocks in shards:
        draws = jax.random.uniform(jax.random.fold_in(jax.random.fold_in(own_key, 6), position), (blocks,), jnp.float32, least / len(shards), largest / len(shards))
        loudness = loudness * jnp.repeat(jnp.exp(draws), dims[position] // blocks).reshape((-1,) + (1,) * (len(dims) - 1 - position))
    return loudness


def normal_values(own_key, shape, spread, reach, cuts=(), kind=jnp.bfloat16):
    values = spread * jax.random.normal(own_key, shape, jnp.float32)
    if cuts:
        values = values * shard_levels(own_key, shape, cuts, -0.22, 0.18)
    return jnp.clip(values, -reach, reach).astype(kind)


def setup_inputs(seed: int = 0) -> dict:
    arg_keys = jax.random.split(jax.random.key(seed), 8)
    queries = draw_queries(jax.random.fold_in(arg_keys[7], 71), 0)
    grad_out = normal_values(arg_keys[1], (TOKENS, HEADS * HS), 1.0, 6.0, ((0, 32), (1, 4)))
    encoded = normal_values(arg_keys[2], (NEIGH, NLEN, D), 1.0, 6.0, ((0, 32), (2, 4)))
    key_weight = normal_values(arg_keys[3], (D, HEADS * HS), D ** -0.5, 0.09375, ((1, 4),))
    value_weight = normal_values(arg_keys[4], (D, HEADS * HS), D ** -0.5, 0.09375, ((1, 4),))
    send_rows = draw_send_rows(jax.random.fold_in(arg_keys[7], 71), 0)
    read_slots = draw_read_slots(jax.random.fold_in(arg_keys[7], 71), 0)
    return dict(queries=queries, grad_out=grad_out, encoded=encoded, key_weight=key_weight, value_weight=value_weight, send_rows=send_rows, read_slots=read_slots)


def rounded(values_in):
    return lax.optimization_barrier(values_in.astype(jnp.bfloat16)).astype(jnp.float32)


def reference(queries, grad_out, encoded, key_weight, value_weight, send_rows, read_slots):
    scaling = HS ** -0.5
    span_total = TOKENS // CLEN
    rows_flat = encoded.reshape(NEIGH * NLEN, D)
    keys = jnp.dot(rows_flat, key_weight, preferred_element_type=jnp.float32).astype(jnp.bfloat16).reshape(NEIGH, NLEN, HEADS, HS)
    values = jnp.dot(rows_flat, value_weight, preferred_element_type=jnp.float32).astype(jnp.bfloat16).reshape(NEIGH, NLEN, HEADS, HS)
    reader = (jnp.arange(span_total, dtype=jnp.int32) // SPAN_DEV).astype(jnp.int32)
    owner_id = (read_slots // CAP).astype(jnp.int32)
    cell_index = (read_slots % CAP).astype(jnp.int32)
    local_row = send_rows[owner_id, reader[:, None], cell_index]
    neighbour = (owner_id * NB_DEV + local_row).astype(jnp.int32)
    query_blocks = queries.reshape(span_total, CLEN, HEADS, HS).astype(jnp.float32)
    key_blocks = keys[neighbour].astype(jnp.float32)
    value_blocks = values[neighbour].astype(jnp.float32)
    scores = jnp.einsum("cqhd,cjkhd->cjhqk", query_blocks, key_blocks) * scaling
    peaks = jnp.max(scores, -1)
    weights = jnp.exp(scores - peaks[..., None])
    totals = jnp.sum(weights, -1)
    partial_out = jnp.einsum("cjhqk,cjkhd->cjqhd", rounded(weights), value_blocks)
    overall = jnp.max(peaks, 1)
    factors = jnp.exp(peaks - overall[:, None])
    denominator = jnp.sum(factors * totals, 1)
    blended = jnp.sum(jnp.swapaxes(factors, 2, 3)[..., None] * partial_out, 1) / jnp.swapaxes(denominator, 1, 2)[..., None]
    attended = blended.reshape(TOKENS, HEADS * HS).astype(jnp.bfloat16)
    log_totals = overall + jnp.log(denominator)
    grad_blocks = grad_out.reshape(span_total, CLEN, HEADS, HS).astype(jnp.float32)
    correction = jnp.swapaxes(jnp.sum(grad_blocks * blended, -1), 1, 2)
    probs = jnp.exp(scores - log_totals[:, None, :, :, None])
    grad_v_read = jnp.einsum("cjhqk,cqhd->cjkhd", rounded(probs), grad_blocks).astype(jnp.bfloat16)
    grad_p = jnp.einsum("cqhd,cjkhd->cjhqk", grad_blocks, value_blocks)
    grad_s = rounded(probs * (grad_p - correction[:, None, :, :, None]))
    grad_q = (jnp.einsum("cjhqk,cjkhd->cqhd", grad_s, key_blocks) * scaling).reshape(TOKENS, HEADS * HS).astype(jnp.bfloat16)
    grad_k_read = (jnp.einsum("cjhqk,cqhd->cjkhd", grad_s, query_blocks) * scaling).astype(jnp.bfloat16)
    flat_ids = neighbour.reshape(span_total * 2)
    grad_k = jax.ops.segment_sum(grad_k_read.astype(jnp.float32).reshape(span_total * 2, NLEN * HEADS * HS), flat_ids, NEIGH)
    grad_v = jax.ops.segment_sum(grad_v_read.astype(jnp.float32).reshape(span_total * 2, NLEN * HEADS * HS), flat_ids, NEIGH)
    grad_k = grad_k.astype(jnp.bfloat16).reshape(NEIGH * NLEN, HEADS * HS)
    grad_v = grad_v.astype(jnp.bfloat16).reshape(NEIGH * NLEN, HEADS * HS)
    grad_e = jnp.dot(grad_k, key_weight.T, preferred_element_type=jnp.float32) + jnp.dot(grad_v, value_weight.T, preferred_element_type=jnp.float32)
    return attended, grad_q, grad_e.reshape(NEIGH, NLEN, D).astype(jnp.bfloat16)
```

```python
import functools

import jax
import jax.numpy as jnp
from jax import lax
from jax.experimental import pallas as pl
from jax.experimental.pallas import tpu as pltpu
from jax.sharding import PartitionSpec as P

HS = 128
CLEN = 64
NLEN = 128
SCALE = HS ** (-0.5)
LAST = (((1,), (1,)), ((), ()))
FIRST = (((0,), (0,)), ((), ()))
MESH = pl.DeviceIdType.MESH
F32 = jnp.float32
BF16 = jnp.bfloat16


def group_index():
    return lax.axis_index("phase") * lax.axis_size("dp") + lax.axis_index("dp")


def peer_id(group):
    dp = lax.axis_size("dp")
    return {"phase": group // dp, "dp": lax.rem(group, dp)}


def greet_group(barrier, groups):
    me = group_index()

    def greet(k, carry):
        pl.semaphore_signal(
            barrier, inc=1, device_id=peer_id(lax.rem(me + k, groups)), device_id_type=MESH
        )
        return carry

    lax.fori_loop(1, groups, greet, 0)


def send_to_group(groups, source, target, send_sem, recv_sem):
    me = group_index()

    def copy_to(k):
        peer = lax.rem(me + k, groups)
        return pltpu.make_async_remote_copy(
            src_ref=source(peer),
            dst_ref=target.at[me],
            send_sem=send_sem.at[k],
            recv_sem=recv_sem.at[k],
            device_id=peer_id(peer),
            device_id_type=MESH,
        )

    def copy_from(k):
        peer = lax.rem(me + groups - k, groups)
        return pltpu.make_async_remote_copy(
            src_ref=source(peer),
            dst_ref=target.at[peer],
            send_sem=send_sem.at[k],
            recv_sem=recv_sem.at[k],
            device_id=peer_id(peer),
            device_id_type=MESH,
        )

    def start():
        lax.fori_loop(1, groups, lambda k, c: (copy_to(k).start(), c)[1], 0)

    def wait():
        def one(k, carry):
            copy_from(k).wait_recv()
            copy_to(k).wait_send()
            return carry

        lax.fori_loop(1, groups, one, 0)

    return start, wait


def project_kernel(
    groups, plan, queries, grads, encoded, key_weight, value_weight,
    keys, values, slots,
    outgoing, own, before, after, far, key_w, value_w, key_acc, value_acc,
    load_sem, ring_send, ring_recv, send_sem, recv_sem, local_sem,
):
    me = group_index()
    z = lax.axis_index("mp")
    ring = lax.axis_size("mp")
    up, down = lax.rem(z + 1, ring), lax.rem(z + ring - 1, ring)
    across = lax.rem(z + 2, ring)
    blocks = encoded.shape[0]
    half = blocks // 2

    barrier = pltpu.get_barrier_semaphore()
    pl.semaphore_signal(barrier, inc=1, device_id={"mp": up}, device_id_type=MESH)
    pl.semaphore_signal(barrier, inc=1, device_id={"mp": down}, device_id_type=MESH)
    greet_group(barrier, groups)

    own_load = pltpu.make_async_copy(encoded, own, load_sem.at[0])
    own_load.start()
    weight_loads = []
    for i, owner in enumerate((z, down, up, across)):
        pair = (
            pltpu.make_async_copy(key_weight.at[owner], key_w.at[i], load_sem.at[1 + 2 * i]),
            pltpu.make_async_copy(value_weight.at[owner], value_w.at[i], load_sem.at[2 + 2 * i]),
        )
        for load in pair:
            load.start()
        weight_loads.append(pair)

    def fill(o, carry):
        span = plan[groups + o]
        live = plan[2 * groups + o] > 0
        outgoing[o, 0] = jnp.where(live, queries[span], jnp.zeros_like(queries[span]))
        outgoing[o, 1] = jnp.where(live, grads[span], jnp.zeros_like(grads[span]))
        return carry

    lax.fori_loop(0, groups, fill, 0)

    def ring_copy(lane, source, target, block, to):
        return pltpu.make_async_remote_copy(
            src_ref=source.at[block],
            dst_ref=target.at[block],
            send_sem=ring_send.at[lane, block],
            recv_sem=ring_recv.at[lane, block],
            device_id={"mp": to},
            device_id_type=MESH,
        )

    def go_up(c):
        return ring_copy(0, encoded, before, c, up)

    def go_down(c):
        return ring_copy(1, encoded, after, c, down)

    def pass_up(c):
        return ring_copy(2, before, far, c, up)

    def pass_down(c):
        return ring_copy(2, after, far, c, down)

    pl.semaphore_wait(barrier, groups - 1 + 2)

    def send_own(c, carry):
        go_up(c).start()
        go_down(blocks - 1 - c).start()
        return carry

    lax.fori_loop(0, blocks, send_own, 0)
    start_slots, wait_slots = send_to_group(
        groups, lambda g: outgoing.at[g], slots, send_sem, recv_sem
    )
    start_slots()
    local = pltpu.make_async_copy(outgoing.at[me], slots.at[me], local_sem)
    local.start()

    def project(block, i):
        return (
            jnp.dot(block, key_w[i], preferred_element_type=F32),
            jnp.dot(block, value_w[i], preferred_element_type=F32),
        )

    def add(source, c, i):
        k, v = project(source[c], i)
        key_acc[c] += k
        value_acc[c] += v

    def finish(c):
        k, v = project(far[c], 3)
        keys[c] = (key_acc[c] + k).astype(BF16)
        values[c] = (value_acc[c] + v).astype(BF16)

    own_load.wait()
    for load in weight_loads[0]:
        load.wait()

    def first(c, carry):
        k, v = project(own[c], 0)
        key_acc[c] = k
        value_acc[c] = v
        return carry

    lax.fori_loop(0, blocks, first, 0)
    for pair in weight_loads[1:]:
        for load in pair:
            load.wait()

    def near(c, carry):
        d = blocks - 1 - c
        go_up(c).wait_recv()
        pass_up(c).start()
        go_down(d).wait_recv()
        pass_down(d).start()
        add(before, c, 1)
        add(after, d, 2)
        return carry

    lax.fori_loop(0, half, near, 0)

    def rest(c, carry):
        d = blocks - 1 - c
        go_up(c).wait_recv()
        add(before, c, 1)
        go_down(d).wait_recv()
        add(after, d, 2)
        return carry

    lax.fori_loop(half, blocks, rest, 0)

    def last(c, carry):
        d = blocks - 1 - c
        pass_up(c).wait_recv()
        finish(c)
        pass_down(d).wait_recv()
        finish(d)
        return carry

    lax.fori_loop(0, half, last, 0)

    def sent(c, carry):
        go_up(c).wait_send()
        go_down(c).wait_send()
        return carry

    lax.fori_loop(0, blocks, sent, 0)

    def passed(c, carry):
        pass_up(c).wait_send()
        pass_down(blocks - 1 - c).wait_send()
        return carry

    lax.fori_loop(0, half, passed, 0)
    wait_slots()
    local.wait()


def pair_operands(plan, pair, keys, values, slots, first, h):
    cols = pl.ds(h * HS, HS)
    top = lax.broadcasted_iota(jnp.int32, (2 * CLEN, HS), 0) < CLEN
    low, high = plan[2 * pair], plan[2 * pair + 1]

    def diagonal(which):
        block = slots[pl.ds(first, 2), which, :, cols].reshape(2 * CLEN, HS)
        zero = jnp.zeros_like(block)
        return jnp.concatenate([jnp.where(top, block, zero), jnp.where(top, zero, block)], 1)

    k = jnp.concatenate([keys[low, :, cols], keys[high, :, cols]], 1)
    v = jnp.concatenate([values[low, :, cols], values[high, :, cols]], 1)
    return k, v, diagonal(0), diagonal(1)


def attend_kernel(
    groups, plan, keys, values, slots, factors,
    stats, fetched, combined, back, landed,
    stat_send, stat_recv, back_send, back_recv, local_sem,
):
    me = group_index()
    heads = keys.shape[2] // HS
    spans = combined.shape[0]
    barrier = pltpu.get_barrier_semaphore()
    greet_group(barrier, groups)

    def one_pair(p, carry):
        for h in range(heads):
            k, v, q, g = pair_operands(plan, p, keys, values, slots, 2 * p, h)
            scores = lax.dot_general(k, q, LAST, preferred_element_type=F32) * SCALE
            grad_p = lax.dot_general(v, g, LAST, preferred_element_type=F32)
            peak = jnp.max(scores, 0, keepdims=True)
            weights = jnp.exp(scores - peak)
            stats[p, h : h + 1] = peak
            stats[p, heads + h : heads + h + 1] = jnp.sum(weights, 0, keepdims=True)
            stats[p, 2 * heads + h : 2 * heads + h + 1] = jnp.sum(
                weights * grad_p, 0, keepdims=True
            )
        stats[p, 3 * heads :] = jnp.zeros((stats.shape[1] - 3 * heads, 2 * CLEN), F32)
        return carry

    lax.fori_loop(0, groups // 2, one_pair, 0)
    pl.semaphore_wait(barrier, groups - 1)

    start, wait = send_to_group(
        groups, lambda g: stats.at[g // 2], fetched, stat_send, stat_recv
    )
    start()
    local = pltpu.make_async_copy(stats.at[me // 2], fetched.at[me], local_sem.at[0])
    local.start()
    local.wait()
    wait()

    def combine(t, carry):
        a = fetched[plan[3 * groups + 2 * t]]
        b = fetched[plan[3 * groups + 2 * t + 1]]
        overall = jnp.maximum(a[:heads], b[:heads])
        fa, fb = jnp.exp(a[:heads] - overall), jnp.exp(b[:heads] - overall)
        total = fa * a[heads : 2 * heads] + fb * b[heads : 2 * heads]
        grad = fa * a[2 * heads : 3 * heads] + fb * b[2 * heads : 3 * heads]
        combined[t, :heads] = overall + jnp.log(total)
        combined[t, heads:] = grad / total
        return carry

    lax.fori_loop(0, spans, combine, 0)

    def answer(o, carry):
        mine = combined[plan[groups + o]]
        back[o] = jnp.where(plan[2 * groups + o] > 0, mine, jnp.zeros_like(mine))
        return carry

    lax.fori_loop(0, groups, answer, 0)
    start, wait = send_to_group(groups, lambda g: back.at[g], landed, back_send, back_recv)
    start()
    local = pltpu.make_async_copy(back.at[me], landed.at[me], local_sem.at[1])
    local.start()
    local.wait()
    wait()
    left = lax.broadcasted_iota(jnp.int32, factors.shape[1:], 1) < CLEN

    def merge(p, carry):
        factors[p] = jnp.where(left, landed[2 * p], landed[2 * p + 1])
        return carry

    lax.fori_loop(0, groups // 2, merge, 0)


def grads_kernel(
    pairs, plan, factors, keys, values, slots, results, grad_keys, grad_values, key_acc, value_acc
):
    heads = keys.shape[2] // HS
    step = pl.program_id(0)

    @pl.when(step == 0)
    def _():
        key_acc[...] = jnp.zeros_like(key_acc)
        value_acc[...] = jnp.zeros_like(value_acc)

    top = lax.broadcasted_iota(jnp.int32, (2 * CLEN, HS), 0) < CLEN

    def one_pair(i, carry):
        p = step * pairs + i
        low, high = plan[2 * p], plan[2 * p + 1]
        for h in range(heads):
            cols = pl.ds(h * HS, HS)
            k, v, q, g = pair_operands(plan, p, keys, values, slots, 2 * i, h)
            scores = lax.dot_general(k, q, LAST, preferred_element_type=F32) * SCALE
            grad_p = lax.dot_general(v, g, LAST, preferred_element_type=F32)
            probs = jnp.exp(scores - factors[i, h : h + 1])
            grad_s = (probs * (grad_p - factors[i, heads + h : heads + h + 1])).astype(BF16)
            probs = probs.astype(BF16)
            grad_v = jnp.dot(probs, g, preferred_element_type=F32)
            grad_k = jnp.dot(grad_s, q, preferred_element_type=F32) * SCALE
            key_acc[low, :, cols] += grad_k[:, :HS]
            key_acc[high, :, cols] += grad_k[:, HS:]
            value_acc[low, :, cols] += grad_v[:, :HS]
            value_acc[high, :, cols] += grad_v[:, HS:]
            out = lax.dot_general(probs, v, FIRST, preferred_element_type=F32)
            grad_q = lax.dot_general(grad_s, k, FIRST, preferred_element_type=F32) * SCALE
            for j, both in enumerate((out, grad_q)):
                picked = jnp.where(top, both[:, :HS], both[:, HS:]).astype(BF16)
                results[pl.ds(2 * i, 2), j, :, cols] = picked.reshape(2, CLEN, HS)
        return carry

    lax.fori_loop(0, pairs, one_pair, 0)

    @pl.when(step == pl.num_programs(0) - 1)
    def _():
        grad_keys[...] = key_acc[...].astype(BF16)
        grad_values[...] = value_acc[...].astype(BF16)


def reduce_kernel(
    groups, plan, results, grad_keys, grad_values, key_weight, value_weight,
    attended, grad_q, grad_e,
    fetched, key_w, value_w, to_across, to_up, to_down, from_far, before, after, total,
    load_sem, ring_send, ring_recv, send_sem, recv_sem, local_sem,
):
    me = group_index()
    z = lax.axis_index("mp")
    ring = lax.axis_size("mp")
    up, down = lax.rem(z + 1, ring), lax.rem(z + ring - 1, ring)
    across = lax.rem(z + 2, ring)
    blocks = grad_keys.shape[0]
    half = blocks // 2
    spans = attended.shape[0]

    barrier = pltpu.get_barrier_semaphore()
    pl.semaphore_signal(barrier, inc=1, device_id={"mp": up}, device_id_type=MESH)
    pl.semaphore_signal(barrier, inc=1, device_id={"mp": down}, device_id_type=MESH)
    weight_loads = []
    for i, owner in enumerate((across, up, down, z)):
        pair = (
            pltpu.make_async_copy(key_weight.at[owner], key_w.at[i], load_sem.at[2 * i]),
            pltpu.make_async_copy(value_weight.at[owner], value_w.at[i], load_sem.at[2 * i + 1]),
        )
        for load in pair:
            load.start()
        weight_loads.append(pair)
    greet_group(barrier, groups)

    def part(c, i):
        return lax.dot_general(
            grad_keys[c], key_w[i], LAST, preferred_element_type=F32
        ) + lax.dot_general(grad_values[c], value_w[i], LAST, preferred_element_type=F32)

    def ring_copy(lane, source, target, block, to):
        return pltpu.make_async_remote_copy(
            src_ref=source.at[block],
            dst_ref=target.at[block],
            send_sem=ring_send.at[lane, block],
            recv_sem=ring_recv.at[lane, block],
            device_id={"mp": to},
            device_id_type=MESH,
        )

    def far_up(c):
        return ring_copy(2, to_across, from_far, c, up)

    def far_down(c):
        return ring_copy(2, to_across, from_far, c, down)

    def go_up(c):
        return ring_copy(0, to_up, before, c, up)

    def go_down(c):
        return ring_copy(1, to_down, after, c, down)

    pl.semaphore_wait(barrier, groups - 1 + 2)
    for load in weight_loads[0]:
        load.wait()

    def send_far(c, carry):
        d = blocks - 1 - c
        to_across[c] = part(c, 0).astype(BF16)
        far_up(c).start()
        to_across[d] = part(d, 0).astype(BF16)
        far_down(d).start()
        return carry

    lax.fori_loop(0, half, send_far, 0)
    start_results, wait_results = send_to_group(
        groups, lambda g: results.at[g], fetched, send_sem, recv_sem
    )
    start_results()
    local = pltpu.make_async_copy(results.at[me], fetched.at[me], local_sem)
    local.start()
    for pair in weight_loads[1:]:
        for load in pair:
            load.wait()

    def send_near(c, carry):
        d = blocks - 1 - c
        to_up[c] = part(c, 1).astype(BF16)
        go_up(c).start()
        to_down[d] = part(d, 2).astype(BF16)
        go_down(d).start()
        return carry

    lax.fori_loop(half, blocks, send_near, 0)

    def send_joined(c, carry):
        d = blocks - 1 - c
        mine = part(c, 1)
        far_up(c).wait_recv()
        to_up[c] = (mine + from_far[c].astype(F32)).astype(BF16)
        go_up(c).start()
        mine = part(d, 2)
        far_down(d).wait_recv()
        to_down[d] = (mine + from_far[d].astype(F32)).astype(BF16)
        go_down(d).start()
        return carry

    lax.fori_loop(0, half, send_joined, 0)

    def own(c, carry):
        total[c] = part(c, 3)
        return carry

    lax.fori_loop(0, blocks, own, 0)

    def add_first(c, carry):
        d = blocks - 1 - c
        go_up(c).wait_recv()
        total[c] += before[c].astype(F32)
        go_down(d).wait_recv()
        total[d] += after[d].astype(F32)
        return carry

    lax.fori_loop(half, blocks, add_first, 0)
    local.wait()
    wait_results()

    def finish_span(t, carry):
        a = plan[3 * groups + 2 * t]
        b = plan[3 * groups + 2 * t + 1]
        attended[t] = (fetched[a, 0].astype(F32) + fetched[b, 0].astype(F32)).astype(BF16)
        grad_q[t] = (fetched[a, 1].astype(F32) + fetched[b, 1].astype(F32)).astype(BF16)
        return carry

    lax.fori_loop(0, spans, finish_span, 0)

    def add_last(c, carry):
        d = blocks - 1 - c
        go_up(c).wait_recv()
        grad_e[c] = (total[c] + before[c].astype(F32)).astype(BF16)
        go_down(d).wait_recv()
        grad_e[d] = (total[d] + after[d].astype(F32)).astype(BF16)
        return carry

    lax.fori_loop(0, half, add_last, 0)

    def sent(c, carry):
        go_up(c).wait_send()
        go_down(c).wait_send()
        return carry

    lax.fori_loop(0, blocks, sent, 0)

    def sent_far(c, carry):
        far_up(c).wait_send()
        far_down(blocks - 1 - c).wait_send()
        return carry

    lax.fori_loop(0, half, sent_far, 0)


def params(collective_id=None, mib=56):
    return pltpu.CompilerParams(
        collective_id=collective_id,
        has_side_effects=collective_id is not None,
        vmem_limit_bytes=mib << 20,
    )


def body(queries, grad_out, encoded, key_weight, value_weight, send_rows, read_slots):
    groups = lax.axis_size(("phase", "dp"))
    ring = lax.axis_size("mp")
    blocks, _, features = encoded.shape
    width = key_weight.shape[1]
    heads = width // HS
    spans = read_slots.shape[0]
    hbm = pl.BlockSpec(memory_space=pl.ANY)
    vmem = pl.BlockSpec(memory_space=pltpu.VMEM)
    smem = pl.BlockSpec(memory_space=pltpu.SMEM)
    dma = pltpu.SemaphoreType.DMA

    reads = read_slots.reshape(2 * spans)
    matches = reads[None, :] == jnp.arange(groups, dtype=jnp.int32)[:, None]
    source = jnp.sum(
        jnp.where(matches, jnp.arange(2 * spans, dtype=jnp.int32)[None, :] // 2, 0), 1
    )
    live = jnp.any(matches, 1).astype(jnp.int32)
    plan = jnp.concatenate([send_rows.reshape(groups), source, live, reads])

    query_spans = queries.reshape(spans, CLEN, width)
    grad_spans = grad_out.reshape(spans, CLEN, width)
    key_parts = key_weight.reshape(ring, features, width)
    value_parts = value_weight.reshape(ring, features, width)

    keys, values, slots = pl.pallas_call(
        functools.partial(project_kernel, groups),
        out_shape=(
            jax.ShapeDtypeStruct((blocks, NLEN, width), BF16),
            jax.ShapeDtypeStruct((blocks, NLEN, width), BF16),
            jax.ShapeDtypeStruct((groups, 2, CLEN, width), BF16),
        ),
        in_specs=[smem, vmem, vmem, hbm, hbm, hbm],
        out_specs=(vmem, vmem, hbm),
        scratch_shapes=[
            pltpu.VMEM((groups, 2, CLEN, width), BF16),
            pltpu.VMEM(encoded.shape, BF16),
            pltpu.VMEM(encoded.shape, BF16),
            pltpu.VMEM(encoded.shape, BF16),
            pltpu.VMEM(encoded.shape, BF16),
            pltpu.VMEM(key_parts.shape, BF16),
            pltpu.VMEM(key_parts.shape, BF16),
            pltpu.VMEM((blocks, NLEN, width), F32),
            pltpu.VMEM((blocks, NLEN, width), F32),
            dma((9,)),
            dma((3, blocks)),
            dma((3, blocks)),
            dma((groups,)),
            dma((groups,)),
            dma,
        ],
        compiler_params=params(0),
        name="project",
    )(plan, query_spans, grad_spans, encoded, key_parts, value_parts)

    stat_rows = 16
    factors = pl.pallas_call(
        functools.partial(attend_kernel, groups),
        out_shape=jax.ShapeDtypeStruct((groups // 2, 2 * heads, 2 * CLEN), F32),
        in_specs=[smem, vmem, vmem, vmem],
        out_specs=vmem,
        scratch_shapes=[
            pltpu.VMEM((groups // 2, stat_rows, 2 * CLEN), F32),
            pltpu.VMEM((groups, stat_rows, 2 * CLEN), F32),
            pltpu.VMEM((spans, 2 * heads, 2 * CLEN), F32),
            pltpu.VMEM((groups, 2 * heads, 2 * CLEN), F32),
            pltpu.VMEM((groups, 2 * heads, 2 * CLEN), F32),
            dma((groups,)),
            dma((groups,)),
            dma((groups,)),
            dma((groups,)),
            dma((2,)),
        ],
        compiler_params=params(1),
        name="attend",
    )(plan, keys, values, slots)

    steps = 4
    pairs = groups // 2 // steps
    whole = pl.BlockSpec((blocks, NLEN, width), lambda i, plan: (0, 0, 0))
    per_step = pl.BlockSpec((2 * pairs, 2, CLEN, width), lambda i, plan: (i, 0, 0, 0))
    results, grad_keys, grad_values = pl.pallas_call(
        functools.partial(grads_kernel, pairs),
        out_shape=(
            jax.ShapeDtypeStruct((groups, 2, CLEN, width), BF16),
            jax.ShapeDtypeStruct((blocks, NLEN, width), BF16),
            jax.ShapeDtypeStruct((blocks, NLEN, width), BF16),
        ),
        grid_spec=pltpu.PrefetchScalarGridSpec(
            num_scalar_prefetch=1,
            grid=(steps,),
            in_specs=[
                pl.BlockSpec((pairs, 2 * heads, 2 * CLEN), lambda i, plan: (i, 0, 0)),
                whole,
                whole,
                per_step,
            ],
            out_specs=(per_step, whole, whole),
            scratch_shapes=[
                pltpu.VMEM((blocks, NLEN, width), F32),
                pltpu.VMEM((blocks, NLEN, width), F32),
            ],
        ),
        compiler_params=params(),
        name="grads",
    )(plan, factors, keys, values, slots)

    attended, grad_q, grad_e = pl.pallas_call(
        functools.partial(reduce_kernel, groups),
        out_shape=(
            jax.ShapeDtypeStruct((spans, CLEN, width), BF16),
            jax.ShapeDtypeStruct((spans, CLEN, width), BF16),
            jax.ShapeDtypeStruct(encoded.shape, BF16),
        ),
        in_specs=[smem, hbm, vmem, vmem, hbm, hbm],
        out_specs=(vmem, vmem, vmem),
        scratch_shapes=[
            pltpu.VMEM((groups, 2, CLEN, width), BF16),
            pltpu.VMEM(key_parts.shape, BF16),
            pltpu.VMEM(key_parts.shape, BF16),
            pltpu.VMEM(encoded.shape, BF16),
            pltpu.VMEM(encoded.shape, BF16),
            pltpu.VMEM(encoded.shape, BF16),
            pltpu.VMEM(encoded.shape, BF16),
            pltpu.VMEM(encoded.shape, BF16),
            pltpu.VMEM(encoded.shape, BF16),
            pltpu.VMEM(encoded.shape, F32),
            dma((8,)),
            dma((3, blocks)),
            dma((3, blocks)),
            dma((groups,)),
            dma((groups,)),
            dma,
        ],
        compiler_params=params(2),
        name="reduce",
    )(plan, results, grad_keys, grad_values, key_parts, value_parts)
    return (attended.reshape(queries.shape), grad_q.reshape(queries.shape), grad_e)


def solution(mesh):
    return jax.shard_map(
        body,
        mesh=mesh,
        in_specs=(
            P(("phase", "dp"), "mp"),
            P(("phase", "dp"), "mp"),
            P(("phase", "dp"), None, "mp"),
            P(None, "mp"),
            P(None, "mp"),
            P(("phase", "dp"), None, None),
            P(("phase", "dp"), None),
        ),
        out_specs=(
            P(("phase", "dp"), "mp"),
            P(("phase", "dp"), "mp"),
            P(("phase", "dp"), None, "mp"),
        ),
        check_vma=False,
    )
```

```python
import functools

import jax
import jax.numpy as jnp
from jax import lax
from jax.experimental import pallas as pl
from jax.experimental.pallas import tpu as pltpu
from jax.sharding import PartitionSpec as P

HS = 128
CLEN = 64
NLEN = 128
SCALE = HS ** (-0.5)
LAST = (((1,), (1,)), ((), ()))
FIRST = (((0,), (0,)), ((), ()))
MESH = pl.DeviceIdType.MESH
F32 = jnp.float32
BF16 = jnp.bfloat16


def group_index():
    return lax.axis_index("phase") * lax.axis_size("dp") + lax.axis_index("dp")


def peer_id(group):
    dp = lax.axis_size("dp")
    return {"phase": group // dp, "dp": lax.rem(group, dp)}


def greet_group(barrier, groups):
    me = group_index()

    def greet(k, carry):
        pl.semaphore_signal(
            barrier, inc=1, device_id=peer_id(lax.rem(me + k, groups)), device_id_type=MESH
        )
        return carry

    lax.fori_loop(1, groups, greet, 0)


def send_to_group(groups, source, target, send_sem, recv_sem):
    me = group_index()

    def copy_to(k):
        peer = lax.rem(me + k, groups)
        return pltpu.make_async_remote_copy(
            src_ref=source(peer),
            dst_ref=target.at[me],
            send_sem=send_sem.at[k],
            recv_sem=recv_sem.at[k],
            device_id=peer_id(peer),
            device_id_type=MESH,
        )

    def copy_from(k):
        peer = lax.rem(me + groups - k, groups)
        return pltpu.make_async_remote_copy(
            src_ref=source(peer),
            dst_ref=target.at[peer],
            send_sem=send_sem.at[k],
            recv_sem=recv_sem.at[k],
            device_id=peer_id(peer),
            device_id_type=MESH,
        )

    def start():
        lax.fori_loop(1, groups, lambda k, c: (copy_to(k).start(), c)[1], 0)

    def wait():
        def one(k, carry):
            copy_from(k).wait_recv()
            copy_to(k).wait_send()
            return carry

        lax.fori_loop(1, groups, one, 0)

    return start, wait


def diagonal(slots, first, which, cols):
    top = lax.broadcasted_iota(jnp.int32, (2 * CLEN, HS), 0) < CLEN
    block = slots[pl.ds(first, 2), which, :, cols].reshape(2 * CLEN, HS)
    zero = jnp.zeros_like(block)
    return jnp.concatenate([jnp.where(top, block, zero), jnp.where(top, zero, block)], 1)


def pair_operands(rows, pair, keys, values, slots, first, h):
    cols = pl.ds(h * HS, HS)
    low, high = rows[0, 2 * pair], rows[0, 2 * pair + 1]
    k = jnp.concatenate([keys[low, :, cols], keys[high, :, cols]], 1)
    v = jnp.concatenate([values[low, :, cols], values[high, :, cols]], 1)
    return k, v, diagonal(slots, first, 0, cols), diagonal(slots, first, 1, cols)


def project_kernel(
    groups, rows, reads, queries, grads, encoded, key_weight, value_weight,
    keys, values, slots_out, probs, grad_s,
    source, live, outgoing, slots, own, before, after, far, key_w, value_w, key_acc, value_acc,
    stats, fetched, combined, back, landed, weights, grad_p,
    load_sem, ring_send, ring_recv, send_sem, recv_sem, local_sem,
    stat_send, stat_recv, back_send, back_recv,
):
    me = group_index()
    z = lax.axis_index("mp")
    ring = lax.axis_size("mp")
    up, down = lax.rem(z + 1, ring), lax.rem(z + ring - 1, ring)
    across = lax.rem(z + 2, ring)
    blocks = encoded.shape[0]
    half = blocks // 2

    barrier = pltpu.get_barrier_semaphore()
    pl.semaphore_signal(barrier, inc=1, device_id={"mp": up}, device_id_type=MESH)
    pl.semaphore_signal(barrier, inc=1, device_id={"mp": down}, device_id_type=MESH)
    greet_group(barrier, groups)

    own_load = pltpu.make_async_copy(encoded, own, load_sem.at[0])
    own_load.start()
    weight_loads = []
    for i, owner in enumerate((z, down, up, across)):
        pair = (
            pltpu.make_async_copy(key_weight.at[owner], key_w.at[i], load_sem.at[1 + 2 * i]),
            pltpu.make_async_copy(value_weight.at[owner], value_w.at[i], load_sem.at[2 + 2 * i]),
        )
        for load in pair:
            load.start()
        weight_loads.append(pair)

    def ring_copy(lane, source, target, block, to):
        return pltpu.make_async_remote_copy(
            src_ref=source.at[block],
            dst_ref=target.at[block],
            send_sem=ring_send.at[lane, block],
            recv_sem=ring_recv.at[lane, block],
            device_id={"mp": to},
            device_id_type=MESH,
        )

    def go_up(c):
        return ring_copy(0, encoded, before, c, up)

    def go_down(c):
        return ring_copy(1, encoded, after, c, down)

    def pass_up(c):
        return ring_copy(2, before, far, c, up)

    def pass_down(c):
        return ring_copy(2, after, far, c, down)

    pl.semaphore_wait(barrier, groups - 1 + 2)

    def send_own(c, carry):
        go_up(c).start()
        go_down(blocks - 1 - c).start()
        return carry

    lax.fori_loop(0, blocks, send_own, 0)
    spans = queries.shape[0]

    def fill(o, carry):
        span = jnp.int32(0)
        found = jnp.int32(0)
        for t in range(spans):
            for j in range(2):
                hit = (reads[j, t] == o).astype(jnp.int32)
                span = jnp.maximum(span, hit * t)
                found = jnp.maximum(found, hit)
        source[o] = span
        live[o] = found
        outgoing[o, 0] = jnp.where(found > 0, queries[span], jnp.zeros_like(queries[span]))
        outgoing[o, 1] = jnp.where(found > 0, grads[span], jnp.zeros_like(grads[span]))
        return carry

    lax.fori_loop(0, groups, fill, 0)
    start_slots, wait_slots = send_to_group(
        groups, lambda g: outgoing.at[g], slots, send_sem, recv_sem
    )
    start_slots()
    local = pltpu.make_async_copy(outgoing.at[me], slots.at[me], local_sem.at[0])
    local.start()

    def project(block, i):
        return (
            jnp.dot(block, key_w[i], preferred_element_type=F32),
            jnp.dot(block, value_w[i], preferred_element_type=F32),
        )

    def add(source, c, i):
        k, v = project(source[c], i)
        key_acc[c] += k
        value_acc[c] += v

    def finish(c):
        k, v = project(far[c], 3)
        keys[c] = (key_acc[c] + k).astype(BF16)
        values[c] = (value_acc[c] + v).astype(BF16)

    own_load.wait()
    for load in weight_loads[0]:
        load.wait()

    def first(c, carry):
        k, v = project(own[c], 0)
        key_acc[c] = k
        value_acc[c] = v
        return carry

    lax.fori_loop(0, blocks, first, 0)
    for pair in weight_loads[1:]:
        for load in pair:
            load.wait()

    def near(c, carry):
        d = blocks - 1 - c
        go_up(c).wait_recv()
        pass_up(c).start()
        go_down(d).wait_recv()
        pass_down(d).start()
        add(before, c, 1)
        add(after, d, 2)
        return carry

    lax.fori_loop(0, half, near, 0)

    def rest(c, carry):
        d = blocks - 1 - c
        go_up(c).wait_recv()
        add(before, c, 1)
        go_down(d).wait_recv()
        add(after, d, 2)
        return carry

    lax.fori_loop(half, blocks, rest, 0)

    wait_slots()
    local.wait()
    slots_copy = pltpu.make_async_copy(slots, slots_out, local_sem.at[1])
    slots_copy.start()

    def last(c, carry):
        d = blocks - 1 - c
        pass_up(c).wait_recv()
        finish(c)
        pass_down(d).wait_recv()
        finish(d)
        return carry

    lax.fori_loop(0, half, last, 0)

    heads = keys.shape[2] // HS

    def score(p, carry):
        for h in range(heads):
            k, v, q, g = pair_operands(rows, p, keys, values, slots, 2 * p, h)
            scores = lax.dot_general(k, q, LAST, preferred_element_type=F32) * SCALE
            gp = lax.dot_general(v, g, LAST, preferred_element_type=F32)
            peak = jnp.max(scores, 0, keepdims=True)
            w = jnp.exp(scores - peak)
            stats[p, h : h + 1] = peak
            stats[p, heads + h : heads + h + 1] = jnp.sum(w, 0, keepdims=True)
            stats[p, 2 * heads + h : 2 * heads + h + 1] = jnp.sum(w * gp, 0, keepdims=True)
            weights[p, h] = w
            grad_p[p, h] = gp
        stats[p, 3 * heads :] = jnp.zeros((stats.shape[1] - 3 * heads, 2 * CLEN), F32)
        return carry

    lax.fori_loop(0, groups // 2, score, 0, unroll=4)

    start, wait = send_to_group(
        groups, lambda g: stats.at[g // 2], fetched, stat_send, stat_recv
    )
    start()
    local = pltpu.make_async_copy(stats.at[me // 2], fetched.at[me], local_sem.at[2])
    local.start()
    local.wait()
    wait()

    def combine(t, carry):
        a = fetched[reads[0, t]]
        b = fetched[reads[1, t]]
        overall = jnp.maximum(a[:heads], b[:heads])
        fa, fb = jnp.exp(a[:heads] - overall), jnp.exp(b[:heads] - overall)
        total = fa * a[heads : 2 * heads] + fb * b[heads : 2 * heads]
        grad = fa * a[2 * heads : 3 * heads] + fb * b[2 * heads : 3 * heads]
        combined[t, :heads] = overall + jnp.log(total)
        combined[t, heads:] = grad / total
        return carry

    lax.fori_loop(0, spans, combine, 0, unroll=8)

    def answer(o, carry):
        mine = combined[source[o]]
        back[o] = jnp.where(live[o] > 0, mine, jnp.zeros_like(mine))
        return carry

    lax.fori_loop(0, groups, answer, 0, unroll=8)
    start, wait = send_to_group(groups, lambda g: back.at[g], landed, back_send, back_recv)
    start()
    local = pltpu.make_async_copy(back.at[me], landed.at[me], local_sem.at[3])
    local.start()
    local.wait()
    wait()
    left = lax.broadcasted_iota(jnp.int32, landed.shape[1:], 1) < CLEN

    def normalise(p, carry):
        both = jnp.where(left, landed[2 * p], landed[2 * p + 1])
        for h in range(heads):
            factor = jnp.exp(stats[p, h : h + 1] - both[h : h + 1])
            pr = weights[p, h] * factor
            probs[p, h] = pr.astype(BF16)
            grad_s[p, h] = (pr * (grad_p[p, h] - both[heads + h : heads + h + 1])).astype(BF16)
        return carry

    lax.fori_loop(0, groups // 2, normalise, 0, unroll=2)
    slots_copy.wait()

    def sent(c, carry):
        go_up(c).wait_send()
        go_down(c).wait_send()
        return carry

    lax.fori_loop(0, blocks, sent, 0)

    def passed(c, carry):
        pass_up(c).wait_send()
        pass_down(blocks - 1 - c).wait_send()
        return carry

    lax.fori_loop(0, half, passed, 0)


def grads_kernel(pairs, rows, probs, grad_s, slots, grad_keys, grad_values, key_acc, value_acc):
    heads = probs.shape[1]
    step = pl.program_id(0)

    @pl.when(step == 0)
    def _():
        key_acc[...] = jnp.zeros_like(key_acc)
        value_acc[...] = jnp.zeros_like(value_acc)

    def one_pair(i, carry):
        p = step * pairs + i
        low, high = rows[2 * p], rows[2 * p + 1]
        for h in range(heads):
            cols = pl.ds(h * HS, HS)
            grad_v = jnp.dot(probs[i, h], diagonal(slots, 2 * i, 1, cols), preferred_element_type=F32)
            grad_k = jnp.dot(grad_s[i, h], diagonal(slots, 2 * i, 0, cols), preferred_element_type=F32)
            key_acc[low, :, cols] += grad_k[:, :HS]
            key_acc[high, :, cols] += grad_k[:, HS:]
            value_acc[low, :, cols] += grad_v[:, :HS]
            value_acc[high, :, cols] += grad_v[:, HS:]
        return carry

    lax.fori_loop(0, pairs, one_pair, 0, unroll=pairs)

    @pl.when(step == pl.num_programs(0) - 1)
    def _():
        grad_keys[...] = (key_acc[...] * SCALE).astype(BF16)
        grad_values[...] = value_acc[...].astype(BF16)


def reduce_kernel(
    groups, rows, reads, keys, values, probs, grad_s, grad_keys, grad_values,
    key_weight, value_weight,
    attended, grad_q, grad_e,
    results, fetched, key_w, value_w, to_across, to_up, to_down, from_far, before, after, total,
    load_sem, ring_send, ring_recv, send_sem, recv_sem, local_sem,
):
    me = group_index()
    z = lax.axis_index("mp")
    ring = lax.axis_size("mp")
    up, down = lax.rem(z + 1, ring), lax.rem(z + ring - 1, ring)
    across = lax.rem(z + 2, ring)
    blocks = grad_keys.shape[0]
    half = blocks // 2
    spans = attended.shape[0]

    barrier = pltpu.get_barrier_semaphore()
    pl.semaphore_signal(barrier, inc=1, device_id={"mp": up}, device_id_type=MESH)
    pl.semaphore_signal(barrier, inc=1, device_id={"mp": down}, device_id_type=MESH)
    weight_loads = []
    for i, owner in enumerate((across, up, down, z)):
        pair = (
            pltpu.make_async_copy(key_weight.at[owner], key_w.at[i], load_sem.at[2 * i]),
            pltpu.make_async_copy(value_weight.at[owner], value_w.at[i], load_sem.at[2 * i + 1]),
        )
        for load in pair:
            load.start()
        weight_loads.append(pair)
    greet_group(barrier, groups)

    def part(c, i):
        return lax.dot_general(
            grad_keys[c], key_w[i], LAST, preferred_element_type=F32
        ) + lax.dot_general(grad_values[c], value_w[i], LAST, preferred_element_type=F32)

    def ring_copy(lane, source, target, block, to):
        return pltpu.make_async_remote_copy(
            src_ref=source.at[block],
            dst_ref=target.at[block],
            send_sem=ring_send.at[lane, block],
            recv_sem=ring_recv.at[lane, block],
            device_id={"mp": to},
            device_id_type=MESH,
        )

    def far_up(c):
        return ring_copy(2, to_across, from_far, c, up)

    def far_down(c):
        return ring_copy(2, to_across, from_far, c, down)

    def go_up(c):
        return ring_copy(0, to_up, before, c, up)

    def go_down(c):
        return ring_copy(1, to_down, after, c, down)

    pl.semaphore_wait(barrier, groups - 1 + 2)
    for load in weight_loads[0]:
        load.wait()

    def send_far(c, carry):
        d = blocks - 1 - c
        to_across[c] = part(c, 0).astype(BF16)
        far_up(c).start()
        to_across[d] = part(d, 0).astype(BF16)
        far_down(d).start()
        return carry

    lax.fori_loop(0, half, send_far, 0)
    top = lax.broadcasted_iota(jnp.int32, (2 * CLEN, HS), 0) < CLEN

    def answers(p, carry):
        low, high = rows[0, 2 * p], rows[0, 2 * p + 1]
        for h in range(keys.shape[2] // HS):
            cols = pl.ds(h * HS, HS)
            k = jnp.concatenate([keys[low, :, cols], keys[high, :, cols]], 1)
            v = jnp.concatenate([values[low, :, cols], values[high, :, cols]], 1)
            out = lax.dot_general(probs[p, h], v, FIRST, preferred_element_type=F32)
            gq = lax.dot_general(grad_s[p, h], k, FIRST, preferred_element_type=F32) * SCALE
            for j, both in enumerate((out, gq)):
                picked = jnp.where(top, both[:, :HS], both[:, HS:]).astype(BF16)
                results[pl.ds(2 * p, 2), j, :, cols] = picked.reshape(2, CLEN, HS)
        return carry

    lax.fori_loop(0, groups // 2, answers, 0, unroll=2)
    start_results, wait_results = send_to_group(
        groups, lambda g: results.at[g], fetched, send_sem, recv_sem
    )
    start_results()
    local = pltpu.make_async_copy(results.at[me], fetched.at[me], local_sem)
    local.start()
    for pair in weight_loads[1:]:
        for load in pair:
            load.wait()

    def send_near(c, carry):
        d = blocks - 1 - c
        to_up[c] = part(c, 1).astype(BF16)
        go_up(c).start()
        to_down[d] = part(d, 2).astype(BF16)
        go_down(d).start()
        return carry

    lax.fori_loop(half, blocks, send_near, 0)

    def send_joined(c, carry):
        d = blocks - 1 - c
        mine = part(c, 1)
        far_up(c).wait_recv()
        to_up[c] = (mine + from_far[c].astype(F32)).astype(BF16)
        go_up(c).start()
        mine = part(d, 2)
        far_down(d).wait_recv()
        to_down[d] = (mine + from_far[d].astype(F32)).astype(BF16)
        go_down(d).start()
        return carry

    lax.fori_loop(0, half, send_joined, 0)

    def own(c, carry):
        total[c] = part(c, 3)
        return carry

    lax.fori_loop(0, blocks, own, 0)

    def add_first(c, carry):
        d = blocks - 1 - c
        go_up(c).wait_recv()
        total[c] += before[c].astype(F32)
        go_down(d).wait_recv()
        total[d] += after[d].astype(F32)
        return carry

    lax.fori_loop(half, blocks, add_first, 0)
    local.wait()
    wait_results()

    def finish_span(t, carry):
        a, b = reads[0, t], reads[1, t]
        attended[t] = (fetched[a, 0].astype(F32) + fetched[b, 0].astype(F32)).astype(BF16)
        grad_q[t] = (fetched[a, 1].astype(F32) + fetched[b, 1].astype(F32)).astype(BF16)
        return carry

    lax.fori_loop(0, spans, finish_span, 0)

    def add_last(c, carry):
        d = blocks - 1 - c
        go_up(c).wait_recv()
        grad_e[c] = (total[c] + before[c].astype(F32)).astype(BF16)
        go_down(d).wait_recv()
        grad_e[d] = (total[d] + after[d].astype(F32)).astype(BF16)
        return carry

    lax.fori_loop(0, half, add_last, 0)

    def sent(c, carry):
        go_up(c).wait_send()
        go_down(c).wait_send()
        return carry

    lax.fori_loop(0, blocks, sent, 0)

    def sent_far(c, carry):
        far_up(c).wait_send()
        far_down(blocks - 1 - c).wait_send()
        return carry

    lax.fori_loop(0, half, sent_far, 0)


def finish_kernel(*refs):
    count = len(refs) // 2
    for source, target in zip(refs[:count], refs[count:]):
        target[...] = source[...]


def params(collective_id=None, mib=56):
    return pltpu.CompilerParams(
        collective_id=collective_id,
        has_side_effects=collective_id is not None,
        vmem_limit_bytes=mib << 20,
    )


def body(queries, grad_out, encoded, key_weight, value_weight, send_rows, read_slots):
    groups = lax.axis_size(("phase", "dp"))
    ring = lax.axis_size("mp")
    blocks, _, features = encoded.shape
    width = key_weight.shape[1]
    heads = width // HS
    spans = read_slots.shape[0]
    hbm = pl.BlockSpec(memory_space=pl.ANY)
    vmem = pl.BlockSpec(memory_space=pltpu.VMEM)
    smem = pl.BlockSpec(memory_space=pltpu.SMEM)
    dma = pltpu.SemaphoreType.DMA
    half_pairs = groups // 2

    rows = send_rows.reshape(1, groups)
    reads = read_slots.T
    query_spans = queries.reshape(spans, CLEN, width)
    grad_spans = grad_out.reshape(spans, CLEN, width)
    key_parts = key_weight.reshape(ring, features, width)
    value_parts = value_weight.reshape(ring, features, width)
    block_shape = jax.ShapeDtypeStruct((blocks, NLEN, width), BF16)
    slot_shape = jax.ShapeDtypeStruct((groups, 2, CLEN, width), BF16)
    prob_shape = jax.ShapeDtypeStruct((half_pairs, heads, NLEN, 2 * CLEN), BF16)

    stat_rows = 16
    keys, values, slots, probs, grad_s = pl.pallas_call(
        functools.partial(project_kernel, groups),
        out_shape=(block_shape, block_shape, slot_shape, prob_shape, prob_shape),
        in_specs=[smem, smem, vmem, vmem, hbm, hbm, hbm],
        out_specs=(vmem, vmem, hbm, vmem, vmem),
        scratch_shapes=[
            pltpu.SMEM((groups,), jnp.int32),
            pltpu.SMEM((groups,), jnp.int32),
            pltpu.VMEM(slot_shape.shape, BF16),
            pltpu.VMEM(slot_shape.shape, BF16),
            pltpu.VMEM(encoded.shape, BF16),
            pltpu.VMEM(encoded.shape, BF16),
            pltpu.VMEM(encoded.shape, BF16),
            pltpu.VMEM(encoded.shape, BF16),
            pltpu.VMEM(key_parts.shape, BF16),
            pltpu.VMEM(key_parts.shape, BF16),
            pltpu.VMEM((blocks, NLEN, width), F32),
            pltpu.VMEM((blocks, NLEN, width), F32),
            pltpu.VMEM((half_pairs, stat_rows, 2 * CLEN), F32),
            pltpu.VMEM((groups, stat_rows, 2 * CLEN), F32),
            pltpu.VMEM((spans, 2 * heads, 2 * CLEN), F32),
            pltpu.VMEM((groups, 2 * heads, 2 * CLEN), F32),
            pltpu.VMEM((groups, 2 * heads, 2 * CLEN), F32),
            pltpu.VMEM(prob_shape.shape, F32),
            pltpu.VMEM(prob_shape.shape, F32),
            dma((9,)),
            dma((3, blocks)),
            dma((3, blocks)),
            dma((groups,)),
            dma((groups,)),
            dma((4,)),
            dma((groups,)),
            dma((groups,)),
            dma((groups,)),
            dma((groups,)),
        ],
        compiler_params=params(0),
        name="project",
    )(rows, reads, query_spans, grad_spans, encoded, key_parts, value_parts)

    steps = 4
    pairs = half_pairs // steps
    whole = pl.BlockSpec(block_shape.shape, lambda i, rows: (0, 0, 0))
    per_pair = pl.BlockSpec((pairs,) + prob_shape.shape[1:], lambda i, rows: (i, 0, 0, 0))
    per_slot = pl.BlockSpec((2 * pairs,) + slot_shape.shape[1:], lambda i, rows: (i, 0, 0, 0))
    grad_keys, grad_values = pl.pallas_call(
        functools.partial(grads_kernel, pairs),
        out_shape=(block_shape, block_shape),
        grid_spec=pltpu.PrefetchScalarGridSpec(
            num_scalar_prefetch=1,
            grid=(steps,),
            in_specs=[per_pair, per_pair, per_slot],
            out_specs=(whole, whole),
            scratch_shapes=[
                pltpu.VMEM(block_shape.shape, F32),
                pltpu.VMEM(block_shape.shape, F32),
            ],
        ),
        compiler_params=params(),
        name="grads",
    )(send_rows.reshape(groups), probs, grad_s, slots)

    results = pl.pallas_call(
        functools.partial(reduce_kernel, groups),
        out_shape=(
            jax.ShapeDtypeStruct((spans, CLEN, width), BF16),
            jax.ShapeDtypeStruct((spans, CLEN, width), BF16),
            jax.ShapeDtypeStruct(encoded.shape, BF16),
        ),
        in_specs=[smem, smem, vmem, vmem, vmem, vmem, vmem, vmem, hbm, hbm],
        out_specs=(vmem, vmem, vmem),
        scratch_shapes=[
            pltpu.VMEM(slot_shape.shape, BF16),
            pltpu.VMEM(slot_shape.shape, BF16),
            pltpu.VMEM(key_parts.shape, BF16),
            pltpu.VMEM(key_parts.shape, BF16),
            pltpu.VMEM(encoded.shape, BF16),
            pltpu.VMEM(encoded.shape, BF16),
            pltpu.VMEM(encoded.shape, BF16),
            pltpu.VMEM(encoded.shape, BF16),
            pltpu.VMEM(encoded.shape, BF16),
            pltpu.VMEM(encoded.shape, BF16),
            pltpu.VMEM(encoded.shape, F32),
            dma((8,)),
            dma((3, blocks)),
            dma((3, blocks)),
            dma((groups,)),
            dma((groups,)),
            dma,
        ],
        compiler_params=params(2),
        name="reduce",
    )(rows, reads, keys, values, probs, grad_s, grad_keys, grad_values, key_parts, value_parts)
    parts = 4
    slices = [
        pl.BlockSpec((r.shape[0] // parts,) + r.shape[1:], lambda i: (i, 0, 0)) for r in results
    ]
    attended, grad_q, grad_e = pl.pallas_call(
        finish_kernel,
        out_shape=tuple(jax.ShapeDtypeStruct(r.shape, r.dtype) for r in results),
        grid=(parts,),
        in_specs=slices,
        out_specs=tuple(slices),
        compiler_params=params(),
        name="finish",
    )(*results)
    return (attended.reshape(queries.shape), grad_q.reshape(queries.shape), grad_e)


def solution(mesh):
    return jax.shard_map(
        body,
        mesh=mesh,
        in_specs=(
            P(("phase", "dp"), "mp"),
            P(("phase", "dp"), "mp"),
            P(("phase", "dp"), None, "mp"),
            P(None, "mp"),
            P(None, "mp"),
            P(("phase", "dp"), None, None),
            P(("phase", "dp"), None),
        ),
        out_specs=(
            P(("phase", "dp"), "mp"),
            P(("phase", "dp"), "mp"),
            P(("phase", "dp"), None, "mp"),
        ),
        check_vma=False,
    )
```

```python
import functools

import jax
import jax.numpy as jnp
from jax import lax
from jax.experimental import pallas as pl
from jax.experimental.pallas import tpu as pltpu
from jax.sharding import PartitionSpec as P

HS = 128
CLEN = 64
NLEN = 128
SCALE = HS ** (-0.5)
LAST = (((1,), (1,)), ((), ()))
FIRST = (((0,), (0,)), ((), ()))
MESH = pl.DeviceIdType.MESH
F32 = jnp.float32
BF16 = jnp.bfloat16


def group_index():
    return lax.axis_index("phase") * lax.axis_size("dp") + lax.axis_index("dp")


def peer_id(group):
    dp = lax.axis_size("dp")
    return {"phase": group // dp, "dp": lax.rem(group, dp)}


def greet_group(barrier, groups):
    me = group_index()

    def greet(k, carry):
        pl.semaphore_signal(
            barrier, inc=1, device_id=peer_id(lax.rem(me + k, groups)), device_id_type=MESH
        )
        return carry

    lax.fori_loop(1, groups, greet, 0)


def send_to_group(groups, source, target, send_sem, recv_sem):
    me = group_index()

    def copy_to(k):
        peer = lax.rem(me + k, groups)
        return pltpu.make_async_remote_copy(
            src_ref=source(peer),
            dst_ref=target.at[me],
            send_sem=send_sem.at[k],
            recv_sem=recv_sem.at[k],
            device_id=peer_id(peer),
            device_id_type=MESH,
        )

    def copy_from(k):
        peer = lax.rem(me + groups - k, groups)
        return pltpu.make_async_remote_copy(
            src_ref=source(peer),
            dst_ref=target.at[peer],
            send_sem=send_sem.at[k],
            recv_sem=recv_sem.at[k],
            device_id=peer_id(peer),
            device_id_type=MESH,
        )

    def start():
        lax.fori_loop(1, groups, lambda k, c: (copy_to(k).start(), c)[1], 0)

    def wait():
        def one(k, carry):
            copy_from(k).wait_recv()
            copy_to(k).wait_send()
            return carry

        lax.fori_loop(1, groups, one, 0)

    return start, wait


def diagonal(slots, first, which, cols):
    top = lax.broadcasted_iota(jnp.int32, (2 * CLEN, HS), 0) < CLEN
    block = slots[pl.ds(first, 2), which, :, cols].reshape(2 * CLEN, HS)
    zero = jnp.zeros_like(block)
    return jnp.concatenate([jnp.where(top, block, zero), jnp.where(top, zero, block)], 1)


def pair_operands(rows, pair, keys, values, slots, first, h):
    cols = pl.ds(h * HS, HS)
    low, high = rows[0, 2 * pair], rows[0, 2 * pair + 1]
    k = jnp.concatenate([keys[low, :, cols], keys[high, :, cols]], 1)
    v = jnp.concatenate([values[low, :, cols], values[high, :, cols]], 1)
    return k, v, diagonal(slots, first, 0, cols), diagonal(slots, first, 1, cols)


def retro_kernel(
    groups, rows, reads, queries, grads, encoded, key_weight, value_weight,
    attended_out, grad_q_out, grad_e_out,
    source, live, rank, order, keep, final, filled,
    query_in, grad_in, outgoing, slots, own, before, after, far, key_w, value_w,
    key_acc, value_acc, keys, values, probs, grad_s, weights, grad_p,
    stats, fetched, combined, back, landed, key_run, value_run, value_sums,
    answers_in, from_far, from_below, from_above,
    load_sem, ring_send, ring_recv, send_sem, recv_sem, local_sem,
    stat_send, stat_recv, back_send, back_recv,
    sum_send, sum_recv, answer_send, answer_recv, out_sem,
):
    me = group_index()
    z = lax.axis_index("mp")
    ring = lax.axis_size("mp")
    up, down = lax.rem(z + 1, ring), lax.rem(z + ring - 1, ring)
    across = lax.rem(z + 2, ring)
    blocks = encoded.shape[0]
    half = blocks // 2

    barrier = pltpu.get_barrier_semaphore()
    pl.semaphore_signal(barrier, inc=1, device_id={"mp": up}, device_id_type=MESH)
    pl.semaphore_signal(barrier, inc=1, device_id={"mp": down}, device_id_type=MESH)
    greet_group(barrier, groups)

    inputs = (
        pltpu.make_async_copy(queries, query_in, load_sem.at[9]),
        pltpu.make_async_copy(grads, grad_in, load_sem.at[10]),
    )
    for load in inputs:
        load.start()
    own_load = pltpu.make_async_copy(encoded, own, load_sem.at[0])
    own_load.start()
    weight_loads = []
    for i, owner in enumerate((z, down, up, across)):
        pair = (
            pltpu.make_async_copy(key_weight.at[owner], key_w.at[i], load_sem.at[1 + 2 * i]),
            pltpu.make_async_copy(value_weight.at[owner], value_w.at[i], load_sem.at[2 + 2 * i]),
        )
        for load in pair:
            load.start()
        weight_loads.append(pair)

    def ring_copy(lane, source, target, block, to):
        return pltpu.make_async_remote_copy(
            src_ref=source.at[block],
            dst_ref=target.at[block],
            send_sem=ring_send.at[lane, block],
            recv_sem=ring_recv.at[lane, block],
            device_id={"mp": to},
            device_id_type=MESH,
        )

    def go_up(c):
        return ring_copy(0, encoded, before, c, up)

    def go_down(c):
        return ring_copy(1, encoded, after, c, down)

    def pass_up(c):
        return ring_copy(2, before, far, c, up)

    def pass_down(c):
        return ring_copy(2, after, far, c, down)

    pl.semaphore_wait(barrier, groups - 1 + 2)

    def send_own(c, carry):
        go_up(c).start()
        go_down(blocks - 1 - c).start()
        return carry

    lax.fori_loop(0, blocks, send_own, 0)
    spans = queries.shape[0]

    def fill(o, carry):
        span = jnp.int32(0)
        found = jnp.int32(0)
        for t in range(spans):
            for j in range(2):
                hit = (reads[j, t] == o).astype(jnp.int32)
                span = jnp.maximum(span, hit * t)
                found = jnp.maximum(found, hit)
        source[o] = span
        live[o] = found
        for j, array in enumerate((query_in, grad_in)):
            block = array[span]
            outgoing[o, j] = jnp.where(found > 0, block, jnp.zeros_like(block))
        return carry

    for load in inputs:
        load.wait()
    lax.fori_loop(0, groups, fill, 0)
    start_slots, wait_slots = send_to_group(
        groups, lambda g: outgoing.at[g], slots, send_sem, recv_sem
    )
    start_slots()
    local = pltpu.make_async_copy(outgoing.at[me], slots.at[me], local_sem.at[0])
    local.start()

    def place(o, carry):
        mine = rows[0, o]
        count = jnp.int32(0)
        for other in range(groups):
            theirs = rows[0, other]
            count += (theirs < mine).astype(jnp.int32)
            count += ((theirs == mine) & (other < o)).astype(jnp.int32)
        rank[o] = count
        return carry

    def invert(i, carry):
        slot = jnp.int32(0)
        for o in range(groups):
            slot = jnp.maximum(slot, (rank[o] == i).astype(jnp.int32) * o)
        order[i] = slot
        return carry

    def follow(i, carry):
        same = rows[0, order[i]] == rows[0, order[jnp.maximum(i - 1, 0)]]
        keep[i] = (same & (i > 0)).astype(jnp.int32)
        return carry

    def close(n, carry):
        upto = jnp.int32(0)
        here = jnp.int32(0)
        for o in range(groups):
            upto += (rows[0, o] <= n).astype(jnp.int32)
            here += (rows[0, o] == n).astype(jnp.int32)
        final[n] = jnp.maximum(upto - 1, 0)
        filled[n] = jnp.minimum(here, 1)
        return carry

    lax.fori_loop(0, groups, place, 0)
    lax.fori_loop(0, groups, invert, 0)
    lax.fori_loop(0, groups, follow, 0)
    lax.fori_loop(0, blocks, close, 0)

    def project(block, i):
        return (
            jnp.dot(block, key_w[i], preferred_element_type=F32),
            jnp.dot(block, value_w[i], preferred_element_type=F32),
        )

    def add(source, c, i):
        k, v = project(source[c], i)
        key_acc[c] += k
        value_acc[c] += v

    def finish(c):
        k, v = project(far[c], 3)
        keys[c] = (key_acc[c] + k).astype(BF16)
        values[c] = (value_acc[c] + v).astype(BF16)

    own_load.wait()
    for load in weight_loads[0]:
        load.wait()

    def first(c, carry):
        k, v = project(own[c], 0)
        key_acc[c] = k
        value_acc[c] = v
        return carry

    lax.fori_loop(0, blocks, first, 0)
    for pair in weight_loads[1:]:
        for load in pair:
            load.wait()

    def near(c, carry):
        d = blocks - 1 - c
        go_up(c).wait_recv()
        pass_up(c).start()
        go_down(d).wait_recv()
        pass_down(d).start()
        add(before, c, 1)
        add(after, d, 2)
        return carry

    lax.fori_loop(0, half, near, 0)

    def rest(c, carry):
        d = blocks - 1 - c
        go_up(c).wait_recv()
        add(before, c, 1)
        go_down(d).wait_recv()
        add(after, d, 2)
        return carry

    lax.fori_loop(half, blocks, rest, 0)

    wait_slots()
    local.wait()

    def last(c, carry):
        d = blocks - 1 - c
        pass_up(c).wait_recv()
        finish(c)
        pass_down(d).wait_recv()
        finish(d)
        return carry

    lax.fori_loop(0, half, last, 0)

    heads = keys.shape[2] // HS

    def score(p, carry):
        for h in range(heads):
            k, v, q, g = pair_operands(rows, p, keys, values, slots, 2 * p, h)
            scores = lax.dot_general(k, q, LAST, preferred_element_type=F32) * SCALE
            gp = lax.dot_general(v, g, LAST, preferred_element_type=F32)
            peak = jnp.max(scores, 0, keepdims=True)
            w = jnp.exp(scores - peak)
            stats[p, h : h + 1] = peak
            stats[p, heads + h : heads + h + 1] = jnp.sum(w, 0, keepdims=True)
            stats[p, 2 * heads + h : 2 * heads + h + 1] = jnp.sum(w * gp, 0, keepdims=True)
            weights[p, h] = w
            grad_p[p, h] = gp
        stats[p, 3 * heads :] = jnp.zeros((stats.shape[1] - 3 * heads, 2 * CLEN), F32)
        return carry

    lax.fori_loop(0, groups // 2, score, 0, unroll=4)

    start, wait = send_to_group(
        groups, lambda g: stats.at[g // 2], fetched, stat_send, stat_recv
    )
    start()
    local = pltpu.make_async_copy(stats.at[me // 2], fetched.at[me], local_sem.at[2])
    local.start()
    local.wait()
    wait()

    def combine(t, carry):
        a = fetched[reads[0, t]]
        b = fetched[reads[1, t]]
        overall = jnp.maximum(a[:heads], b[:heads])
        fa, fb = jnp.exp(a[:heads] - overall), jnp.exp(b[:heads] - overall)
        total = fa * a[heads : 2 * heads] + fb * b[heads : 2 * heads]
        grad = fa * a[2 * heads : 3 * heads] + fb * b[2 * heads : 3 * heads]
        combined[t, :heads] = overall + jnp.log(total)
        combined[t, heads:] = grad / total
        return carry

    lax.fori_loop(0, spans, combine, 0, unroll=8)

    def answer(o, carry):
        mine = combined[source[o]]
        back[o] = jnp.where(live[o] > 0, mine, jnp.zeros_like(mine))
        return carry

    lax.fori_loop(0, groups, answer, 0, unroll=8)
    start, wait = send_to_group(groups, lambda g: back.at[g], landed, back_send, back_recv)
    start()
    local = pltpu.make_async_copy(back.at[me], landed.at[me], local_sem.at[3])
    local.start()
    local.wait()
    wait()
    left = lax.broadcasted_iota(jnp.int32, landed.shape[1:], 1) < CLEN

    def normalise(p, carry):
        both = jnp.where(left, landed[2 * p], landed[2 * p + 1])
        for h in range(heads):
            factor = jnp.exp(stats[p, h : h + 1] - both[h : h + 1])
            pr = weights[p, h] * factor
            probs[p, h] = pr.astype(BF16)
            grad_s[p, h] = (pr * (grad_p[p, h] - both[heads + h : heads + h + 1])).astype(BF16)
        return carry

    lax.fori_loop(0, groups // 2, normalise, 0, unroll=2)

    half_lane = lax.broadcasted_iota(jnp.int32, (NLEN, 2 * CLEN), 1) // CLEN
    key_run[...] = jnp.zeros_like(key_run)
    value_run[...] = jnp.zeros_like(value_run)

    def accumulate(i, carry):
        slot = order[i]
        pair = slot // 2
        mine = half_lane == lax.rem(slot, 2)
        more = keep[i].astype(F32)
        for h in range(heads):
            cols = pl.ds(h * HS, HS)
            zero = jnp.zeros((NLEN, 2 * CLEN), BF16)
            p = jnp.where(mine, probs[pair, h], zero)
            s = jnp.where(mine, grad_s[pair, h], zero)
            q, g = slots[slot, 0, :, cols], slots[slot, 1, :, cols]
            k = key_run[:, cols] * more + jnp.dot(
                s, jnp.concatenate([q, q], 0), preferred_element_type=F32
            )
            v = value_run[:, cols] * more + jnp.dot(
                p, jnp.concatenate([g, g], 0), preferred_element_type=F32
            )
            key_run[:, cols] = k
            value_run[:, cols] = v
            outgoing[i, :, :, cols] = (k * SCALE).astype(BF16).reshape(2, CLEN, HS)
            value_sums[i, :, :, cols] = v.astype(BF16).reshape(2, CLEN, HS)
        return carry

    lax.fori_loop(0, groups, accumulate, 0, unroll=4)
    width = keys.shape[2]

    def gather(n, carry):
        for j, sums in enumerate((outgoing, value_sums)):
            block = sums[final[n]].reshape(NLEN, width)
            far[n, :, j * width : (j + 1) * width] = jnp.where(
                filled[n] > 0, block, jnp.zeros_like(block)
            )
        return carry

    lax.fori_loop(0, blocks, gather, 0)

    def sent(c, carry):
        go_up(c).wait_send()
        go_down(c).wait_send()
        return carry

    lax.fori_loop(0, blocks, sent, 0)

    def passed(c, carry):
        pass_up(c).wait_send()
        pass_down(blocks - 1 - c).wait_send()
        return carry

    lax.fori_loop(0, half, passed, 0)

    def part(c, i):
        return lax.dot_general(
            far[c, :, :width], key_w[i], LAST, preferred_element_type=F32
        ) + lax.dot_general(far[c, :, width:], value_w[i], LAST, preferred_element_type=F32)

    def sum_copy(lane, source, target, block, to):
        return pltpu.make_async_remote_copy(
            src_ref=source.at[block],
            dst_ref=target.at[block],
            send_sem=sum_send.at[lane, block],
            recv_sem=sum_recv.at[lane, block],
            device_id={"mp": to},
            device_id_type=MESH,
        )

    to_across, to_up, to_down = own, before, after

    def far_up(c):
        return sum_copy(2, to_across, from_far, c, up)

    def far_down(c):
        return sum_copy(2, to_across, from_far, c, down)

    def sum_up(c):
        return sum_copy(0, to_up, from_below, c, up)

    def sum_down(c):
        return sum_copy(1, to_down, from_above, c, down)

    def send_far(c, carry):
        d = blocks - 1 - c
        to_across[c] = part(c, 3).astype(BF16)
        far_up(c).start()
        to_across[d] = part(d, 3).astype(BF16)
        far_down(d).start()
        return carry

    lax.fori_loop(0, half, send_far, 0)
    results = slots
    top = lax.broadcasted_iota(jnp.int32, (2 * CLEN, HS), 0) < CLEN

    def answers(p, carry):
        low, high = rows[0, 2 * p], rows[0, 2 * p + 1]
        for h in range(heads):
            cols = pl.ds(h * HS, HS)
            k = jnp.concatenate([keys[low, :, cols], keys[high, :, cols]], 1)
            v = jnp.concatenate([values[low, :, cols], values[high, :, cols]], 1)
            out = lax.dot_general(probs[p, h], v, FIRST, preferred_element_type=F32)
            gq = lax.dot_general(grad_s[p, h], k, FIRST, preferred_element_type=F32) * SCALE
            for j, both in enumerate((out, gq)):
                picked = jnp.where(top, both[:, :HS], both[:, HS:]).astype(BF16)
                results[pl.ds(2 * p, 2), j, :, cols] = picked.reshape(2, CLEN, HS)
        return carry

    lax.fori_loop(0, groups // 2, answers, 0, unroll=4)
    start, wait_answers = send_to_group(
        groups, lambda g: results.at[g], answers_in, answer_send, answer_recv
    )
    start()
    local_answer = pltpu.make_async_copy(results.at[me], answers_in.at[me], local_sem.at[1])
    local_answer.start()

    def send_near(c, carry):
        d = blocks - 1 - c
        to_up[c] = part(c, 2).astype(BF16)
        sum_up(c).start()
        to_down[d] = part(d, 1).astype(BF16)
        sum_down(d).start()
        return carry

    lax.fori_loop(half, blocks, send_near, 0)

    def send_joined(c, carry):
        d = blocks - 1 - c
        mine = part(c, 2)
        far_up(c).wait_recv()
        to_up[c] = (mine + from_far[c].astype(F32)).astype(BF16)
        sum_up(c).start()
        mine = part(d, 1)
        far_down(d).wait_recv()
        to_down[d] = (mine + from_far[d].astype(F32)).astype(BF16)
        sum_down(d).start()
        return carry

    lax.fori_loop(0, half, send_joined, 0)

    def keep_own(c, carry):
        mine = part(c, 0)
        key_acc[c] = mine[:, :width]
        value_acc[c] = mine[:, width:]
        return carry

    lax.fori_loop(0, blocks, keep_own, 0)

    def total(c, arrived):
        other = arrived[c].astype(F32)
        return key_acc[c] + other[:, :width], value_acc[c] + other[:, width:]

    def add_first(c, carry):
        d = blocks - 1 - c
        sum_up(c).wait_recv()
        key_acc[c], value_acc[c] = total(c, from_below)
        sum_down(d).wait_recv()
        key_acc[d], value_acc[d] = total(d, from_above)
        return carry

    lax.fori_loop(half, blocks, add_first, 0)
    local_answer.wait()
    wait_answers()

    def finish_span(t, carry):
        a, b = reads[0, t], reads[1, t]
        for j, target in enumerate((query_in, grad_in)):
            target[t] = (answers_in[a, j].astype(F32) + answers_in[b, j].astype(F32)).astype(BF16)
        return carry

    lax.fori_loop(0, spans, finish_span, 0)
    out_copies = (
        pltpu.make_async_copy(query_in, attended_out, out_sem.at[blocks]),
        pltpu.make_async_copy(grad_in, grad_q_out, out_sem.at[blocks + 1]),
    )
    for copy in out_copies:
        copy.start()

    def sent_far(c, carry):
        far_up(c).wait_send()
        far_down(blocks - 1 - c).wait_send()
        return carry

    lax.fori_loop(0, half, sent_far, 0)
    grad_e = own

    def out_copy(c):
        return pltpu.make_async_copy(grad_e.at[c], grad_e_out.at[c], out_sem.at[c])

    def emit(c, arrived):
        low, high = total(c, arrived)
        grad_e[c, :, :width] = low.astype(BF16)
        grad_e[c, :, width:] = high.astype(BF16)
        out_copy(c).start()

    def add_last(c, carry):
        d = blocks - 1 - c
        sum_up(c).wait_recv()
        emit(c, from_below)
        sum_down(d).wait_recv()
        emit(d, from_above)
        return carry

    lax.fori_loop(0, half, add_last, 0)

    def sums_sent(c, carry):
        sum_up(c).wait_send()
        sum_down(c).wait_send()
        out_copy(c).wait()
        return carry

    lax.fori_loop(0, blocks, sums_sent, 0)
    for copy in out_copies:
        copy.wait()


def finish_kernel(*refs):
    count = len(refs) // 2
    for source, target in zip(refs[:count], refs[count:]):
        target[...] = source[...]


def params(collective_id=None, mib=56):
    return pltpu.CompilerParams(
        collective_id=collective_id,
        has_side_effects=collective_id is not None,
        vmem_limit_bytes=mib << 20,
    )


def body(queries, grad_out, encoded, key_weight, value_weight, send_rows, read_slots):
    groups = lax.axis_size(("phase", "dp"))
    ring = lax.axis_size("mp")
    blocks, _, features = encoded.shape
    width = key_weight.shape[1]
    heads = width // HS
    spans = read_slots.shape[0]
    hbm = pl.BlockSpec(memory_space=pl.ANY)
    vmem = pl.BlockSpec(memory_space=pltpu.VMEM)
    smem = pl.BlockSpec(memory_space=pltpu.SMEM)
    dma = pltpu.SemaphoreType.DMA
    half_pairs = groups // 2

    rows = send_rows.reshape(1, groups)
    reads = read_slots.T
    query_spans = queries.reshape(spans, CLEN, width)
    grad_spans = grad_out.reshape(spans, CLEN, width)
    key_parts = key_weight.reshape(ring, features, width)
    value_parts = value_weight.reshape(ring, features, width)
    block_shape = jax.ShapeDtypeStruct((blocks, NLEN, width), BF16)
    slot_shape = jax.ShapeDtypeStruct((groups, 2, CLEN, width), BF16)
    prob_shape = jax.ShapeDtypeStruct((half_pairs, heads, NLEN, 2 * CLEN), BF16)

    stat_rows = 16
    stat_shape = (groups, stat_rows, 2 * CLEN)
    factor_shape = (groups, 2 * heads, 2 * CLEN)
    span_shape = jax.ShapeDtypeStruct((spans, CLEN, width), BF16)
    results = pl.pallas_call(
        functools.partial(retro_kernel, groups),
        out_shape=(span_shape, span_shape, jax.ShapeDtypeStruct(encoded.shape, BF16)),
        in_specs=[smem, smem, hbm, hbm, hbm, hbm, hbm],
        out_specs=(hbm, hbm, hbm),
        scratch_shapes=[
            pltpu.SMEM((groups,), jnp.int32),
            pltpu.SMEM((groups,), jnp.int32),
            pltpu.SMEM((groups,), jnp.int32),
            pltpu.SMEM((groups,), jnp.int32),
            pltpu.SMEM((groups,), jnp.int32),
            pltpu.SMEM((blocks,), jnp.int32),
            pltpu.SMEM((blocks,), jnp.int32),
            pltpu.VMEM(span_shape.shape, BF16),
            pltpu.VMEM(span_shape.shape, BF16),
            pltpu.VMEM(slot_shape.shape, BF16),
            pltpu.VMEM(slot_shape.shape, BF16),
            pltpu.VMEM(encoded.shape, BF16),
            pltpu.VMEM(encoded.shape, BF16),
            pltpu.VMEM(encoded.shape, BF16),
            pltpu.VMEM(encoded.shape, BF16),
            pltpu.VMEM(key_parts.shape, BF16),
            pltpu.VMEM(key_parts.shape, BF16),
            pltpu.VMEM(block_shape.shape, F32),
            pltpu.VMEM(block_shape.shape, F32),
            pltpu.VMEM(block_shape.shape, BF16),
            pltpu.VMEM(block_shape.shape, BF16),
            pltpu.VMEM(prob_shape.shape, BF16),
            pltpu.VMEM(prob_shape.shape, BF16),
            pltpu.VMEM(prob_shape.shape, F32),
            pltpu.VMEM(prob_shape.shape, F32),
            pltpu.VMEM((half_pairs,) + stat_shape[1:], F32),
            pltpu.VMEM(stat_shape, F32),
            pltpu.VMEM((spans,) + factor_shape[1:], F32),
            pltpu.VMEM(factor_shape, F32),
            pltpu.VMEM(factor_shape, F32),
            pltpu.VMEM((NLEN, width), F32),
            pltpu.VMEM((NLEN, width), F32),
            pltpu.VMEM(slot_shape.shape, BF16),
            pltpu.VMEM(slot_shape.shape, BF16),
            pltpu.VMEM(encoded.shape, BF16),
            pltpu.VMEM(encoded.shape, BF16),
            pltpu.VMEM(encoded.shape, BF16),
            dma((11,)),
            dma((3, blocks)),
            dma((3, blocks)),
            dma((groups,)),
            dma((groups,)),
            dma((4,)),
            dma((groups,)),
            dma((groups,)),
            dma((groups,)),
            dma((groups,)),
            dma((3, blocks)),
            dma((3, blocks)),
            dma((groups,)),
            dma((groups,)),
            dma((blocks + 2,)),
        ],
        compiler_params=params(0, 62),
        name="retro",
    )(rows, reads, query_spans, grad_spans, encoded, key_parts, value_parts)
    parts = 4
    slices = [
        pl.BlockSpec((r.shape[0] // parts,) + r.shape[1:], lambda i: (i, 0, 0)) for r in results
    ]
    attended, grad_q, grad_e = pl.pallas_call(
        finish_kernel,
        out_shape=tuple(jax.ShapeDtypeStruct(r.shape, r.dtype) for r in results),
        grid=(parts,),
        in_specs=slices,
        out_specs=tuple(slices),
        compiler_params=params(),
        name="finish",
    )(*results)
    return (attended.reshape(queries.shape), grad_q.reshape(queries.shape), grad_e)


def solution(mesh):
    return jax.shard_map(
        body,
        mesh=mesh,
        in_specs=(
            P(("phase", "dp"), "mp"),
            P(("phase", "dp"), "mp"),
            P(("phase", "dp"), None, "mp"),
            P(None, "mp"),
            P(None, "mp"),
            P(("phase", "dp"), None, None),
            P(("phase", "dp"), None),
        ),
        out_specs=(
            P(("phase", "dp"), "mp"),
            P(("phase", "dp"), "mp"),
            P(("phase", "dp"), None, "mp"),
        ),
        check_vma=False,
    )
```

```python
import functools

import jax
import jax.numpy as jnp
from jax import lax
from jax.experimental import pallas as pl
from jax.experimental.pallas import tpu as pltpu
from jax.sharding import PartitionSpec as P

HS = 128
CLEN = 64
NLEN = 128
SCALE = HS ** (-0.5)
LAST = (((1,), (1,)), ((), ()))
FIRST = (((0,), (0,)), ((), ()))
MESH = pl.DeviceIdType.MESH
F32 = jnp.float32
BF16 = jnp.bfloat16


def group_index():
    return lax.axis_index("phase") * lax.axis_size("dp") + lax.axis_index("dp")


def peer_id(group):
    dp = lax.axis_size("dp")
    return {"phase": group // dp, "dp": lax.rem(group, dp)}


def greet_group(barrier, groups):
    me = group_index()

    def greet(k, carry):
        pl.semaphore_signal(
            barrier, inc=1, device_id=peer_id(lax.rem(me + k, groups)), device_id_type=MESH
        )
        return carry

    lax.fori_loop(1, groups, greet, 0)


def send_to_group(groups, source, target, send_sem, recv_sem):
    me = group_index()

    def copy_to(k):
        peer = lax.rem(me + k, groups)
        return pltpu.make_async_remote_copy(
            src_ref=source(peer),
            dst_ref=target.at[me],
            send_sem=send_sem.at[k],
            recv_sem=recv_sem.at[k],
            device_id=peer_id(peer),
            device_id_type=MESH,
        )

    def copy_from(k):
        peer = lax.rem(me + groups - k, groups)
        return pltpu.make_async_remote_copy(
            src_ref=source(peer),
            dst_ref=target.at[peer],
            send_sem=send_sem.at[k],
            recv_sem=recv_sem.at[k],
            device_id=peer_id(peer),
            device_id_type=MESH,
        )

    def arrive():
        lax.fori_loop(1, groups, lambda k, c: (copy_from(k).wait_recv(), c)[1], 0)

    def leave():
        lax.fori_loop(1, groups, lambda k, c: (copy_to(k).wait_send(), c)[1], 0)

    return copy_to, arrive, leave


def start_all(groups, copy_to):
    lax.fori_loop(1, groups, lambda k, c: (copy_to(k).start(), c)[1], 0)


def diagonal(slots, first, which, cols):
    top = lax.broadcasted_iota(jnp.int32, (2 * CLEN, HS), 0) < CLEN
    block = slots[pl.ds(first, 2), which, :, cols].reshape(2 * CLEN, HS)
    zero = jnp.zeros_like(block)
    return jnp.concatenate([jnp.where(top, block, zero), jnp.where(top, zero, block)], 1)


def pair_operands(rows, pair, keys, values, slots, first, h):
    cols = pl.ds(h * HS, HS)
    low, high = rows[0, 2 * pair], rows[0, 2 * pair + 1]
    k = jnp.concatenate([keys[low, :, cols], keys[high, :, cols]], 1)
    v = jnp.concatenate([values[low, :, cols], values[high, :, cols]], 1)
    return k, v, diagonal(slots, first, 0, cols), diagonal(slots, first, 1, cols)


def retro_kernel(
    groups, rows, reads, queries, grads, encoded, key_weight, value_weight,
    attended, grad_q, grad_e,
    source, live, rank, order, keep, final, filled,
    query_in, grad_in, outgoing, slots, own, before, after, far, key_w, value_w,
    totals, keys, values, probs, grad_s, grad_p,
    peaks, stats, fetched, combined, back, landed, key_run, value_run, value_sums,
    answers_in, from_far, from_below, from_above,
    load_sem, ring_send, ring_recv, send_sem, recv_sem, local_sem,
    stat_send, stat_recv, back_send, back_recv,
    sum_send, sum_recv, answer_send, answer_recv,
):
    me = group_index()
    z = lax.axis_index("mp")
    ring = lax.axis_size("mp")
    up, down = lax.rem(z + 1, ring), lax.rem(z + ring - 1, ring)
    across = lax.rem(z + 2, ring)
    blocks = encoded.shape[0]
    half = blocks // 2
    key_acc, value_acc, weights = totals.at[0], totals.at[1], totals

    barrier = pltpu.get_barrier_semaphore()
    pl.semaphore_signal(barrier, inc=1, device_id={"mp": up}, device_id_type=MESH)
    pl.semaphore_signal(barrier, inc=1, device_id={"mp": down}, device_id_type=MESH)
    greet_group(barrier, groups)

    inputs = (
        pltpu.make_async_copy(queries, query_in, load_sem.at[9]),
        pltpu.make_async_copy(grads, grad_in, load_sem.at[10]),
    )
    for load in inputs:
        load.start()
    own_load = pltpu.make_async_copy(encoded, own, load_sem.at[0])
    own_load.start()
    weight_loads = []
    for i, owner in enumerate((z, down, up, across)):
        pair = (
            pltpu.make_async_copy(key_weight.at[owner], key_w.at[i], load_sem.at[1 + 2 * i]),
            pltpu.make_async_copy(value_weight.at[owner], value_w.at[i], load_sem.at[2 + 2 * i]),
        )
        for load in pair:
            load.start()
        weight_loads.append(pair)

    def ring_copy(lane, source, target, block, to):
        return pltpu.make_async_remote_copy(
            src_ref=source.at[block],
            dst_ref=target.at[block],
            send_sem=ring_send.at[lane, block],
            recv_sem=ring_recv.at[lane, block],
            device_id={"mp": to},
            device_id_type=MESH,
        )

    def go_up(c):
        return ring_copy(0, encoded, before, c, up)

    def go_down(c):
        return ring_copy(1, encoded, after, c, down)

    def pass_up(c):
        return ring_copy(2, before, far, c, up)

    def pass_down(c):
        return ring_copy(2, after, far, c, down)

    pl.semaphore_wait(barrier, groups - 1 + 2)

    def send_own(c, carry):
        go_up(c).start()
        go_down(blocks - 1 - c).start()
        return carry

    lax.fori_loop(0, blocks, send_own, 0)
    spans = queries.shape[0]

    def fill(o, carry):
        span = jnp.int32(0)
        found = jnp.int32(0)
        for t in range(spans):
            for j in range(2):
                hit = (reads[j, t] == o).astype(jnp.int32)
                span = jnp.maximum(span, hit * t)
                found = jnp.maximum(found, hit)
        source[o] = span
        live[o] = found
        for j, array in enumerate((query_in, grad_in)):
            block = array[span]
            outgoing[o, j] = jnp.where(found > 0, block, jnp.zeros_like(block))
        return carry

    for load in inputs:
        load.wait()
    lax.fori_loop(0, groups, fill, 0)
    slot_to, slots_arrive, slots_leave = send_to_group(
        groups, lambda g: outgoing.at[g], slots, send_sem, recv_sem
    )
    start_all(groups, slot_to)
    local = pltpu.make_async_copy(outgoing.at[me], slots.at[me], local_sem.at[0])
    local.start()

    def place(o, carry):
        mine = rows[0, o]
        count = jnp.int32(0)
        for other in range(groups):
            theirs = rows[0, other]
            count += (theirs < mine).astype(jnp.int32)
            count += ((theirs == mine) & (other < o)).astype(jnp.int32)
        rank[o] = count
        return carry

    def invert(i, carry):
        slot = jnp.int32(0)
        for o in range(groups):
            slot = jnp.maximum(slot, (rank[o] == i).astype(jnp.int32) * o)
        order[i] = slot
        return carry

    def follow(i, carry):
        same = rows[0, order[i]] == rows[0, order[jnp.maximum(i - 1, 0)]]
        keep[i] = (same & (i > 0)).astype(jnp.int32)
        return carry

    def close(n, carry):
        upto = jnp.int32(0)
        here = jnp.int32(0)
        for o in range(groups):
            upto += (rows[0, o] <= n).astype(jnp.int32)
            here += (rows[0, o] == n).astype(jnp.int32)
        final[n] = jnp.maximum(upto - 1, 0)
        filled[n] = jnp.minimum(here, 1)
        return carry

    lax.fori_loop(0, groups, place, 0)
    lax.fori_loop(0, groups, invert, 0)
    lax.fori_loop(0, groups, follow, 0)
    lax.fori_loop(0, blocks, close, 0)

    def project(block, i):
        return (
            jnp.dot(block, key_w[i], preferred_element_type=F32),
            jnp.dot(block, value_w[i], preferred_element_type=F32),
        )

    def add(source, c, i):
        k, v = project(source[c], i)
        key_acc[c] += k
        value_acc[c] += v

    def finish(c):
        k, v = project(far[c], 3)
        keys[c] = (key_acc[c] + k).astype(BF16)
        values[c] = (value_acc[c] + v).astype(BF16)

    own_load.wait()
    for load in weight_loads[0]:
        load.wait()

    def first(c, carry):
        k, v = project(own[c], 0)
        key_acc[c] = k
        value_acc[c] = v
        return carry

    lax.fori_loop(0, blocks, first, 0)
    for pair in weight_loads[1:]:
        for load in pair:
            load.wait()

    def near(c, carry):
        d = blocks - 1 - c
        go_up(c).wait_recv()
        pass_up(c).start()
        go_down(d).wait_recv()
        pass_down(d).start()
        add(before, c, 1)
        add(after, d, 2)
        return carry

    lax.fori_loop(0, half, near, 0)

    def rest(c, carry):
        d = blocks - 1 - c
        go_up(c).wait_recv()
        add(before, c, 1)
        go_down(d).wait_recv()
        add(after, d, 2)
        return carry

    lax.fori_loop(half, blocks, rest, 0)

    slots_arrive()
    slots_leave()
    local.wait()

    def last(c, carry):
        d = blocks - 1 - c
        pass_up(c).wait_recv()
        finish(c)
        pass_down(d).wait_recv()
        finish(d)
        return carry

    lax.fori_loop(0, half, last, 0)

    heads = keys.shape[2] // HS

    def score(p):
        for h in range(heads):
            k, v, q, g = pair_operands(rows, p, keys, values, slots, 2 * p, h)
            scores = lax.dot_general(k, q, LAST, preferred_element_type=F32) * SCALE
            gp = lax.dot_general(v, g, LAST, preferred_element_type=F32)
            peak = jnp.max(scores, 0, keepdims=True)
            w = jnp.exp(scores - peak)
            total = jnp.sum(w, 0, keepdims=True)
            peaks[p, h : h + 1] = peak
            stats[p, h : h + 1] = peak + jnp.log(total)
            stats[p, heads + h : heads + h + 1] = jnp.sum(w * gp, 0, keepdims=True) / total
            weights[p // blocks, p % blocks, :, h * HS : (h + 1) * HS] = w
            grad_p[p, h] = gp

    stat_to, stats_arrive, stats_leave = send_to_group(
        groups, lambda g: stats.at[g // 2], fetched, stat_send, stat_recv
    )
    local_stat = pltpu.make_async_copy(stats.at[me // 2], fetched.at[me], local_sem.at[2])
    together = 4
    chunks = groups // 2 // together

    def score_some(j, carry):
        first = together * lax.rem(me // (2 * together) + j, chunks)
        for u in range(together):
            score(first + u)
        for u in range(2 * together):
            k = lax.rem(2 * first + u + groups - me, groups)

            @pl.when(k > 0)
            def _():
                stat_to(k).start()

            @pl.when(k == 0)
            def _():
                local_stat.start()

        return carry

    lax.fori_loop(0, chunks, score_some, 0)

    def sent(c, carry):
        go_up(c).wait_send()
        go_down(c).wait_send()
        return carry

    lax.fori_loop(0, blocks, sent, 0)

    def passed(c, carry):
        pass_up(c).wait_send()
        pass_down(blocks - 1 - c).wait_send()
        return carry

    lax.fori_loop(0, half, passed, 0)
    local_stat.wait()
    stats_arrive()

    def combine(t, carry):
        a = fetched[reads[0, t]]
        b = fetched[reads[1, t]]
        overall = jnp.maximum(a[:heads], b[:heads])
        fa, fb = jnp.exp(a[:heads] - overall), jnp.exp(b[:heads] - overall)
        total = fa + fb
        combined[t, :heads] = overall + jnp.log(total)
        combined[t, heads:] = (fa * a[heads:] + fb * b[heads:]) / total
        return carry

    lax.fori_loop(0, spans, combine, 0, unroll=8)
    back_to, backs_arrive, backs_leave = send_to_group(
        groups, lambda g: back.at[g], landed, back_send, back_recv
    )

    def answer(o):
        mine = combined[source[o]]
        back[o] = jnp.where(live[o] > 0, mine, jnp.zeros_like(mine))

    def answer_to(k, carry):
        answer(lax.rem(me + k, groups))
        back_to(k).start()
        return carry

    lax.fori_loop(1, groups, answer_to, 0)
    answer(me)
    local = pltpu.make_async_copy(back.at[me], landed.at[me], local_sem.at[3])
    local.start()
    local.wait()
    backs_arrive()
    left = lax.broadcasted_iota(jnp.int32, landed.shape[1:], 1) < CLEN

    def normalise(p, carry):
        both = jnp.where(left, landed[2 * p], landed[2 * p + 1])
        for h in range(heads):
            factor = jnp.exp(peaks[p, h : h + 1] - both[h : h + 1])
            pr = weights[p // blocks, p % blocks, :, h * HS : (h + 1) * HS] * factor
            probs[p, h] = pr.astype(BF16)
            grad_s[p, h] = (pr * (grad_p[p, h] - both[heads + h : heads + h + 1])).astype(BF16)
        return carry

    lax.fori_loop(0, groups // 2, normalise, 0, unroll=2)

    half_lane = lax.broadcasted_iota(jnp.int32, (NLEN, 2 * CLEN), 1) // CLEN
    key_run[...] = jnp.zeros_like(key_run)
    value_run[...] = jnp.zeros_like(value_run)

    def accumulate(i, carry):
        slot = order[i]
        pair = slot // 2
        mine = half_lane == lax.rem(slot, 2)
        more = keep[i].astype(F32)
        for h in range(heads):
            cols = pl.ds(h * HS, HS)
            zero = jnp.zeros((NLEN, 2 * CLEN), BF16)
            p = jnp.where(mine, probs[pair, h], zero)
            s = jnp.where(mine, grad_s[pair, h], zero)
            q, g = slots[slot, 0, :, cols], slots[slot, 1, :, cols]
            k = key_run[:, cols] * more + jnp.dot(
                s, jnp.concatenate([q, q], 0), preferred_element_type=F32
            )
            v = value_run[:, cols] * more + jnp.dot(
                p, jnp.concatenate([g, g], 0), preferred_element_type=F32
            )
            key_run[:, cols] = k
            value_run[:, cols] = v
            outgoing[i, :, :, cols] = (k * SCALE).astype(BF16).reshape(2, CLEN, HS)
            value_sums[i, :, :, cols] = v.astype(BF16).reshape(2, CLEN, HS)
        return carry

    lax.fori_loop(0, groups, accumulate, 0, unroll=8)
    width = keys.shape[2]

    def gather(n):
        for j, sums in enumerate((outgoing, value_sums)):
            block = sums[final[n]].reshape(NLEN, width)
            far[n, :, j * width : (j + 1) * width] = jnp.where(
                filled[n] > 0, block, jnp.zeros_like(block)
            )


    def part(c, i):
        return lax.dot_general(
            far[c, :, :width], key_w[i], LAST, preferred_element_type=F32
        ) + lax.dot_general(far[c, :, width:], value_w[i], LAST, preferred_element_type=F32)

    def sum_copy(lane, source, target, block, to):
        return pltpu.make_async_remote_copy(
            src_ref=source.at[block],
            dst_ref=target.at[block],
            send_sem=sum_send.at[lane, block],
            recv_sem=sum_recv.at[lane, block],
            device_id={"mp": to},
            device_id_type=MESH,
        )

    to_across, to_up, to_down = own, before, after

    def far_up(c):
        return sum_copy(2, to_across, from_far, c, up)

    def far_down(c):
        return sum_copy(2, to_across, from_far, c, down)

    def sum_up(c):
        return sum_copy(0, to_up, from_below, c, up)

    def sum_down(c):
        return sum_copy(1, to_down, from_above, c, down)

    def send_far(c, carry):
        d = blocks - 1 - c
        gather(c)
        to_across[c] = part(c, 3).astype(BF16)
        far_up(c).start()
        gather(d)
        to_across[d] = part(d, 3).astype(BF16)
        far_down(d).start()
        return carry

    lax.fori_loop(0, half, send_far, 0)
    results = slots
    top = lax.broadcasted_iota(jnp.int32, (2 * CLEN, HS), 0) < CLEN

    def answers(p, carry):
        low, high = rows[0, 2 * p], rows[0, 2 * p + 1]
        for h in range(heads):
            cols = pl.ds(h * HS, HS)
            k = jnp.concatenate([keys[low, :, cols], keys[high, :, cols]], 1)
            v = jnp.concatenate([values[low, :, cols], values[high, :, cols]], 1)
            out = lax.dot_general(probs[p, h], v, FIRST, preferred_element_type=F32)
            gq = lax.dot_general(grad_s[p, h], k, FIRST, preferred_element_type=F32) * SCALE
            for j, both in enumerate((out, gq)):
                picked = jnp.where(top, both[:, :HS], both[:, HS:]).astype(BF16)
                results[pl.ds(2 * p, 2), j, :, cols] = picked.reshape(2, CLEN, HS)
        return carry

    lax.fori_loop(0, groups // 2, answers, 0, unroll=4)
    answer_copy, answers_arrive, answers_leave = send_to_group(
        groups, lambda g: results.at[g], answers_in, answer_send, answer_recv
    )
    start_all(groups, answer_copy)
    local_answer = pltpu.make_async_copy(results.at[me], answers_in.at[me], local_sem.at[1])
    local_answer.start()

    def send_near(c, carry):
        d = blocks - 1 - c
        to_up[c] = part(c, 2).astype(BF16)
        sum_up(c).start()
        to_down[d] = part(d, 1).astype(BF16)
        sum_down(d).start()
        return carry

    lax.fori_loop(half, blocks, send_near, 0)

    def send_joined(c, carry):
        d = blocks - 1 - c
        mine = part(c, 2)
        far_up(c).wait_recv()
        to_up[c] = (mine + from_far[c].astype(F32)).astype(BF16)
        sum_up(c).start()
        mine = part(d, 1)
        far_down(d).wait_recv()
        to_down[d] = (mine + from_far[d].astype(F32)).astype(BF16)
        sum_down(d).start()
        return carry

    lax.fori_loop(0, half, send_joined, 0)

    def keep_own(c, carry):
        mine = part(c, 0)
        key_acc[c] = mine[:, :width]
        value_acc[c] = mine[:, width:]
        return carry

    lax.fori_loop(0, blocks, keep_own, 0)

    def total(c, arrived):
        other = arrived[c].astype(F32)
        return key_acc[c] + other[:, :width], value_acc[c] + other[:, width:]

    def add_first(c, carry):
        d = blocks - 1 - c
        sum_up(c).wait_recv()
        key_acc[c], value_acc[c] = total(c, from_below)
        sum_down(d).wait_recv()
        key_acc[d], value_acc[d] = total(d, from_above)
        return carry

    lax.fori_loop(half, blocks, add_first, 0)
    local_answer.wait()
    answers_arrive()
    answers_leave()
    stats_leave()
    backs_leave()

    def finish_span(t, carry):
        a, b = reads[0, t], reads[1, t]
        for j, target in enumerate((attended, grad_q)):
            target[t] = (answers_in[a, j].astype(F32) + answers_in[b, j].astype(F32)).astype(BF16)
        return carry

    lax.fori_loop(0, spans, finish_span, 0)
    def sent_far(c, carry):
        far_up(c).wait_send()
        far_down(blocks - 1 - c).wait_send()
        return carry

    lax.fori_loop(0, half, sent_far, 0)

    def emit(c, arrived):
        low, high = total(c, arrived)
        grad_e[c, :, :width] = low.astype(BF16)
        grad_e[c, :, width:] = high.astype(BF16)

    def add_last(c, carry):
        d = blocks - 1 - c
        sum_up(c).wait_recv()
        emit(c, from_below)
        sum_down(d).wait_recv()
        emit(d, from_above)
        return carry

    lax.fori_loop(0, half, add_last, 0)

    def sums_sent(c, carry):
        sum_up(c).wait_send()
        sum_down(c).wait_send()
        return carry

    lax.fori_loop(0, blocks, sums_sent, 0)


def params(collective_id=None, mib=56):
    return pltpu.CompilerParams(
        collective_id=collective_id,
        has_side_effects=collective_id is not None,
        vmem_limit_bytes=mib << 20,
    )


def body(queries, grad_out, encoded, key_weight, value_weight, send_rows, read_slots):
    groups = lax.axis_size(("phase", "dp"))
    ring = lax.axis_size("mp")
    blocks, _, features = encoded.shape
    width = key_weight.shape[1]
    heads = width // HS
    spans = read_slots.shape[0]
    hbm = pl.BlockSpec(memory_space=pl.ANY)
    vmem = pl.BlockSpec(memory_space=pltpu.VMEM)
    smem = pl.BlockSpec(memory_space=pltpu.SMEM)
    dma = pltpu.SemaphoreType.DMA
    half_pairs = groups // 2

    rows = send_rows.reshape(1, groups)
    reads = read_slots.T
    query_spans = queries.reshape(spans, CLEN, width)
    grad_spans = grad_out.reshape(spans, CLEN, width)
    key_parts = key_weight.reshape(ring, features, width)
    value_parts = value_weight.reshape(ring, features, width)
    block_shape = jax.ShapeDtypeStruct((blocks, NLEN, width), BF16)
    slot_shape = jax.ShapeDtypeStruct((groups, 2, CLEN, width), BF16)
    prob_shape = jax.ShapeDtypeStruct((half_pairs, heads, NLEN, 2 * CLEN), BF16)

    stat_shape = (groups, 2 * heads, 2 * CLEN)
    factor_shape = (groups, 2 * heads, 2 * CLEN)
    span_shape = jax.ShapeDtypeStruct((spans, CLEN, width), BF16)
    attended, grad_q, grad_e = pl.pallas_call(
        functools.partial(retro_kernel, groups),
        out_shape=(
            pltpu.VMEM(span_shape.shape, BF16),
            pltpu.VMEM(span_shape.shape, BF16),
            pltpu.VMEM(encoded.shape, BF16),
        ),
        in_specs=[smem, smem, hbm, hbm, hbm, hbm, hbm],
        out_specs=(vmem, vmem, vmem),
        scratch_shapes=[
            pltpu.SMEM((groups,), jnp.int32),
            pltpu.SMEM((groups,), jnp.int32),
            pltpu.SMEM((groups,), jnp.int32),
            pltpu.SMEM((groups,), jnp.int32),
            pltpu.SMEM((groups,), jnp.int32),
            pltpu.SMEM((blocks,), jnp.int32),
            pltpu.SMEM((blocks,), jnp.int32),
            pltpu.VMEM(span_shape.shape, BF16),
            pltpu.VMEM(span_shape.shape, BF16),
            pltpu.VMEM(slot_shape.shape, BF16),
            pltpu.VMEM(slot_shape.shape, BF16),
            pltpu.VMEM(encoded.shape, BF16),
            pltpu.VMEM(encoded.shape, BF16),
            pltpu.VMEM(encoded.shape, BF16),
            pltpu.VMEM(encoded.shape, BF16),
            pltpu.VMEM(key_parts.shape, BF16),
            pltpu.VMEM(key_parts.shape, BF16),
            pltpu.VMEM((2,) + block_shape.shape, F32),
            pltpu.VMEM(block_shape.shape, BF16),
            pltpu.VMEM(block_shape.shape, BF16),
            pltpu.VMEM(prob_shape.shape, BF16),
            pltpu.VMEM(prob_shape.shape, BF16),
            pltpu.VMEM(prob_shape.shape, F32),
            pltpu.VMEM((half_pairs,) + stat_shape[1:], F32),
            pltpu.VMEM((half_pairs,) + stat_shape[1:], F32),
            pltpu.VMEM(stat_shape, F32),
            pltpu.VMEM((spans,) + factor_shape[1:], F32),
            pltpu.VMEM(factor_shape, F32),
            pltpu.VMEM(factor_shape, F32),
            pltpu.VMEM((NLEN, width), F32),
            pltpu.VMEM((NLEN, width), F32),
            pltpu.VMEM(slot_shape.shape, BF16),
            pltpu.VMEM(slot_shape.shape, BF16),
            pltpu.VMEM(encoded.shape, BF16),
            pltpu.VMEM(encoded.shape, BF16),
            pltpu.VMEM(encoded.shape, BF16),
            dma((11,)),
            dma((3, blocks)),
            dma((3, blocks)),
            dma((groups,)),
            dma((groups,)),
            dma((4,)),
            dma((groups,)),
            dma((groups,)),
            dma((groups,)),
            dma((groups,)),
            dma((3, blocks)),
            dma((3, blocks)),
            dma((groups,)),
            dma((groups,)),
        ],
        compiler_params=params(0, 58),
        name="retro",
    )(rows, reads, query_spans, grad_spans, encoded, key_parts, value_parts)
    return (attended.reshape(queries.shape), grad_q.reshape(queries.shape), grad_e)


def solution(mesh):
    return jax.shard_map(
        body,
        mesh=mesh,
        in_specs=(
            P(("phase", "dp"), "mp"),
            P(("phase", "dp"), "mp"),
            P(("phase", "dp"), None, "mp"),
            P(None, "mp"),
            P(None, "mp"),
            P(("phase", "dp"), None, None),
            P(("phase", "dp"), None),
        ),
        out_specs=(
            P(("phase", "dp"), "mp"),
            P(("phase", "dp"), "mp"),
            P(("phase", "dp"), None, "mp"),
        ),
        check_vma=False,
    )
```

```python
import functools

import jax
import jax.numpy as jnp
from jax import lax
from jax.experimental import pallas as pl
from jax.experimental.pallas import tpu as pltpu
from jax.sharding import PartitionSpec as P

HS = 128
CLEN = 64
NLEN = 128
SCALE = HS ** (-0.5)
LAST = (((1,), (1,)), ((), ()))
FIRST = (((0,), (0,)), ((), ()))
MESH = pl.DeviceIdType.MESH
F32 = jnp.float32
BF16 = jnp.bfloat16


def group_index():
    return lax.axis_index("phase") * lax.axis_size("dp") + lax.axis_index("dp")


def peer_id(group):
    dp = lax.axis_size("dp")
    return {"phase": group // dp, "dp": lax.rem(group, dp)}


def greet_group(barrier, groups):
    me = group_index()

    def greet(k, carry):
        pl.semaphore_signal(
            barrier, inc=1, device_id=peer_id(lax.rem(me + k, groups)), device_id_type=MESH
        )
        return carry

    lax.fori_loop(1, groups, greet, 0)


def send_to_group(groups, source, target, send_sem, recv_sem):
    me = group_index()

    def copy_to(k):
        peer = lax.rem(me + k, groups)
        return pltpu.make_async_remote_copy(
            src_ref=source(peer),
            dst_ref=target.at[me],
            send_sem=send_sem,
            recv_sem=recv_sem,
            device_id=peer_id(peer),
            device_id_type=MESH,
        )

    def everything():
        others = target.at[pl.ds(0, groups - 1)]
        return pltpu.make_async_remote_copy(
            src_ref=others,
            dst_ref=others,
            send_sem=send_sem,
            recv_sem=recv_sem,
            device_id=peer_id(lax.rem(me + 1, groups)),
            device_id_type=MESH,
        )

    def arrive():
        everything().wait_recv()

    def leave():
        everything().wait_send()

    return copy_to, arrive, leave


def start_all(groups, copy_to):
    lax.fori_loop(1, groups, lambda k, c: (copy_to(k).start(), c)[1], 0)


def diagonal(slots, first, which, cols):
    top = lax.broadcasted_iota(jnp.int32, (2 * CLEN, HS), 0) < CLEN
    block = slots[pl.ds(first, 2), which, :, cols].reshape(2 * CLEN, HS)
    zero = jnp.zeros_like(block)
    return jnp.concatenate([jnp.where(top, block, zero), jnp.where(top, zero, block)], 1)


def pair_operands(rows, pair, keys, values, slots, first, h):
    cols = pl.ds(h * HS, HS)
    low, high = rows[0, 2 * pair], rows[0, 2 * pair + 1]
    k = jnp.concatenate([keys[low, :, cols], keys[high, :, cols]], 1)
    v = jnp.concatenate([values[low, :, cols], values[high, :, cols]], 1)
    return k, v, diagonal(slots, first, 0, cols), diagonal(slots, first, 1, cols)


def retro_kernel(
    groups, rows, reads, queries, grads, encoded, key_weight, value_weight,
    attended, grad_q, grad_e,
    source, live, rank, order, keep, final, filled,
    query_in, grad_in, outgoing, slots, own, before, after, far, key_w, value_w,
    totals, keys, values, probs, grad_s, grad_p,
    peaks, stats, fetched, combined, back, landed, key_run, value_run, value_sums,
    answers_in, from_far, from_below, from_above,
    load_sem, ring_send, ring_recv, send_sem, recv_sem, local_sem,
    stat_send, stat_recv, back_send, back_recv,
    sum_send, sum_recv, answer_send, answer_recv,
):
    me = group_index()
    z = lax.axis_index("mp")
    ring = lax.axis_size("mp")
    up, down = lax.rem(z + 1, ring), lax.rem(z + ring - 1, ring)
    across = lax.rem(z + 2, ring)
    blocks = encoded.shape[0]
    half = blocks // 2
    key_acc, value_acc, weights = totals.at[0], totals.at[1], totals

    barrier = pltpu.get_barrier_semaphore()
    pl.semaphore_signal(barrier, inc=1, device_id={"mp": up}, device_id_type=MESH)
    pl.semaphore_signal(barrier, inc=1, device_id={"mp": down}, device_id_type=MESH)
    greet_group(barrier, groups)

    inputs = (
        pltpu.make_async_copy(queries, query_in, load_sem.at[9]),
        pltpu.make_async_copy(grads, grad_in, load_sem.at[10]),
    )
    for load in inputs:
        load.start()
    own_load = pltpu.make_async_copy(encoded, own, load_sem.at[0])
    own_load.start()
    weight_loads = []
    for i, owner in enumerate((z, down, up, across)):
        pair = (
            pltpu.make_async_copy(key_weight.at[owner], key_w.at[i], load_sem.at[1 + 2 * i]),
            pltpu.make_async_copy(value_weight.at[owner], value_w.at[i], load_sem.at[2 + 2 * i]),
        )
        for load in pair:
            load.start()
        weight_loads.append(pair)

    def ring_copy(lane, source, target, block, to):
        return pltpu.make_async_remote_copy(
            src_ref=source.at[block],
            dst_ref=target.at[block],
            send_sem=ring_send.at[lane],
            recv_sem=ring_recv.at[lane, block],
            device_id={"mp": to},
            device_id_type=MESH,
        )

    def go_up(c):
        return ring_copy(0, encoded, before, c, up)

    def go_down(c):
        return ring_copy(1, encoded, after, c, down)

    def pass_up(c):
        return ring_copy(2, before, far, c, up)

    def pass_down(c):
        return ring_copy(2, after, far, c, down)

    pl.semaphore_wait(barrier, groups - 1 + 2)

    def send_own(c, carry):
        go_up(c).start()
        go_down(blocks - 1 - c).start()
        return carry

    lax.fori_loop(0, blocks, send_own, 0)
    spans = queries.shape[0]

    def fill(o, carry):
        span = jnp.int32(0)
        found = jnp.int32(0)
        for t in range(spans):
            for j in range(2):
                hit = (reads[j, t] == o).astype(jnp.int32)
                span = jnp.maximum(span, hit * t)
                found = jnp.maximum(found, hit)
        source[o] = span
        live[o] = found
        for j, array in enumerate((query_in, grad_in)):
            block = array[span]
            outgoing[o, j] = jnp.where(found > 0, block, jnp.zeros_like(block))
        return carry

    for load in inputs:
        load.wait()
    lax.fori_loop(0, groups, fill, 0)
    slot_to, slots_arrive, slots_leave = send_to_group(
        groups, lambda g: outgoing.at[g], slots, send_sem, recv_sem
    )
    start_all(groups, slot_to)
    local = pltpu.make_async_copy(outgoing.at[me], slots.at[me], local_sem.at[0])
    local.start()

    def place(o, carry):
        mine = rows[0, o]
        count = jnp.int32(0)
        for other in range(groups):
            theirs = rows[0, other]
            count += (theirs < mine).astype(jnp.int32)
            count += ((theirs == mine) & (other < o)).astype(jnp.int32)
        rank[o] = count
        return carry

    def invert(i, carry):
        slot = jnp.int32(0)
        for o in range(groups):
            slot = jnp.maximum(slot, (rank[o] == i).astype(jnp.int32) * o)
        order[i] = slot
        return carry

    def follow(i, carry):
        same = rows[0, order[i]] == rows[0, order[jnp.maximum(i - 1, 0)]]
        keep[i] = (same & (i > 0)).astype(jnp.int32)
        return carry

    def close(n, carry):
        upto = jnp.int32(0)
        here = jnp.int32(0)
        for o in range(groups):
            upto += (rows[0, o] <= n).astype(jnp.int32)
            here += (rows[0, o] == n).astype(jnp.int32)
        final[n] = jnp.maximum(upto - 1, 0)
        filled[n] = jnp.minimum(here, 1)
        return carry

    lax.fori_loop(0, groups, place, 0)
    lax.fori_loop(0, groups, invert, 0)
    lax.fori_loop(0, groups, follow, 0)
    lax.fori_loop(0, blocks, close, 0)

    def project(block, i):
        return (
            jnp.dot(block, key_w[i], preferred_element_type=F32),
            jnp.dot(block, value_w[i], preferred_element_type=F32),
        )

    def add(source, c, i):
        k, v = project(source[c], i)
        key_acc[c] += k
        value_acc[c] += v

    def finish(c):
        k, v = project(far[c], 3)
        keys[c] = (key_acc[c] + k).astype(BF16)
        values[c] = (value_acc[c] + v).astype(BF16)

    own_load.wait()
    for load in weight_loads[0]:
        load.wait()

    def first(c, carry):
        k, v = project(own[c], 0)
        key_acc[c] = k
        value_acc[c] = v
        return carry

    lax.fori_loop(0, blocks, first, 0)
    for pair in weight_loads[1:]:
        for load in pair:
            load.wait()

    def near(c, carry):
        d = blocks - 1 - c
        go_up(c).wait_recv()
        pass_up(c).start()
        go_down(d).wait_recv()
        pass_down(d).start()
        add(before, c, 1)
        add(after, d, 2)
        return carry

    lax.fori_loop(0, half, near, 0)

    def rest(c, carry):
        d = blocks - 1 - c
        go_up(c).wait_recv()
        add(before, c, 1)
        go_down(d).wait_recv()
        add(after, d, 2)
        return carry

    lax.fori_loop(half, blocks, rest, 0)

    slots_arrive()
    slots_leave()
    local.wait()

    def last(c, carry):
        d = blocks - 1 - c
        pass_up(c).wait_recv()
        finish(c)
        pass_down(d).wait_recv()
        finish(d)
        return carry

    lax.fori_loop(0, half, last, 0)

    heads = keys.shape[2] // HS

    def score(p):
        for h in range(heads):
            k, v, q, g = pair_operands(rows, p, keys, values, slots, 2 * p, h)
            scores = lax.dot_general(k, q, LAST, preferred_element_type=F32) * SCALE
            gp = lax.dot_general(v, g, LAST, preferred_element_type=F32)
            peak = jnp.max(scores, 0, keepdims=True)
            w = jnp.exp(scores - peak)
            total = jnp.sum(w, 0, keepdims=True)
            peaks[p, h : h + 1] = peak
            stats[p, h : h + 1] = peak + jnp.log(total)
            stats[p, heads + h : heads + h + 1] = jnp.sum(w * gp, 0, keepdims=True) / total
            weights[p // blocks, p % blocks, :, h * HS : (h + 1) * HS] = w
            grad_p[p, h] = gp

    stat_to, stats_arrive, stats_leave = send_to_group(
        groups, lambda g: stats.at[g // 2], fetched, stat_send, stat_recv
    )
    local_stat = pltpu.make_async_copy(stats.at[me // 2], fetched.at[me], local_sem.at[2])
    together = 4
    chunks = groups // 2 // together

    def score_some(j, carry):
        first = together * lax.rem(me // (2 * together) + j, chunks)
        for u in range(together):
            score(first + u)
        for u in range(2 * together):
            k = lax.rem(2 * first + u + groups - me, groups)

            @pl.when(k > 0)
            def _():
                stat_to(k).start()

            @pl.when(k == 0)
            def _():
                local_stat.start()

        return carry

    lax.fori_loop(0, chunks, score_some, 0)

    def all_sent(lane, source, sem):
        pltpu.make_async_remote_copy(
            src_ref=source,
            dst_ref=source,
            send_sem=sem.at[lane],
            recv_sem=ring_recv.at[0, 0],
            device_id={"mp": up},
            device_id_type=MESH,
        ).wait_send()

    for lane in range(3):
        all_sent(lane, far, ring_send)

    local_stat.wait()
    stats_arrive()

    def combine(t, carry):
        a = fetched[reads[0, t]]
        b = fetched[reads[1, t]]
        overall = jnp.maximum(a[:heads], b[:heads])
        fa, fb = jnp.exp(a[:heads] - overall), jnp.exp(b[:heads] - overall)
        total = fa + fb
        combined[t, :heads] = overall + jnp.log(total)
        combined[t, heads:] = (fa * a[heads:] + fb * b[heads:]) / total
        return carry

    lax.fori_loop(0, spans, combine, 0, unroll=8)
    back_to, backs_arrive, backs_leave = send_to_group(
        groups, lambda g: back.at[g], landed, back_send, back_recv
    )

    def answer(o):
        mine = combined[source[o]]
        back[o] = jnp.where(live[o] > 0, mine, jnp.zeros_like(mine))

    def answer_to(k, carry):
        answer(lax.rem(me + k, groups))
        back_to(k).start()
        return carry

    lax.fori_loop(1, groups, answer_to, 0)
    answer(me)
    local = pltpu.make_async_copy(back.at[me], landed.at[me], local_sem.at[3])
    local.start()
    local.wait()
    backs_arrive()
    left = lax.broadcasted_iota(jnp.int32, landed.shape[1:], 1) < CLEN

    def normalise(p, carry):
        both = jnp.where(left, landed[2 * p], landed[2 * p + 1])
        for h in range(heads):
            factor = jnp.exp(peaks[p, h : h + 1] - both[h : h + 1])
            pr = weights[p // blocks, p % blocks, :, h * HS : (h + 1) * HS] * factor
            probs[p, h] = pr.astype(BF16)
            grad_s[p, h] = (pr * (grad_p[p, h] - both[heads + h : heads + h + 1])).astype(BF16)
        return carry

    lax.fori_loop(0, groups // 2, normalise, 0, unroll=2)

    half_lane = lax.broadcasted_iota(jnp.int32, (NLEN, 2 * CLEN), 1) // CLEN
    key_run[...] = jnp.zeros_like(key_run)
    value_run[...] = jnp.zeros_like(value_run)

    def accumulate(i, carry):
        slot = order[i]
        pair = slot // 2
        mine = half_lane == lax.rem(slot, 2)
        more = keep[i].astype(F32)
        for h in range(heads):
            cols = pl.ds(h * HS, HS)
            zero = jnp.zeros((NLEN, 2 * CLEN), BF16)
            p = jnp.where(mine, probs[pair, h], zero)
            s = jnp.where(mine, grad_s[pair, h], zero)
            q, g = slots[slot, 0, :, cols], slots[slot, 1, :, cols]
            k = key_run[:, cols] * more + jnp.dot(
                s, jnp.concatenate([q, q], 0), preferred_element_type=F32
            )
            v = value_run[:, cols] * more + jnp.dot(
                p, jnp.concatenate([g, g], 0), preferred_element_type=F32
            )
            key_run[:, cols] = k
            value_run[:, cols] = v
            outgoing[i, :, :, cols] = (k * SCALE).astype(BF16).reshape(2, CLEN, HS)
            value_sums[i, :, :, cols] = v.astype(BF16).reshape(2, CLEN, HS)
        return carry

    lax.fori_loop(0, groups, accumulate, 0, unroll=8)
    width = keys.shape[2]

    def gather(n):
        for j, sums in enumerate((outgoing, value_sums)):
            block = sums[final[n]].reshape(NLEN, width)
            far[n, :, j * width : (j + 1) * width] = jnp.where(
                filled[n] > 0, block, jnp.zeros_like(block)
            )


    def part(c, i):
        return lax.dot_general(
            far[c, :, :width], key_w[i], LAST, preferred_element_type=F32
        ) + lax.dot_general(far[c, :, width:], value_w[i], LAST, preferred_element_type=F32)

    def sum_copy(lane, source, target, block, to):
        return pltpu.make_async_remote_copy(
            src_ref=source.at[block],
            dst_ref=target.at[block],
            send_sem=sum_send.at[lane],
            recv_sem=sum_recv.at[lane, block],
            device_id={"mp": to},
            device_id_type=MESH,
        )

    to_across, to_up, to_down = own, before, after

    def far_up(c):
        return sum_copy(2, to_across, from_far, c, up)

    def far_down(c):
        return sum_copy(2, to_across, from_far, c, down)

    def sum_up(c):
        return sum_copy(0, to_up, from_below, c, up)

    def sum_down(c):
        return sum_copy(1, to_down, from_above, c, down)

    def send_far(c, carry):
        d = blocks - 1 - c
        gather(c)
        to_across[c] = part(c, 3).astype(BF16)
        far_up(c).start()
        gather(d)
        to_across[d] = part(d, 3).astype(BF16)
        far_down(d).start()
        return carry

    lax.fori_loop(0, half, send_far, 0)
    results = slots
    top = lax.broadcasted_iota(jnp.int32, (2 * CLEN, HS), 0) < CLEN

    def answers(p, carry):
        low, high = rows[0, 2 * p], rows[0, 2 * p + 1]
        for h in range(heads):
            cols = pl.ds(h * HS, HS)
            k = jnp.concatenate([keys[low, :, cols], keys[high, :, cols]], 1)
            v = jnp.concatenate([values[low, :, cols], values[high, :, cols]], 1)
            out = lax.dot_general(probs[p, h], v, FIRST, preferred_element_type=F32)
            gq = lax.dot_general(grad_s[p, h], k, FIRST, preferred_element_type=F32) * SCALE
            for j, both in enumerate((out, gq)):
                picked = jnp.where(top, both[:, :HS], both[:, HS:]).astype(BF16)
                results[pl.ds(2 * p, 2), j, :, cols] = picked.reshape(2, CLEN, HS)
        return carry

    lax.fori_loop(0, groups // 2, answers, 0, unroll=4)
    answer_copy, answers_arrive, answers_leave = send_to_group(
        groups, lambda g: results.at[g], answers_in, answer_send, answer_recv
    )
    start_all(groups, answer_copy)
    local_answer = pltpu.make_async_copy(results.at[me], answers_in.at[me], local_sem.at[1])
    local_answer.start()

    def send_near(c, carry):
        d = blocks - 1 - c
        to_up[c] = part(c, 2).astype(BF16)
        sum_up(c).start()
        to_down[d] = part(d, 1).astype(BF16)
        sum_down(d).start()
        return carry

    lax.fori_loop(half, blocks, send_near, 0)

    def send_joined(c, carry):
        d = blocks - 1 - c
        mine = part(c, 2)
        far_up(c).wait_recv()
        to_up[c] = (mine + from_far[c].astype(F32)).astype(BF16)
        sum_up(c).start()
        mine = part(d, 1)
        far_down(d).wait_recv()
        to_down[d] = (mine + from_far[d].astype(F32)).astype(BF16)
        sum_down(d).start()
        return carry

    lax.fori_loop(0, half, send_joined, 0)

    def keep_own(c, carry):
        mine = part(c, 0)
        key_acc[c] = mine[:, :width]
        value_acc[c] = mine[:, width:]
        return carry

    lax.fori_loop(0, blocks, keep_own, 0)

    def total(c, arrived):
        other = arrived[c].astype(F32)
        return key_acc[c] + other[:, :width], value_acc[c] + other[:, width:]

    def add_first(c, carry):
        d = blocks - 1 - c
        sum_up(c).wait_recv()
        key_acc[c], value_acc[c] = total(c, from_below)
        sum_down(d).wait_recv()
        key_acc[d], value_acc[d] = total(d, from_above)
        return carry

    lax.fori_loop(half, blocks, add_first, 0)
    local_answer.wait()
    answers_arrive()
    answers_leave()
    stats_leave()
    backs_leave()

    def finish_span(t, carry):
        a, b = reads[0, t], reads[1, t]
        for j, target in enumerate((attended, grad_q)):
            target[t] = (answers_in[a, j].astype(F32) + answers_in[b, j].astype(F32)).astype(BF16)
        return carry

    lax.fori_loop(0, spans, finish_span, 0)
    def emit(c, arrived):
        low, high = total(c, arrived)
        grad_e[c, :, :width] = low.astype(BF16)
        grad_e[c, :, width:] = high.astype(BF16)

    def add_last(c, carry):
        d = blocks - 1 - c
        sum_up(c).wait_recv()
        emit(c, from_below)
        sum_down(d).wait_recv()
        emit(d, from_above)
        return carry

    lax.fori_loop(0, half, add_last, 0)

    for lane in range(3):
        all_sent(lane, far, sum_send)


def params(collective_id=None, mib=56):
    return pltpu.CompilerParams(
        collective_id=collective_id,
        has_side_effects=collective_id is not None,
        vmem_limit_bytes=mib << 20,
    )


def body(queries, grad_out, encoded, key_weight, value_weight, send_rows, read_slots):
    groups = lax.axis_size(("phase", "dp"))
    ring = lax.axis_size("mp")
    blocks, _, features = encoded.shape
    width = key_weight.shape[1]
    heads = width // HS
    spans = read_slots.shape[0]
    hbm = pl.BlockSpec(memory_space=pl.ANY)
    vmem = pl.BlockSpec(memory_space=pltpu.VMEM)
    smem = pl.BlockSpec(memory_space=pltpu.SMEM)
    dma = pltpu.SemaphoreType.DMA
    half_pairs = groups // 2

    rows = send_rows.reshape(1, groups)
    reads = read_slots.T
    query_spans = queries.reshape(spans, CLEN, width)
    grad_spans = grad_out.reshape(spans, CLEN, width)
    key_parts = key_weight.reshape(ring, features, width)
    value_parts = value_weight.reshape(ring, features, width)
    block_shape = jax.ShapeDtypeStruct((blocks, NLEN, width), BF16)
    slot_shape = jax.ShapeDtypeStruct((groups, 2, CLEN, width), BF16)
    prob_shape = jax.ShapeDtypeStruct((half_pairs, heads, NLEN, 2 * CLEN), BF16)

    stat_shape = (groups, 2 * heads, 2 * CLEN)
    factor_shape = (groups, 2 * heads, 2 * CLEN)
    span_shape = jax.ShapeDtypeStruct((spans, CLEN, width), BF16)
    attended, grad_q, grad_e = pl.pallas_call(
        functools.partial(retro_kernel, groups),
        out_shape=(
            pltpu.VMEM(span_shape.shape, BF16),
            pltpu.VMEM(span_shape.shape, BF16),
            pltpu.VMEM(encoded.shape, BF16),
        ),
        in_specs=[smem, smem, hbm, hbm, hbm, hbm, hbm],
        out_specs=(vmem, vmem, vmem),
        scratch_shapes=[
            pltpu.SMEM((groups,), jnp.int32),
            pltpu.SMEM((groups,), jnp.int32),
            pltpu.SMEM((groups,), jnp.int32),
            pltpu.SMEM((groups,), jnp.int32),
            pltpu.SMEM((groups,), jnp.int32),
            pltpu.SMEM((blocks,), jnp.int32),
            pltpu.SMEM((blocks,), jnp.int32),
            pltpu.VMEM(span_shape.shape, BF16),
            pltpu.VMEM(span_shape.shape, BF16),
            pltpu.VMEM(slot_shape.shape, BF16),
            pltpu.VMEM(slot_shape.shape, BF16),
            pltpu.VMEM(encoded.shape, BF16),
            pltpu.VMEM(encoded.shape, BF16),
            pltpu.VMEM(encoded.shape, BF16),
            pltpu.VMEM(encoded.shape, BF16),
            pltpu.VMEM(key_parts.shape, BF16),
            pltpu.VMEM(key_parts.shape, BF16),
            pltpu.VMEM((2,) + block_shape.shape, F32),
            pltpu.VMEM(block_shape.shape, BF16),
            pltpu.VMEM(block_shape.shape, BF16),
            pltpu.VMEM(prob_shape.shape, BF16),
            pltpu.VMEM(prob_shape.shape, BF16),
            pltpu.VMEM(prob_shape.shape, F32),
            pltpu.VMEM((half_pairs,) + stat_shape[1:], F32),
            pltpu.VMEM((half_pairs,) + stat_shape[1:], F32),
            pltpu.VMEM(stat_shape, F32),
            pltpu.VMEM((spans,) + factor_shape[1:], F32),
            pltpu.VMEM(factor_shape, F32),
            pltpu.VMEM(factor_shape, F32),
            pltpu.VMEM((NLEN, width), F32),
            pltpu.VMEM((NLEN, width), F32),
            pltpu.VMEM(slot_shape.shape, BF16),
            pltpu.VMEM(slot_shape.shape, BF16),
            pltpu.VMEM(encoded.shape, BF16),
            pltpu.VMEM(encoded.shape, BF16),
            pltpu.VMEM(encoded.shape, BF16),
            dma((11,)),
            dma((3,)),
            dma((3, blocks)),
            dma,
            dma,
            dma((4,)),
            dma,
            dma,
            dma,
            dma,
            dma((3,)),
            dma((3, blocks)),
            dma,
            dma,
        ],
        compiler_params=params(0, 58),
        name="retro",
    )(rows, reads, query_spans, grad_spans, encoded, key_parts, value_parts)
    return (attended.reshape(queries.shape), grad_q.reshape(queries.shape), grad_e)


def solution(mesh):
    return jax.shard_map(
        body,
        mesh=mesh,
        in_specs=(
            P(("phase", "dp"), "mp"),
            P(("phase", "dp"), "mp"),
            P(("phase", "dp"), None, "mp"),
            P(None, "mp"),
            P(None, "mp"),
            P(("phase", "dp"), None, None),
            P(("phase", "dp"), None),
        ),
        out_specs=(
            P(("phase", "dp"), "mp"),
            P(("phase", "dp"), "mp"),
            P(("phase", "dp"), None, "mp"),
        ),
        check_vma=False,
    )
```

```python
import functools

import jax
import jax.numpy as jnp
from jax import lax
from jax.experimental import pallas as pl
from jax.experimental.pallas import tpu as pltpu
from jax.sharding import PartitionSpec as P

HS = 128
CLEN = 64
NLEN = 128
SCALE = HS ** (-0.5)
LAST = (((1,), (1,)), ((), ()))
FIRST = (((0,), (0,)), ((), ()))
MESH = pl.DeviceIdType.MESH
F32 = jnp.float32
BF16 = jnp.bfloat16


def group_index():
    return lax.axis_index("phase") * lax.axis_size("dp") + lax.axis_index("dp")


def peer_id(group):
    dp = lax.axis_size("dp")
    return {"phase": group // dp, "dp": lax.rem(group, dp)}


def greet_group(barrier, groups):
    me = group_index()

    def greet(k, carry):
        pl.semaphore_signal(
            barrier, inc=1, device_id=peer_id(lax.rem(me + k, groups)), device_id_type=MESH
        )
        return carry

    lax.fori_loop(1, groups, greet, 0)


def send_to_group(groups, source, target, send_sem, recv_sem):
    me = group_index()

    def copy_to(k):
        peer = lax.rem(me + k, groups)
        return pltpu.make_async_remote_copy(
            src_ref=source(peer),
            dst_ref=target.at[me],
            send_sem=send_sem,
            recv_sem=recv_sem,
            device_id=peer_id(peer),
            device_id_type=MESH,
        )

    def everything():
        others = target.at[pl.ds(0, groups - 1)]
        return pltpu.make_async_remote_copy(
            src_ref=others,
            dst_ref=others,
            send_sem=send_sem,
            recv_sem=recv_sem,
            device_id=peer_id(lax.rem(me + 1, groups)),
            device_id_type=MESH,
        )

    def arrive():
        everything().wait_recv()

    def leave():
        everything().wait_send()

    return copy_to, arrive, leave


def start_all(groups, copy_to):
    lax.fori_loop(1, groups, lambda k, c: (copy_to(k).start(), c)[1], 0)


def diagonal(slots, first, which, cols):
    top = lax.broadcasted_iota(jnp.int32, (2 * CLEN, HS), 0) < CLEN
    block = slots[pl.ds(first, 2), which, :, cols].reshape(2 * CLEN, HS)
    zero = jnp.zeros_like(block)
    return jnp.concatenate([jnp.where(top, block, zero), jnp.where(top, zero, block)], 1)


def pair_operands(rows, pair, keys, values, slots, first, h):
    cols = pl.ds(h * HS, HS)
    low, high = rows[0, 2 * pair], rows[0, 2 * pair + 1]
    k = jnp.concatenate([keys[low, :, cols], keys[high, :, cols]], 1)
    v = jnp.concatenate([values[low, :, cols], values[high, :, cols]], 1)
    return k, v, diagonal(slots, first, 0, cols), diagonal(slots, first, 1, cols)


def retro_kernel(
    groups, rows, reads, queries, grads, encoded, key_weight, value_weight,
    attended, grad_q, grad_e,
    source, live, rank, order, keep, final, filled,
    query_in, grad_in, outgoing, slots, own, before, after, far, key_w, value_w,
    totals, keys, values, probs, grad_s, grad_p,
    peaks, stats, fetched, combined, back, landed, key_run, value_run, value_sums,
    outs_in, grad_qs_in, cross_grads, pair_sums, cross_w,
    load_sem, ring_send, ring_recv, send_sem, recv_sem, local_sem,
    stat_send, stat_recv, back_send, back_recv,
    sum_send, sum_recv, answer_send, answer_recv, grad_q_send, grad_q_recv, weight_send, weight_recv,
):
    me = group_index()
    z = lax.axis_index("mp")
    ring = lax.axis_size("mp")
    up, down = lax.rem(z + 1, ring), lax.rem(z + ring - 1, ring)
    across = lax.rem(z + 2, ring)
    cross = ring - 1 - z
    partner = z + 1 - 2 * lax.rem(z, 2)
    pair_slot = 2 - lax.rem(z, 2)
    phase, dp = lax.axis_index("phase"), lax.axis_index("dp")
    in_phase = lax.axis_size("dp")
    blocks = encoded.shape[0]
    half = blocks // 2
    key_acc, value_acc, weights = totals.at[0], totals.at[1], totals

    barrier = pltpu.get_barrier_semaphore()
    pl.semaphore_signal(barrier, inc=1, device_id={"mp": up}, device_id_type=MESH)
    pl.semaphore_signal(barrier, inc=1, device_id={"mp": down}, device_id_type=MESH)
    greet_group(barrier, groups)

    inputs = (
        pltpu.make_async_copy(queries, query_in, load_sem.at[9]),
        pltpu.make_async_copy(grads, grad_in, load_sem.at[10]),
    )
    for load in inputs:
        load.start()
    own_load = pltpu.make_async_copy(encoded, own, load_sem.at[0])
    own_load.start()
    weight_loads = []
    for i, owner in enumerate((z, down, up, across)):
        pair = (
            pltpu.make_async_copy(key_weight.at[owner], key_w.at[i], load_sem.at[1 + 2 * i]),
            pltpu.make_async_copy(value_weight.at[owner], value_w.at[i], load_sem.at[2 + 2 * i]),
        )
        for load in pair:
            load.start()
        weight_loads.append(pair)

    def ring_copy(lane, source, target, block, to):
        return pltpu.make_async_remote_copy(
            src_ref=source.at[block],
            dst_ref=target.at[block],
            send_sem=ring_send.at[lane],
            recv_sem=ring_recv.at[lane, block],
            device_id={"mp": to},
            device_id_type=MESH,
        )

    def go_up(c):
        return ring_copy(0, encoded, before, c, up)

    def go_down(c):
        return ring_copy(1, encoded, after, c, down)

    def pass_up(c):
        return ring_copy(2, before, far, c, up)

    def pass_down(c):
        return ring_copy(2, after, far, c, down)

    pl.semaphore_wait(barrier, groups - 1 + 2)

    cross_pair = cross + 1 - 2 * lax.rem(cross, 2)
    their_part = cross * (1 - phase) + cross_pair * phase
    piece_rows = pl.ds(pl.multiple_of(dp * CLEN, CLEN), CLEN)

    def piece_copy(j, weight):
        return pltpu.make_async_remote_copy(
            src_ref=weight.at[their_part, piece_rows],
            dst_ref=cross_w.at[me, j],
            send_sem=weight_send.at[0],
            recv_sem=weight_recv.at[0],
            device_id={"mp": cross},
            device_id_type=MESH,
        )

    def weight_copy(stage, block, to):
        return pltpu.make_async_remote_copy(
            src_ref=cross_w.at[block],
            dst_ref=cross_w.at[block],
            send_sem=weight_send.at[stage],
            recv_sem=weight_recv.at[stage],
            device_id=to,
            device_id_type=MESH,
        )

    side = round(in_phase**0.5)
    x, y = lax.rem(dp, side), dp // side

    def first_line(k):
        return lax.rem(y + k * phase, side) * side + lax.rem(x + k * (1 - phase), side)

    def second_line(k):
        return lax.rem(y + k * (1 - phase), side) * side + lax.rem(x + k * phase, side)

    def spread_first(k, carry):
        weight_copy(1, me, {"dp": first_line(k)}).start()
        return carry

    def spread_second(i, carry):
        piece = phase * in_phase + first_line(i // (side - 1))
        to = second_line(1 + lax.rem(i, side - 1))
        weight_copy(2, piece, {"dp": to}).start()
        return carry

    pieces = weight_copy(0, me, {"mp": cross})
    firsts = weight_copy(1, pl.ds(0, side - 1), {"dp": first_line(1)})
    seconds = weight_copy(2, pl.ds(0, side * (side - 1)), {"dp": second_line(1)})
    halves = weight_copy(3, pl.ds(phase * in_phase, in_phase), {"phase": 1 - phase})
    piece_copy(0, key_weight).start()
    piece_copy(1, value_weight).start()

    def send_own(c, carry):
        go_up(c).start()
        go_down(blocks - 1 - c).start()
        return carry

    lax.fori_loop(0, blocks, send_own, 0)
    spans = queries.shape[0]

    def fill(o, carry):
        span = jnp.int32(0)
        found = jnp.int32(0)
        for t in range(spans):
            for j in range(2):
                hit = (reads[j, t] == o).astype(jnp.int32)
                span = jnp.maximum(span, hit * t)
                found = jnp.maximum(found, hit)
        source[o] = span
        live[o] = found
        for j, array in enumerate((query_in, grad_in)):
            block = array[span]
            outgoing[o, j] = jnp.where(found > 0, block, jnp.zeros_like(block))
        return carry

    for load in inputs:
        load.wait()
    lax.fori_loop(0, groups, fill, 0)
    pieces.wait_recv()
    lax.fori_loop(1, side, spread_first, 0)
    slot_to, slots_arrive, slots_leave = send_to_group(
        groups, lambda g: outgoing.at[g], slots, send_sem, recv_sem
    )
    start_all(groups, slot_to)
    local = pltpu.make_async_copy(outgoing.at[me], slots.at[me], local_sem.at[0])
    local.start()

    def place(o, carry):
        mine = rows[0, o]
        count = jnp.int32(0)
        for other in range(groups):
            theirs = rows[0, other]
            count += (theirs < mine).astype(jnp.int32)
            count += ((theirs == mine) & (other < o)).astype(jnp.int32)
        rank[o] = count
        return carry

    def invert(i, carry):
        slot = jnp.int32(0)
        for o in range(groups):
            slot = jnp.maximum(slot, (rank[o] == i).astype(jnp.int32) * o)
        order[i] = slot
        return carry

    def follow(i, carry):
        same = rows[0, order[i]] == rows[0, order[jnp.maximum(i - 1, 0)]]
        keep[i] = (same & (i > 0)).astype(jnp.int32)
        return carry

    def close(n, carry):
        upto = jnp.int32(0)
        here = jnp.int32(0)
        for o in range(groups):
            upto += (rows[0, o] <= n).astype(jnp.int32)
            here += (rows[0, o] == n).astype(jnp.int32)
        final[n] = jnp.maximum(upto - 1, 0)
        filled[n] = jnp.minimum(here, 1)
        return carry

    lax.fori_loop(0, groups, place, 0)
    lax.fori_loop(0, groups, invert, 0)
    lax.fori_loop(0, groups, follow, 0)
    lax.fori_loop(0, blocks, close, 0)
    firsts.wait_recv()
    lax.fori_loop(0, side * (side - 1), spread_second, 0)

    def project(block, i):
        return (
            jnp.dot(block, key_w[i], preferred_element_type=F32),
            jnp.dot(block, value_w[i], preferred_element_type=F32),
        )

    def add(source, c, i):
        k, v = project(source[c], i)
        key_acc[c] += k
        value_acc[c] += v

    def finish(c):
        k, v = project(far[c], 3)
        keys[c] = (key_acc[c] + k).astype(BF16)
        values[c] = (value_acc[c] + v).astype(BF16)

    own_load.wait()
    for load in weight_loads[0]:
        load.wait()

    def first(c, carry):
        k, v = project(own[c], 0)
        key_acc[c] = k
        value_acc[c] = v
        return carry

    lax.fori_loop(0, blocks, first, 0)
    for pair in weight_loads[1:]:
        for load in pair:
            load.wait()

    def near(c, carry):
        d = blocks - 1 - c
        go_up(c).wait_recv()
        pass_up(c).start()
        go_down(d).wait_recv()
        pass_down(d).start()
        add(before, c, 1)
        add(after, d, 2)
        return carry

    lax.fori_loop(0, half, near, 0)

    def rest(c, carry):
        d = blocks - 1 - c
        go_up(c).wait_recv()
        add(before, c, 1)
        go_down(d).wait_recv()
        add(after, d, 2)
        return carry

    lax.fori_loop(half, blocks, rest, 0)


    def last(c, carry):
        d = blocks - 1 - c
        pass_up(c).wait_recv()
        finish(c)
        pass_down(d).wait_recv()
        finish(d)
        return carry

    lax.fori_loop(0, half, last, 0)

    slots_arrive()
    slots_leave()
    local.wait()
    seconds.wait_recv()
    halves.start()
    width = keys.shape[2]
    heads = width // HS

    def score(p):
        for h in range(heads):
            k, v, q, g = pair_operands(rows, p, keys, values, slots, 2 * p, h)
            scores = lax.dot_general(k, q, LAST, preferred_element_type=F32) * SCALE
            gp = lax.dot_general(v, g, LAST, preferred_element_type=F32)
            peak = jnp.max(scores, 0, keepdims=True)
            w = jnp.exp(scores - peak)
            total = jnp.sum(w, 0, keepdims=True)
            peaks[p, h : h + 1] = peak
            stats[p, h : h + 1] = peak + jnp.log(total)
            stats[p, heads + h : heads + h + 1] = jnp.sum(w * gp, 0, keepdims=True) / total
            weights[p // blocks, p % blocks, :, h * HS : (h + 1) * HS] = w
            grad_p[p, h] = gp

    stat_to, stats_arrive, stats_leave = send_to_group(
        groups, lambda g: stats.at[g // 2], fetched, stat_send, stat_recv
    )
    local_stat = pltpu.make_async_copy(stats.at[me // 2], fetched.at[me], local_sem.at[2])
    together = 4
    chunks = groups // 2 // together

    def score_some(j, carry):
        first = together * lax.rem(me // (2 * together) + j, chunks)
        for u in range(together):
            score(first + u)
        for u in range(2 * together):
            k = lax.rem(2 * first + u + groups - me, groups)

            @pl.when(k > 0)
            def _():
                stat_to(k).start()

            @pl.when(k == 0)
            def _():
                local_stat.start()

        return carry

    lax.fori_loop(0, chunks, score_some, 0)

    def all_sent(lane, source, sem):
        pltpu.make_async_remote_copy(
            src_ref=source,
            dst_ref=source,
            send_sem=sem.at[lane],
            recv_sem=ring_recv.at[0, 0],
            device_id={"mp": up},
            device_id_type=MESH,
        ).wait_send()

    for lane in range(3):
        all_sent(lane, far, ring_send)

    local_stat.wait()
    stats_arrive()

    def combine(t, carry):
        a = fetched[reads[0, t]]
        b = fetched[reads[1, t]]
        overall = jnp.maximum(a[:heads], b[:heads])
        fa, fb = jnp.exp(a[:heads] - overall), jnp.exp(b[:heads] - overall)
        total = fa + fb
        combined[t, :heads] = overall + jnp.log(total)
        combined[t, heads:] = (fa * a[heads:] + fb * b[heads:]) / total
        return carry

    lax.fori_loop(0, spans, combine, 0, unroll=8)
    back_to, backs_arrive, backs_leave = send_to_group(
        groups, lambda g: back.at[g], landed, back_send, back_recv
    )

    def answer(o):
        mine = combined[source[o]]
        back[o] = jnp.where(live[o] > 0, mine, jnp.zeros_like(mine))

    def answer_to(k, carry):
        answer(lax.rem(me + k, groups))
        back_to(k).start()
        return carry

    lax.fori_loop(1, groups, answer_to, 0)
    answer(me)
    local = pltpu.make_async_copy(back.at[me], landed.at[me], local_sem.at[3])
    local.start()
    local.wait()
    backs_arrive()
    left = lax.broadcasted_iota(jnp.int32, landed.shape[1:], 1) < CLEN

    def normalise(p, carry):
        both = jnp.where(left, landed[2 * p], landed[2 * p + 1])
        for h in range(heads):
            factor = jnp.exp(peaks[p, h : h + 1] - both[h : h + 1])
            pr = weights[p // blocks, p % blocks, :, h * HS : (h + 1) * HS] * factor
            probs[p, h] = pr.astype(BF16)
            grad_s[p, h] = (pr * (grad_p[p, h] - both[heads + h : heads + h + 1])).astype(BF16)
        return carry

    lax.fori_loop(0, groups // 2, normalise, 0, unroll=2)

    top = lax.broadcasted_iota(jnp.int32, (2 * CLEN, HS), 0) < CLEN

    def slot_view(buffer, g):
        start = pl.multiple_of(lax.rem(g // 2, 2) * CLEN, CLEN)
        column = pl.multiple_of(lax.rem(g, 2) * width, width)
        return buffer.at[g // 4, pl.ds(start, CLEN), pl.ds(column, width)]

    def answer_all(lefts, rights, scale, buffer):
        def one(p, carry):
            low, high = rows[0, 2 * p], rows[0, 2 * p + 1]
            start = pl.multiple_of(lax.rem(p, 2) * CLEN, CLEN)
            for h in range(heads):
                cols = pl.ds(h * HS, HS)
                right = jnp.concatenate([rights[low, :, cols], rights[high, :, cols]], 1)
                both = lax.dot_general(lefts[p, h], right, FIRST, preferred_element_type=F32)
                picked = (jnp.where(top, both[:, :HS], both[:, HS:]) * scale).astype(BF16)
                buffer[p // 2, pl.ds(start, CLEN), h * HS : (h + 1) * HS] = picked[:CLEN]
                buffer[p // 2, pl.ds(start, CLEN), width + h * HS : width + (h + 1) * HS] = picked[CLEN:]
            return carry

        lax.fori_loop(0, groups // 2, one, 0, unroll=4)

    answer_all(probs, values, 1.0, before)
    out_to, outs_arrive, outs_leave = send_to_group(
        groups, lambda g: slot_view(before, g), outs_in, answer_send, answer_recv
    )
    start_all(groups, out_to)
    local_out = pltpu.make_async_copy(slot_view(before, me), outs_in.at[me], local_sem.at[1])
    local_out.start()
    half_lane = lax.broadcasted_iota(jnp.int32, (NLEN, 2 * CLEN), 1) // CLEN
    key_run[...] = jnp.zeros_like(key_run)
    value_run[...] = jnp.zeros_like(value_run)

    def accumulate(i, carry):
        slot = order[i]
        pair = slot // 2
        mine = half_lane == lax.rem(slot, 2)
        more = keep[i].astype(F32)
        for h in range(heads):
            cols = pl.ds(h * HS, HS)
            zero = jnp.zeros((NLEN, 2 * CLEN), BF16)
            p = jnp.where(mine, probs[pair, h], zero)
            s = jnp.where(mine, grad_s[pair, h], zero)
            q, g = slots[slot, 0, :, cols], slots[slot, 1, :, cols]
            k = key_run[:, cols] * more + jnp.dot(
                s, jnp.concatenate([q, q], 0), preferred_element_type=F32
            )
            v = value_run[:, cols] * more + jnp.dot(
                p, jnp.concatenate([g, g], 0), preferred_element_type=F32
            )
            key_run[:, cols] = k
            value_run[:, cols] = v
            outgoing[i, :, :, cols] = (k * SCALE).astype(BF16).reshape(2, CLEN, HS)
            value_sums[i, :, :, cols] = v.astype(BF16).reshape(2, CLEN, HS)
        return carry

    lax.fori_loop(0, groups, accumulate, 0, unroll=8)
    def gather(n):
        for j, sums in enumerate((outgoing, value_sums)):
            block = sums[final[n]].reshape(NLEN, width)
            far[n, :, j * width : (j + 1) * width] = jnp.where(
                filled[n] > 0, block, jnp.zeros_like(block)
            )


    def own_part(c, i):
        return lax.dot_general(
            far[c, :, :width], key_w[i], LAST, preferred_element_type=F32
        ) + lax.dot_general(far[c, :, width:], value_w[i], LAST, preferred_element_type=F32)

    def cross_part(c, i):
        some = pl.ds(i * in_phase, in_phase)
        shape = (in_phase * CLEN, width)
        return lax.dot_general(
            cross_grads[c, :, :width], cross_w[some, 0].reshape(shape), LAST, preferred_element_type=F32
        ) + lax.dot_general(
            cross_grads[c, :, width:], cross_w[some, 1].reshape(shape), LAST, preferred_element_type=F32
        )

    def sum_copy(lane, source, target, block, to):
        return pltpu.make_async_remote_copy(
            src_ref=source.at[block],
            dst_ref=target.at[block],
            send_sem=sum_send.at[lane],
            recv_sem=sum_recv.at[lane, block],
            device_id={"mp": to},
            device_id_type=MESH,
        )

    to_pair = own

    def cross_copy(c):
        return sum_copy(0, far, cross_grads, c, cross)

    def pair_copy(c):
        return sum_copy(1, to_pair, pair_sums, c, partner)

    def send_cross(c, carry):
        gather(c)
        cross_copy(c).start()
        return carry

    lax.fori_loop(0, blocks, send_cross, 0)
    answer_all(grad_s, keys, SCALE, after)
    grad_q_to, grad_qs_arrive, grad_qs_leave = send_to_group(
        groups, lambda g: slot_view(after, g), grad_qs_in, grad_q_send, grad_q_recv
    )
    start_all(groups, grad_q_to)
    local_grad_q = pltpu.make_async_copy(slot_view(after, me), grad_qs_in.at[me], load_sem.at[0])
    local_grad_q.start()
    halves.wait_recv()

    def send_pair(c, carry):
        mine = own_part(c, pair_slot)
        cross_copy(c).wait_recv()
        to_pair[c] = (mine + cross_part(c, 1)).astype(BF16)
        pair_copy(c).start()
        mine = own_part(c, 0) + cross_part(c, 0)
        key_acc[c] = mine[:, :width]
        value_acc[c] = mine[:, width:]
        return carry

    lax.fori_loop(0, blocks, send_pair, 0)

    def add_pair(c, carry):
        pair_copy(c).wait_recv()
        other = pair_sums[c].astype(F32)
        grad_e[c, :, :width] = (key_acc[c] + other[:, :width]).astype(BF16)
        grad_e[c, :, width:] = (value_acc[c] + other[:, width:]).astype(BF16)
        return carry

    lax.fori_loop(0, blocks, add_pair, 0)
    local_out.wait()
    local_grad_q.wait()
    outs_arrive()
    grad_qs_arrive()
    outs_leave()
    grad_qs_leave()
    stats_leave()
    backs_leave()

    def finish_span(t, carry):
        a, b = reads[0, t], reads[1, t]
        for target, parts in ((attended, outs_in), (grad_q, grad_qs_in)):
            target[t] = (parts[a].astype(F32) + parts[b].astype(F32)).astype(BF16)
        return carry

    lax.fori_loop(0, spans, finish_span, 0)
    for lane in range(2):
        all_sent(lane, far, sum_send)
    for copy in (pieces, firsts, seconds, halves):
        copy.wait_send()


def params(collective_id=None, mib=56):
    return pltpu.CompilerParams(
        collective_id=collective_id,
        has_side_effects=collective_id is not None,
        vmem_limit_bytes=mib << 20,
    )


def body(queries, grad_out, encoded, key_weight, value_weight, send_rows, read_slots):
    groups = lax.axis_size(("phase", "dp"))
    ring = lax.axis_size("mp")
    in_phase = lax.axis_size("dp")
    blocks, _, features = encoded.shape
    width = key_weight.shape[1]
    heads = width // HS
    spans = read_slots.shape[0]
    hbm = pl.BlockSpec(memory_space=pl.ANY)
    vmem = pl.BlockSpec(memory_space=pltpu.VMEM)
    smem = pl.BlockSpec(memory_space=pltpu.SMEM)
    dma = pltpu.SemaphoreType.DMA
    half_pairs = groups // 2

    rows = send_rows.reshape(1, groups)
    reads = read_slots.T
    query_spans = queries.reshape(spans, CLEN, width)
    grad_spans = grad_out.reshape(spans, CLEN, width)
    key_parts = key_weight.reshape(ring, features, width)
    value_parts = value_weight.reshape(ring, features, width)
    block_shape = jax.ShapeDtypeStruct((blocks, NLEN, width), BF16)
    slot_shape = jax.ShapeDtypeStruct((groups, 2, CLEN, width), BF16)
    prob_shape = jax.ShapeDtypeStruct((half_pairs, heads, NLEN, 2 * CLEN), BF16)

    stat_shape = (groups, 2 * heads, 2 * CLEN)
    factor_shape = (groups, 2 * heads, 2 * CLEN)
    span_shape = jax.ShapeDtypeStruct((spans, CLEN, width), BF16)
    attended, grad_q, grad_e = pl.pallas_call(
        functools.partial(retro_kernel, groups),
        out_shape=(
            pltpu.VMEM(span_shape.shape, BF16),
            pltpu.VMEM(span_shape.shape, BF16),
            pltpu.VMEM(encoded.shape, BF16),
        ),
        in_specs=[smem, smem, hbm, hbm, hbm, hbm, hbm],
        out_specs=(vmem, vmem, vmem),
        scratch_shapes=[
            pltpu.SMEM((groups,), jnp.int32),
            pltpu.SMEM((groups,), jnp.int32),
            pltpu.SMEM((groups,), jnp.int32),
            pltpu.SMEM((groups,), jnp.int32),
            pltpu.SMEM((groups,), jnp.int32),
            pltpu.SMEM((blocks,), jnp.int32),
            pltpu.SMEM((blocks,), jnp.int32),
            pltpu.VMEM(span_shape.shape, BF16),
            pltpu.VMEM(span_shape.shape, BF16),
            pltpu.VMEM(slot_shape.shape, BF16),
            pltpu.VMEM(slot_shape.shape, BF16),
            pltpu.VMEM(encoded.shape, BF16),
            pltpu.VMEM(encoded.shape, BF16),
            pltpu.VMEM(encoded.shape, BF16),
            pltpu.VMEM(encoded.shape, BF16),
            pltpu.VMEM(key_parts.shape, BF16),
            pltpu.VMEM(key_parts.shape, BF16),
            pltpu.VMEM((2,) + block_shape.shape, F32),
            pltpu.VMEM(block_shape.shape, BF16),
            pltpu.VMEM(block_shape.shape, BF16),
            pltpu.VMEM(prob_shape.shape, BF16),
            pltpu.VMEM(prob_shape.shape, BF16),
            pltpu.VMEM(prob_shape.shape, F32),
            pltpu.VMEM((half_pairs,) + stat_shape[1:], F32),
            pltpu.VMEM((half_pairs,) + stat_shape[1:], F32),
            pltpu.VMEM(stat_shape, F32),
            pltpu.VMEM((spans,) + factor_shape[1:], F32),
            pltpu.VMEM(factor_shape, F32),
            pltpu.VMEM(factor_shape, F32),
            pltpu.VMEM((NLEN, width), F32),
            pltpu.VMEM((NLEN, width), F32),
            pltpu.VMEM(slot_shape.shape, BF16),
            pltpu.VMEM((groups, CLEN, width), BF16),
            pltpu.VMEM((groups, CLEN, width), BF16),
            pltpu.VMEM(encoded.shape, BF16),
            pltpu.VMEM(encoded.shape, BF16),
            pltpu.VMEM((2 * in_phase, 2, CLEN, width), BF16),
            dma((11,)),
            dma((3,)),
            dma((3, blocks)),
            dma,
            dma,
            dma((4,)),
            dma,
            dma,
            dma,
            dma,
            dma((2,)),
            dma((2, blocks)),
            dma,
            dma,
            dma,
            dma,
            dma((4,)),
            dma((4,)),
        ],
        compiler_params=params(0, 60),
        name="retro",
    )(rows, reads, query_spans, grad_spans, encoded, key_parts, value_parts)
    return (attended.reshape(queries.shape), grad_q.reshape(queries.shape), grad_e)


def solution(mesh):
    return jax.shard_map(
        body,
        mesh=mesh,
        in_specs=(
            P(("phase", "dp"), "mp"),
            P(("phase", "dp"), "mp"),
            P(("phase", "dp"), None, "mp"),
            P(None, "mp"),
            P(None, "mp"),
            P(("phase", "dp"), None, None),
            P(("phase", "dp"), None),
        ),
        out_specs=(
            P(("phase", "dp"), "mp"),
            P(("phase", "dp"), "mp"),
            P(("phase", "dp"), None, "mp"),
        ),
        check_vma=False,
    )
```

```python
import functools

import jax
import jax.numpy as jnp
from jax import lax
from jax.experimental import pallas as pl
from jax.experimental.pallas import tpu as pltpu
from jax.sharding import PartitionSpec as P

HS = 128
CLEN = 64
NLEN = 128
SCALE = HS ** (-0.5)
LAST = (((1,), (1,)), ((), ()))
FIRST = (((0,), (0,)), ((), ()))
MESH = pl.DeviceIdType.MESH
F32 = jnp.float32
BF16 = jnp.bfloat16


def group_index():
    return lax.axis_index("phase") * lax.axis_size("dp") + lax.axis_index("dp")


def peer_id(group):
    dp = lax.axis_size("dp")
    return {"phase": group // dp, "dp": lax.rem(group, dp)}


def greet_group(barrier, groups):
    me = group_index()

    def greet(k, carry):
        pl.semaphore_signal(
            barrier, inc=1, device_id=peer_id(lax.rem(me + k, groups)), device_id_type=MESH
        )
        return carry

    lax.fori_loop(1, groups, greet, 0)


def send_to_group(groups, source, target, send_sem, recv_sem):
    me = group_index()

    def copy_to(k):
        peer = lax.rem(me + k, groups)
        return pltpu.make_async_remote_copy(
            src_ref=source(peer),
            dst_ref=target.at[me],
            send_sem=send_sem,
            recv_sem=recv_sem,
            device_id=peer_id(peer),
            device_id_type=MESH,
        )

    def everything():
        others = target.at[pl.ds(0, groups - 1)]
        return pltpu.make_async_remote_copy(
            src_ref=others,
            dst_ref=others,
            send_sem=send_sem,
            recv_sem=recv_sem,
            device_id=peer_id(lax.rem(me + 1, groups)),
            device_id_type=MESH,
        )

    def arrive():
        everything().wait_recv()

    def leave():
        everything().wait_send()

    return copy_to, arrive, leave


def start_all(groups, copy_to):
    lax.fori_loop(1, groups, lambda k, c: (copy_to(k).start(), c)[1], 0)


def diagonal(slots, first, which, cols):
    top = lax.broadcasted_iota(jnp.int32, (2 * CLEN, HS), 0) < CLEN
    block = slots[pl.ds(first, 2), which, :, cols].reshape(2 * CLEN, HS)
    zero = jnp.zeros_like(block)
    return jnp.concatenate([jnp.where(top, block, zero), jnp.where(top, zero, block)], 1)


def pair_operands(rows, pair, keys, values, slots, first, h):
    cols = pl.ds(h * HS, HS)
    low, high = rows[0, 2 * pair], rows[0, 2 * pair + 1]
    k = jnp.concatenate([keys[low, :, cols], keys[high, :, cols]], 1)
    v = jnp.concatenate([values[low, :, cols], values[high, :, cols]], 1)
    return k, v, diagonal(slots, first, 0, cols), diagonal(slots, first, 1, cols)


def retro_kernel(
    groups, rows, reads, queries, grads, encoded, key_weight, value_weight,
    attended, grad_q, grad_e,
    source, live, rank, order, keep, final, filled,
    query_in, grad_in, outgoing, slots, own, before, after, far, key_w, value_w,
    totals, keys, values, probs, grad_s, grad_p,
    peaks, stats, fetched, combined, back, landed, key_run, value_run, value_sums,
    outs_in, grad_qs_in, cross_grads, pair_sums, cross_w,
    load_sem, ring_send, ring_recv, send_sem, recv_sem, local_sem,
    stat_send, stat_recv, back_send, back_recv,
    sum_send, sum_recv, answer_send, answer_recv, grad_q_send, grad_q_recv, weight_send, weight_recv,
):
    me = group_index()
    z = lax.axis_index("mp")
    ring = lax.axis_size("mp")
    up, down = lax.rem(z + 1, ring), lax.rem(z + ring - 1, ring)
    across = lax.rem(z + 2, ring)
    cross = ring - 1 - z
    partner = z + 1 - 2 * lax.rem(z, 2)
    pair_slot = 2 - lax.rem(z, 2)
    phase, dp = lax.axis_index("phase"), lax.axis_index("dp")
    in_phase = lax.axis_size("dp")
    blocks = encoded.shape[0]
    half = blocks // 2
    key_acc, value_acc, weights = totals.at[0], totals.at[1], totals

    barrier = pltpu.get_barrier_semaphore()
    pl.semaphore_signal(barrier, inc=1, device_id={"mp": up}, device_id_type=MESH)
    pl.semaphore_signal(barrier, inc=1, device_id={"mp": down}, device_id_type=MESH)
    greet_group(barrier, groups)

    inputs = (
        pltpu.make_async_copy(queries, query_in, load_sem.at[9]),
        pltpu.make_async_copy(grads, grad_in, load_sem.at[10]),
    )
    for load in inputs:
        load.start()
    own_load = pltpu.make_async_copy(encoded, own, load_sem.at[0])
    own_load.start()
    weight_loads = []
    for i, owner in enumerate((z, down, up, across)):
        pair = (
            pltpu.make_async_copy(key_weight.at[owner], key_w.at[i], load_sem.at[1 + 2 * i]),
            pltpu.make_async_copy(value_weight.at[owner], value_w.at[i], load_sem.at[2 + 2 * i]),
        )
        for load in pair:
            load.start()
        weight_loads.append(pair)

    def ring_copy(lane, source, target, block, to):
        return pltpu.make_async_remote_copy(
            src_ref=source.at[block],
            dst_ref=target.at[block],
            send_sem=ring_send.at[lane],
            recv_sem=ring_recv.at[lane, block],
            device_id={"mp": to},
            device_id_type=MESH,
        )

    def go_up(c):
        return ring_copy(0, encoded, before, c, up)

    def go_down(c):
        return ring_copy(1, encoded, after, c, down)

    def pass_up(c):
        return ring_copy(2, before, far, c, up)

    def pass_down(c):
        return ring_copy(2, after, far, c, down)

    pl.semaphore_wait(barrier, groups - 1 + 2)

    cross_pair = cross + 1 - 2 * lax.rem(cross, 2)
    their_part = cross * (1 - phase) + cross_pair * phase
    piece_rows = pl.ds(pl.multiple_of(dp * CLEN, CLEN), CLEN)

    def piece_copy(j, weight):
        return pltpu.make_async_remote_copy(
            src_ref=weight.at[their_part, piece_rows],
            dst_ref=cross_w.at[me, j],
            send_sem=weight_send.at[0],
            recv_sem=weight_recv.at[0],
            device_id={"mp": cross},
            device_id_type=MESH,
        )

    def weight_copy(stage, block, to):
        return pltpu.make_async_remote_copy(
            src_ref=cross_w.at[block],
            dst_ref=cross_w.at[block],
            send_sem=weight_send.at[stage],
            recv_sem=weight_recv.at[stage],
            device_id=to,
            device_id_type=MESH,
        )

    side = round(in_phase**0.5)
    x, y = lax.rem(dp, side), dp // side

    def first_line(k):
        return lax.rem(y + k * phase, side) * side + lax.rem(x + k * (1 - phase), side)

    def second_line(k):
        return lax.rem(y + k * (1 - phase), side) * side + lax.rem(x + k * phase, side)

    def spread_first(k, carry):
        weight_copy(1, me, {"dp": first_line(k)}).start()
        return carry

    def spread_second(i, carry):
        piece = phase * in_phase + first_line(i // (side - 1))
        to = second_line(1 + lax.rem(i, side - 1))
        weight_copy(2, piece, {"dp": to}).start()
        return carry

    pieces = weight_copy(0, me, {"mp": cross})
    firsts = weight_copy(1, pl.ds(0, side - 1), {"dp": first_line(1)})
    seconds = weight_copy(2, pl.ds(0, side * (side - 1)), {"dp": second_line(1)})
    halves = weight_copy(3, pl.ds(phase * in_phase, in_phase), {"phase": 1 - phase})
    piece_copy(0, key_weight).start()
    piece_copy(1, value_weight).start()

    def send_own(c, carry):
        go_up(c).start()
        go_down(blocks - 1 - c).start()
        return carry

    lax.fori_loop(0, blocks, send_own, 0)
    spans = queries.shape[0]

    def fill(o, carry):
        span = jnp.int32(0)
        found = jnp.int32(0)
        for t in range(spans):
            for j in range(2):
                hit = (reads[j, t] == o).astype(jnp.int32)
                span = jnp.maximum(span, hit * t)
                found = jnp.maximum(found, hit)
        source[o] = span
        live[o] = found
        for j, array in enumerate((query_in, grad_in)):
            block = array[span]
            outgoing[o, j] = jnp.where(found > 0, block, jnp.zeros_like(block))
        return carry

    for load in inputs:
        load.wait()
    lax.fori_loop(0, groups, fill, 0)
    pieces.wait_recv()
    lax.fori_loop(1, side, spread_first, 0)
    slot_to, slots_arrive, slots_leave = send_to_group(
        groups, lambda g: outgoing.at[g], slots, send_sem, recv_sem
    )
    start_all(groups, slot_to)
    local = pltpu.make_async_copy(outgoing.at[me], slots.at[me], local_sem.at[0])
    local.start()

    def place(o, carry):
        mine = rows[0, o]
        count = jnp.int32(0)
        for other in range(groups):
            theirs = rows[0, other]
            count += (theirs < mine).astype(jnp.int32)
            count += ((theirs == mine) & (other < o)).astype(jnp.int32)
        rank[o] = count
        return carry

    def invert(i, carry):
        slot = jnp.int32(0)
        for o in range(groups):
            slot = jnp.maximum(slot, (rank[o] == i).astype(jnp.int32) * o)
        order[i] = slot
        return carry

    def follow(i, carry):
        same = rows[0, order[i]] == rows[0, order[jnp.maximum(i - 1, 0)]]
        keep[i] = (same & (i > 0)).astype(jnp.int32)
        return carry

    def close(n, carry):
        upto = jnp.int32(0)
        here = jnp.int32(0)
        for o in range(groups):
            upto += (rows[0, o] <= n).astype(jnp.int32)
            here += (rows[0, o] == n).astype(jnp.int32)
        final[n] = jnp.maximum(upto - 1, 0)
        filled[n] = jnp.minimum(here, 1)
        return carry

    lax.fori_loop(0, groups, place, 0)
    lax.fori_loop(0, groups, invert, 0)
    lax.fori_loop(0, groups, follow, 0)
    lax.fori_loop(0, blocks, close, 0)
    firsts.wait_recv()
    lax.fori_loop(0, side * (side - 1), spread_second, 0)

    def project(block, i):
        return (
            jnp.dot(block, key_w[i], preferred_element_type=F32),
            jnp.dot(block, value_w[i], preferred_element_type=F32),
        )

    def add(source, c, i):
        k, v = project(source[c], i)
        key_acc[c] += k
        value_acc[c] += v

    def finish(c):
        k, v = project(far[c], 3)
        keys[c] = (key_acc[c] + k).astype(BF16)
        values[c] = (value_acc[c] + v).astype(BF16)

    own_load.wait()
    for load in weight_loads[0]:
        load.wait()

    def first(c, carry):
        k, v = project(own[c], 0)
        key_acc[c] = k
        value_acc[c] = v
        return carry

    lax.fori_loop(0, blocks, first, 0)
    for pair in weight_loads[1:]:
        for load in pair:
            load.wait()

    def near(c, carry):
        d = blocks - 1 - c
        go_up(c).wait_recv()
        pass_up(c).start()
        go_down(d).wait_recv()
        pass_down(d).start()
        add(before, c, 1)
        add(after, d, 2)
        return carry

    lax.fori_loop(0, half, near, 0)

    def rest(c, carry):
        d = blocks - 1 - c
        go_up(c).wait_recv()
        add(before, c, 1)
        go_down(d).wait_recv()
        add(after, d, 2)
        return carry

    lax.fori_loop(half, blocks, rest, 0)


    def last(c, carry):
        d = blocks - 1 - c
        pass_up(c).wait_recv()
        finish(c)
        pass_down(d).wait_recv()
        finish(d)
        return carry

    lax.fori_loop(0, half, last, 0)

    slots_arrive()
    slots_leave()
    local.wait()
    seconds.wait_recv()
    halves.start()
    width = keys.shape[2]
    heads = width // HS

    def score(p):
        for h in range(heads):
            k, v, q, g = pair_operands(rows, p, keys, values, slots, 2 * p, h)
            scores = lax.dot_general(k, q, LAST, preferred_element_type=F32) * SCALE
            gp = lax.dot_general(v, g, LAST, preferred_element_type=F32)
            peak = jnp.max(scores, 0, keepdims=True)
            w = jnp.exp(scores - peak)
            total = jnp.sum(w, 0, keepdims=True)
            peaks[p, h : h + 1] = peak
            stats[p, h : h + 1] = peak + jnp.log(total)
            stats[p, heads + h : heads + h + 1] = jnp.sum(w * gp, 0, keepdims=True) / total
            weights[p // blocks, p % blocks, :, h * HS : (h + 1) * HS] = w
            grad_p[p, h] = gp

    stat_to, stats_arrive, stats_leave = send_to_group(
        groups, lambda g: stats.at[g // 2], fetched, stat_send, stat_recv
    )
    local_stat = pltpu.make_async_copy(stats.at[me // 2], fetched.at[me], local_sem.at[2])
    together = 4
    chunks = groups // 2 // together

    def score_some(j, carry):
        first = together * lax.rem(me // (2 * together) + j, chunks)
        for u in range(together):
            score(first + u)
        for u in range(2 * together):
            k = lax.rem(2 * first + u + groups - me, groups)

            @pl.when(k > 0)
            def _():
                stat_to(k).start()

            @pl.when(k == 0)
            def _():
                local_stat.start()

        return carry

    lax.fori_loop(0, chunks, score_some, 0)

    def all_sent(lane, source, sem):
        pltpu.make_async_remote_copy(
            src_ref=source,
            dst_ref=source,
            send_sem=sem.at[lane],
            recv_sem=ring_recv.at[0, 0],
            device_id={"mp": up},
            device_id_type=MESH,
        ).wait_send()

    for lane in range(3):
        all_sent(lane, far, ring_send)

    local_stat.wait()
    stats_arrive()

    def combine(t, carry):
        a = fetched[reads[0, t]]
        b = fetched[reads[1, t]]
        overall = jnp.maximum(a[:heads], b[:heads])
        fa, fb = jnp.exp(a[:heads] - overall), jnp.exp(b[:heads] - overall)
        total = fa + fb
        combined[t, :heads] = overall + jnp.log(total)
        combined[t, heads:] = (fa * a[heads:] + fb * b[heads:]) / total
        return carry

    lax.fori_loop(0, spans, combine, 0, unroll=8)
    back_to, backs_arrive, backs_leave = send_to_group(
        groups, lambda g: back.at[g], landed, back_send, back_recv
    )

    def answer(o):
        mine = combined[source[o]]
        back[o] = jnp.where(live[o] > 0, mine, jnp.zeros_like(mine))

    def answer_to(k, carry):
        answer(lax.rem(me + k, groups))
        back_to(k).start()
        return carry

    lax.fori_loop(1, groups, answer_to, 0)
    answer(me)
    local = pltpu.make_async_copy(back.at[me], landed.at[me], local_sem.at[3])
    local.start()
    local.wait()
    backs_arrive()
    left = lax.broadcasted_iota(jnp.int32, landed.shape[1:], 1) < CLEN

    def normalise(p, carry):
        both = jnp.where(left, landed[2 * p], landed[2 * p + 1])
        for h in range(heads):
            factor = jnp.exp(peaks[p, h : h + 1] - both[h : h + 1])
            pr = weights[p // blocks, p % blocks, :, h * HS : (h + 1) * HS] * factor
            probs[p, h] = pr.astype(BF16)
            grad_s[p, h] = (pr * (grad_p[p, h] - both[heads + h : heads + h + 1])).astype(BF16)
        return carry

    lax.fori_loop(0, groups // 2, normalise, 0, unroll=2)

    top = lax.broadcasted_iota(jnp.int32, (2 * CLEN, HS), 0) < CLEN

    def slot_view(buffer, g):
        start = pl.multiple_of(lax.rem(g // 2, 2) * CLEN, CLEN)
        column = pl.multiple_of(lax.rem(g, 2) * width, width)
        return buffer.at[g // 4, pl.ds(start, CLEN), pl.ds(column, width)]

    def answer_all(lefts, rights, scale, buffer):
        def one(p, carry):
            low, high = rows[0, 2 * p], rows[0, 2 * p + 1]
            start = pl.multiple_of(lax.rem(p, 2) * CLEN, CLEN)
            for h in range(heads):
                cols = pl.ds(h * HS, HS)
                right = jnp.concatenate([rights[low, :, cols], rights[high, :, cols]], 1)
                both = lax.dot_general(lefts[p, h], right, FIRST, preferred_element_type=F32)
                picked = (jnp.where(top, both[:, :HS], both[:, HS:]) * scale).astype(BF16)
                buffer[p // 2, pl.ds(start, CLEN), h * HS : (h + 1) * HS] = picked[:CLEN]
                buffer[p // 2, pl.ds(start, CLEN), width + h * HS : width + (h + 1) * HS] = picked[CLEN:]
            return carry

        lax.fori_loop(0, groups // 2, one, 0, unroll=4)

    half_lane = lax.broadcasted_iota(jnp.int32, (NLEN, 2 * CLEN), 1) // CLEN
    key_run[...] = jnp.zeros_like(key_run)
    value_run[...] = jnp.zeros_like(value_run)

    def accumulate(i, carry):
        slot = order[i]
        pair = slot // 2
        mine = half_lane == lax.rem(slot, 2)
        more = keep[i].astype(F32)
        for h in range(heads):
            cols = pl.ds(h * HS, HS)
            zero = jnp.zeros((NLEN, 2 * CLEN), BF16)
            p = jnp.where(mine, probs[pair, h], zero)
            s = jnp.where(mine, grad_s[pair, h], zero)
            q, g = slots[slot, 0, :, cols], slots[slot, 1, :, cols]
            k = key_run[:, cols] * more + jnp.dot(
                s, jnp.concatenate([q, q], 0), preferred_element_type=F32
            )
            v = value_run[:, cols] * more + jnp.dot(
                p, jnp.concatenate([g, g], 0), preferred_element_type=F32
            )
            key_run[:, cols] = k
            value_run[:, cols] = v
            outgoing[i, :, :, cols] = (k * SCALE).astype(BF16).reshape(2, CLEN, HS)
            value_sums[i, :, :, cols] = v.astype(BF16).reshape(2, CLEN, HS)
        return carry

    lax.fori_loop(0, groups, accumulate, 0, unroll=8)
    def gather(n):
        for j, sums in enumerate((outgoing, value_sums)):
            block = sums[final[n]].reshape(NLEN, width)
            far[n, :, j * width : (j + 1) * width] = jnp.where(
                filled[n] > 0, block, jnp.zeros_like(block)
            )


    def own_part(c, i):
        return lax.dot_general(
            far[c, :, :width], key_w[i], LAST, preferred_element_type=F32
        ) + lax.dot_general(far[c, :, width:], value_w[i], LAST, preferred_element_type=F32)

    def cross_part(c, i):
        some = pl.ds(i * in_phase, in_phase)
        shape = (in_phase * CLEN, width)
        return lax.dot_general(
            cross_grads[c, :, :width], cross_w[some, 0].reshape(shape), LAST, preferred_element_type=F32
        ) + lax.dot_general(
            cross_grads[c, :, width:], cross_w[some, 1].reshape(shape), LAST, preferred_element_type=F32
        )

    def sum_copy(lane, source, target, block, to):
        return pltpu.make_async_remote_copy(
            src_ref=source.at[block],
            dst_ref=target.at[block],
            send_sem=sum_send.at[lane],
            recv_sem=sum_recv.at[lane, block],
            device_id={"mp": to},
            device_id_type=MESH,
        )

    to_pair = own

    def cross_copy(c):
        return sum_copy(0, far, cross_grads, c, cross)

    def pair_copy(c):
        return sum_copy(1, to_pair, pair_sums, c, partner)

    def send_cross(c, carry):
        gather(c)
        cross_copy(c).start()
        return carry

    lax.fori_loop(0, blocks, send_cross, 0)
    answer_all(probs, values, 1.0, before)
    out_to, outs_arrive, outs_leave = send_to_group(
        groups, lambda g: slot_view(before, g), outs_in, answer_send, answer_recv
    )
    start_all(groups, out_to)
    local_out = pltpu.make_async_copy(slot_view(before, me), outs_in.at[me], local_sem.at[1])
    local_out.start()
    halves.wait_recv()

    def send_pair(c, carry):
        mine = own_part(c, pair_slot)
        cross_copy(c).wait_recv()
        to_pair[c] = (mine + cross_part(c, 1)).astype(BF16)
        pair_copy(c).start()
        mine = own_part(c, 0) + cross_part(c, 0)
        key_acc[c] = mine[:, :width]
        value_acc[c] = mine[:, width:]
        return carry

    lax.fori_loop(0, 2, send_pair, 0)
    answer_all(grad_s, keys, SCALE, after)
    grad_q_to, grad_qs_arrive, grad_qs_leave = send_to_group(
        groups, lambda g: slot_view(after, g), grad_qs_in, grad_q_send, grad_q_recv
    )
    start_all(groups, grad_q_to)
    local_grad_q = pltpu.make_async_copy(slot_view(after, me), grad_qs_in.at[me], load_sem.at[0])
    local_grad_q.start()
    lax.fori_loop(2, blocks, send_pair, 0)

    def add_pair(c, carry):
        pair_copy(c).wait_recv()
        other = pair_sums[c].astype(F32)
        grad_e[c, :, :width] = (key_acc[c] + other[:, :width]).astype(BF16)
        grad_e[c, :, width:] = (value_acc[c] + other[:, width:]).astype(BF16)
        return carry

    lax.fori_loop(0, blocks, add_pair, 0)
    local_out.wait()
    local_grad_q.wait()
    outs_arrive()
    grad_qs_arrive()
    outs_leave()
    grad_qs_leave()
    stats_leave()
    backs_leave()

    def finish_span(t, carry):
        a, b = reads[0, t], reads[1, t]
        for target, parts in ((attended, outs_in), (grad_q, grad_qs_in)):
            target[t] = (parts[a].astype(F32) + parts[b].astype(F32)).astype(BF16)
        return carry

    lax.fori_loop(0, spans, finish_span, 0)
    for lane in range(2):
        all_sent(lane, far, sum_send)
    for copy in (pieces, firsts, seconds, halves):
        copy.wait_send()


def params(collective_id=None, mib=56):
    return pltpu.CompilerParams(
        collective_id=collective_id,
        has_side_effects=collective_id is not None,
        vmem_limit_bytes=mib << 20,
    )


def body(queries, grad_out, encoded, key_weight, value_weight, send_rows, read_slots):
    groups = lax.axis_size(("phase", "dp"))
    ring = lax.axis_size("mp")
    in_phase = lax.axis_size("dp")
    blocks, _, features = encoded.shape
    width = key_weight.shape[1]
    heads = width // HS
    spans = read_slots.shape[0]
    hbm = pl.BlockSpec(memory_space=pl.ANY)
    vmem = pl.BlockSpec(memory_space=pltpu.VMEM)
    smem = pl.BlockSpec(memory_space=pltpu.SMEM)
    dma = pltpu.SemaphoreType.DMA
    half_pairs = groups // 2

    rows = send_rows.reshape(1, groups)
    reads = read_slots.T
    query_spans = queries.reshape(spans, CLEN, width)
    grad_spans = grad_out.reshape(spans, CLEN, width)
    key_parts = key_weight.reshape(ring, features, width)
    value_parts = value_weight.reshape(ring, features, width)
    block_shape = jax.ShapeDtypeStruct((blocks, NLEN, width), BF16)
    slot_shape = jax.ShapeDtypeStruct((groups, 2, CLEN, width), BF16)
    prob_shape = jax.ShapeDtypeStruct((half_pairs, heads, NLEN, 2 * CLEN), BF16)

    stat_shape = (groups, 2 * heads, 2 * CLEN)
    factor_shape = (groups, 2 * heads, 2 * CLEN)
    span_shape = jax.ShapeDtypeStruct((spans, CLEN, width), BF16)
    attended, grad_q, grad_e = pl.pallas_call(
        functools.partial(retro_kernel, groups),
        out_shape=(
            pltpu.VMEM(span_shape.shape, BF16),
            pltpu.VMEM(span_shape.shape, BF16),
            pltpu.VMEM(encoded.shape, BF16),
        ),
        in_specs=[smem, smem, hbm, hbm, hbm, hbm, hbm],
        out_specs=(vmem, vmem, vmem),
        scratch_shapes=[
            pltpu.SMEM((groups,), jnp.int32),
            pltpu.SMEM((groups,), jnp.int32),
            pltpu.SMEM((groups,), jnp.int32),
            pltpu.SMEM((groups,), jnp.int32),
            pltpu.SMEM((groups,), jnp.int32),
            pltpu.SMEM((blocks,), jnp.int32),
            pltpu.SMEM((blocks,), jnp.int32),
            pltpu.VMEM(span_shape.shape, BF16),
            pltpu.VMEM(span_shape.shape, BF16),
            pltpu.VMEM(slot_shape.shape, BF16),
            pltpu.VMEM(slot_shape.shape, BF16),
            pltpu.VMEM(encoded.shape, BF16),
            pltpu.VMEM(encoded.shape, BF16),
            pltpu.VMEM(encoded.shape, BF16),
            pltpu.VMEM(encoded.shape, BF16),
            pltpu.VMEM(key_parts.shape, BF16),
            pltpu.VMEM(key_parts.shape, BF16),
            pltpu.VMEM((2,) + block_shape.shape, F32),
            pltpu.VMEM(block_shape.shape, BF16),
            pltpu.VMEM(block_shape.shape, BF16),
            pltpu.VMEM(prob_shape.shape, BF16),
            pltpu.VMEM(prob_shape.shape, BF16),
            pltpu.VMEM(prob_shape.shape, F32),
            pltpu.VMEM((half_pairs,) + stat_shape[1:], F32),
            pltpu.VMEM((half_pairs,) + stat_shape[1:], F32),
            pltpu.VMEM(stat_shape, F32),
            pltpu.VMEM((spans,) + factor_shape[1:], F32),
            pltpu.VMEM(factor_shape, F32),
            pltpu.VMEM(factor_shape, F32),
            pltpu.VMEM((NLEN, width), F32),
            pltpu.VMEM((NLEN, width), F32),
            pltpu.VMEM(slot_shape.shape, BF16),
            pltpu.VMEM((groups, CLEN, width), BF16),
            pltpu.VMEM((groups, CLEN, width), BF16),
            pltpu.VMEM(encoded.shape, BF16),
            pltpu.VMEM(encoded.shape, BF16),
            pltpu.VMEM((2 * in_phase, 2, CLEN, width), BF16),
            dma((11,)),
            dma((3,)),
            dma((3, blocks)),
            dma,
            dma,
            dma((4,)),
            dma,
            dma,
            dma,
            dma,
            dma((2,)),
            dma((2, blocks)),
            dma,
            dma,
            dma,
            dma,
            dma((4,)),
            dma((4,)),
        ],
        compiler_params=params(0, 60),
        name="retro",
    )(rows, reads, query_spans, grad_spans, encoded, key_parts, value_parts)
    return (attended.reshape(queries.shape), grad_q.reshape(queries.shape), grad_e)


def solution(mesh):
    return jax.shard_map(
        body,
        mesh=mesh,
        in_specs=(
            P(("phase", "dp"), "mp"),
            P(("phase", "dp"), "mp"),
            P(("phase", "dp"), None, "mp"),
            P(None, "mp"),
            P(None, "mp"),
            P(("phase", "dp"), None, None),
            P(("phase", "dp"), None),
        ),
        out_specs=(
            P(("phase", "dp"), "mp"),
            P(("phase", "dp"), "mp"),
            P(("phase", "dp"), None, "mp"),
        ),
        check_vma=False,
    )
```

```python
import functools

import jax
import jax.numpy as jnp
from jax import lax
from jax.experimental import pallas as pl
from jax.experimental.pallas import tpu as pltpu
from jax.sharding import PartitionSpec as P

HS = 128
CLEN = 64
NLEN = 128
SCALE = HS ** (-0.5)
LAST = (((1,), (1,)), ((), ()))
FIRST = (((0,), (0,)), ((), ()))
MESH = pl.DeviceIdType.MESH
F32 = jnp.float32
BF16 = jnp.bfloat16


def group_index():
    return lax.axis_index("phase") * lax.axis_size("dp") + lax.axis_index("dp")


def peer_id(group):
    dp = lax.axis_size("dp")
    return {"phase": group // dp, "dp": lax.rem(group, dp)}


def greet_group(barrier, groups):
    me = group_index()

    def greet(k, carry):
        pl.semaphore_signal(
            barrier, inc=1, device_id=peer_id(lax.rem(me + k, groups)), device_id_type=MESH
        )
        return carry

    lax.fori_loop(1, groups, greet, 0)


def send_to_group(groups, source, target, send_sem, recv_sem):
    me = group_index()

    def copy_to(k):
        peer = lax.rem(me + k, groups)
        return pltpu.make_async_remote_copy(
            src_ref=source(peer),
            dst_ref=target.at[me],
            send_sem=send_sem,
            recv_sem=recv_sem,
            device_id=peer_id(peer),
            device_id_type=MESH,
        )

    def everything():
        others = target.at[pl.ds(0, groups - 1)]
        return pltpu.make_async_remote_copy(
            src_ref=others,
            dst_ref=others,
            send_sem=send_sem,
            recv_sem=recv_sem,
            device_id=peer_id(lax.rem(me + 1, groups)),
            device_id_type=MESH,
        )

    def arrive():
        everything().wait_recv()

    def leave():
        everything().wait_send()

    return copy_to, arrive, leave


def start_all(groups, copy_to):
    lax.fori_loop(1, groups, lambda k, c: (copy_to(k).start(), c)[1], 0)


def diagonal(slots, first, which, cols):
    top = lax.broadcasted_iota(jnp.int32, (2 * CLEN, HS), 0) < CLEN
    block = slots[pl.ds(first, 2), which, :, cols].reshape(2 * CLEN, HS)
    zero = jnp.zeros_like(block)
    return jnp.concatenate([jnp.where(top, block, zero), jnp.where(top, zero, block)], 1)


def pair_operands(rows, pair, keys, values, slots, first, h):
    cols = pl.ds(h * HS, HS)
    low, high = rows[0, 2 * pair], rows[0, 2 * pair + 1]
    k = jnp.concatenate([keys[low, :, cols], keys[high, :, cols]], 1)
    v = jnp.concatenate([values[low, :, cols], values[high, :, cols]], 1)
    return k, v, diagonal(slots, first, 0, cols), diagonal(slots, first, 1, cols)


def retro_kernel(
    groups, rows, reads, queries, grads, encoded, key_weight, value_weight,
    attended, grad_q, grad_e,
    source, live, rank, order, keep, final, filled,
    query_in, grad_in, outgoing, slots, own, before, after, far, key_w, value_w,
    totals, keys, values, probs, grad_s, grad_p,
    peaks, stats, fetched, combined, back, landed, key_run, value_run, value_sums,
    outs_in, grad_qs_in, cross_grads, pair_sums, cross_w,
    load_sem, ring_send, ring_recv, send_sem, recv_sem, local_sem,
    stat_send, stat_recv, back_send, back_recv,
    sum_send, sum_recv, answer_send, answer_recv, grad_q_send, grad_q_recv, weight_send, weight_recv,
):
    me = group_index()
    z = lax.axis_index("mp")
    ring = lax.axis_size("mp")
    up, down = lax.rem(z + 1, ring), lax.rem(z + ring - 1, ring)
    across = lax.rem(z + 2, ring)
    cross = ring - 1 - z
    partner = z + 1 - 2 * lax.rem(z, 2)
    pair_slot = 2 - lax.rem(z, 2)
    phase, dp = lax.axis_index("phase"), lax.axis_index("dp")
    in_phase = lax.axis_size("dp")
    blocks = encoded.shape[0]
    half = blocks // 2
    key_acc, value_acc, weights = totals.at[0], totals.at[1], totals

    barrier = pltpu.get_barrier_semaphore()
    pl.semaphore_signal(barrier, inc=1, device_id={"mp": up}, device_id_type=MESH)
    pl.semaphore_signal(barrier, inc=1, device_id={"mp": down}, device_id_type=MESH)
    greet_group(barrier, groups)

    inputs = (
        pltpu.make_async_copy(queries, query_in, load_sem.at[9]),
        pltpu.make_async_copy(grads, grad_in, load_sem.at[10]),
    )
    for load in inputs:
        load.start()
    own_load = pltpu.make_async_copy(encoded, own, load_sem.at[0])
    own_load.start()
    weight_loads = []
    for i, owner in enumerate((z, down, up, across)):
        pair = (
            pltpu.make_async_copy(key_weight.at[owner], key_w.at[i], load_sem.at[1 + 2 * i]),
            pltpu.make_async_copy(value_weight.at[owner], value_w.at[i], load_sem.at[2 + 2 * i]),
        )
        for load in pair:
            load.start()
        weight_loads.append(pair)

    def ring_copy(lane, source, target, block, to):
        return pltpu.make_async_remote_copy(
            src_ref=source.at[block],
            dst_ref=target.at[block],
            send_sem=ring_send.at[lane],
            recv_sem=ring_recv.at[lane, block],
            device_id={"mp": to},
            device_id_type=MESH,
        )

    def go_up(c):
        return ring_copy(0, encoded, before, c, up)

    def go_down(c):
        return ring_copy(1, encoded, after, c, down)

    def pass_up(c):
        return ring_copy(2, before, far, c, up)

    def pass_down(c):
        return ring_copy(2, after, far, c, down)

    pl.semaphore_wait(barrier, groups - 1 + 2)

    cross_pair = cross + 1 - 2 * lax.rem(cross, 2)
    their_part = cross * (1 - phase) + cross_pair * phase
    piece_rows = pl.ds(pl.multiple_of(dp * CLEN, CLEN), CLEN)

    def piece_copy(j, weight):
        return pltpu.make_async_remote_copy(
            src_ref=weight.at[their_part, piece_rows],
            dst_ref=cross_w.at[me, j],
            send_sem=weight_send.at[0],
            recv_sem=weight_recv.at[0],
            device_id={"mp": cross},
            device_id_type=MESH,
        )

    def weight_copy(stage, block, to):
        return pltpu.make_async_remote_copy(
            src_ref=cross_w.at[block],
            dst_ref=cross_w.at[block],
            send_sem=weight_send.at[stage],
            recv_sem=weight_recv.at[stage],
            device_id=to,
            device_id_type=MESH,
        )

    side = round(in_phase**0.5)
    x, y = lax.rem(dp, side), dp // side

    def first_line(k):
        return lax.rem(y + k * phase, side) * side + lax.rem(x + k * (1 - phase), side)

    def second_line(k):
        return lax.rem(y + k * (1 - phase), side) * side + lax.rem(x + k * phase, side)

    def spread_first(k, carry):
        weight_copy(1, me, {"dp": first_line(k)}).start()
        return carry

    def spread_second(i, carry):
        piece = phase * in_phase + first_line(i // (side - 1))
        to = second_line(1 + lax.rem(i, side - 1))
        weight_copy(2, piece, {"dp": to}).start()
        return carry

    pieces = weight_copy(0, me, {"mp": cross})
    firsts = weight_copy(1, pl.ds(0, side - 1), {"dp": first_line(1)})
    seconds = weight_copy(2, pl.ds(0, side * (side - 1)), {"dp": second_line(1)})
    halves = weight_copy(3, pl.ds(phase * in_phase, in_phase), {"phase": 1 - phase})
    piece_copy(0, key_weight).start()
    piece_copy(1, value_weight).start()

    def send_own(c, carry):
        go_up(c).start()
        go_down(blocks - 1 - c).start()
        return carry

    lax.fori_loop(0, blocks, send_own, 0)
    spans = queries.shape[0]

    def fill(o, carry):
        span = jnp.int32(0)
        found = jnp.int32(0)
        for t in range(spans):
            for j in range(2):
                hit = (reads[j, t] == o).astype(jnp.int32)
                span = jnp.maximum(span, hit * t)
                found = jnp.maximum(found, hit)
        source[o] = span
        live[o] = found
        for j, array in enumerate((query_in, grad_in)):
            block = array[span]
            outgoing[o, j] = jnp.where(found > 0, block, jnp.zeros_like(block))
        return carry

    for load in inputs:
        load.wait()
    lax.fori_loop(0, groups, fill, 0)
    pieces.wait_recv()
    lax.fori_loop(1, side, spread_first, 0)
    slot_to, slots_arrive, slots_leave = send_to_group(
        groups, lambda g: outgoing.at[g], slots, send_sem, recv_sem
    )
    start_all(groups, slot_to)
    local = pltpu.make_async_copy(outgoing.at[me], slots.at[me], local_sem.at[0])
    local.start()

    def place(o, carry):
        mine = rows[0, o]
        count = jnp.int32(0)
        for other in range(groups):
            theirs = rows[0, other]
            count += (theirs < mine).astype(jnp.int32)
            count += ((theirs == mine) & (other < o)).astype(jnp.int32)
        rank[o] = count
        return carry

    def invert(i, carry):
        slot = jnp.int32(0)
        for o in range(groups):
            slot = jnp.maximum(slot, (rank[o] == i).astype(jnp.int32) * o)
        order[i] = slot
        return carry

    def follow(i, carry):
        same = rows[0, order[i]] == rows[0, order[jnp.maximum(i - 1, 0)]]
        keep[i] = (same & (i > 0)).astype(jnp.int32)
        return carry

    def close(n, carry):
        upto = jnp.int32(0)
        here = jnp.int32(0)
        for o in range(groups):
            upto += (rows[0, o] <= n).astype(jnp.int32)
            here += (rows[0, o] == n).astype(jnp.int32)
        final[n] = jnp.maximum(upto - 1, 0)
        filled[n] = jnp.minimum(here, 1)
        return carry

    lax.fori_loop(0, groups, place, 0)
    lax.fori_loop(0, groups, invert, 0)
    lax.fori_loop(0, groups, follow, 0)
    lax.fori_loop(0, blocks, close, 0)
    firsts.wait_recv()
    lax.fori_loop(0, side * (side - 1), spread_second, 0)

    def project(block, i):
        return (
            jnp.dot(block, key_w[i], preferred_element_type=F32),
            jnp.dot(block, value_w[i], preferred_element_type=F32),
        )

    def add(source, c, i):
        k, v = project(source[c], i)
        key_acc[c] += k
        value_acc[c] += v

    def finish(c):
        k, v = project(far[c], 3)
        keys[c] = (key_acc[c] + k).astype(BF16)
        values[c] = (value_acc[c] + v).astype(BF16)

    own_load.wait()
    for load in weight_loads[0]:
        load.wait()

    def first(c, carry):
        k, v = project(own[c], 0)
        key_acc[c] = k
        value_acc[c] = v
        return carry

    lax.fori_loop(0, blocks, first, 0)
    for pair in weight_loads[1:]:
        for load in pair:
            load.wait()

    def near(c, carry):
        d = blocks - 1 - c
        go_up(c).wait_recv()
        pass_up(c).start()
        go_down(d).wait_recv()
        pass_down(d).start()
        add(before, c, 1)
        add(after, d, 2)
        return carry

    lax.fori_loop(0, half, near, 0)

    def rest(c, carry):
        d = blocks - 1 - c
        go_up(c).wait_recv()
        add(before, c, 1)
        go_down(d).wait_recv()
        add(after, d, 2)
        return carry

    lax.fori_loop(half, blocks, rest, 0)


    def last(c, carry):
        d = blocks - 1 - c
        pass_up(c).wait_recv()
        finish(c)
        pass_down(d).wait_recv()
        finish(d)
        return carry

    lax.fori_loop(0, half, last, 0)

    slots_arrive()
    slots_leave()
    local.wait()
    seconds.wait_recv()
    halves.start()
    width = keys.shape[2]
    heads = width // HS

    def score(p):
        for h in range(heads):
            k, v, q, g = pair_operands(rows, p, keys, values, slots, 2 * p, h)
            scores = lax.dot_general(k, q, LAST, preferred_element_type=F32) * SCALE
            gp = lax.dot_general(v, g, LAST, preferred_element_type=F32)
            peak = jnp.max(scores, 0, keepdims=True)
            w = jnp.exp(scores - peak)
            total = jnp.sum(w, 0, keepdims=True)
            peaks[p, h : h + 1] = peak
            stats[p, h : h + 1] = peak + jnp.log(total)
            stats[p, heads + h : heads + h + 1] = jnp.sum(w * gp, 0, keepdims=True) / total
            weights[p // blocks, p % blocks, :, h * HS : (h + 1) * HS] = w
            grad_p[p, h] = gp

    stat_to, stats_arrive, stats_leave = send_to_group(
        groups, lambda g: stats.at[g // 2], fetched, stat_send, stat_recv
    )
    local_stat = pltpu.make_async_copy(stats.at[me // 2], fetched.at[me], local_sem.at[2])
    together = 2
    chunks = groups // 2 // together

    def score_some(j, carry):
        first = together * lax.rem(me // (2 * together) + j, chunks)
        for u in range(together):
            score(first + u)
        for u in range(2 * together):
            k = lax.rem(2 * first + u + groups - me, groups)

            @pl.when(k > 0)
            def _():
                stat_to(k).start()

            @pl.when(k == 0)
            def _():
                local_stat.start()

        return carry

    lax.fori_loop(0, chunks, score_some, 0)

    def all_sent(lane, source, sem):
        pltpu.make_async_remote_copy(
            src_ref=source,
            dst_ref=source,
            send_sem=sem.at[lane],
            recv_sem=ring_recv.at[0, 0],
            device_id={"mp": up},
            device_id_type=MESH,
        ).wait_send()

    for lane in range(3):
        all_sent(lane, far, ring_send)

    local_stat.wait()
    stats_arrive()

    def combine(t, carry):
        a = fetched[reads[0, t]]
        b = fetched[reads[1, t]]
        overall = jnp.maximum(a[:heads], b[:heads])
        fa, fb = jnp.exp(a[:heads] - overall), jnp.exp(b[:heads] - overall)
        total = fa + fb
        combined[t, :heads] = overall + jnp.log(total)
        combined[t, heads:] = (fa * a[heads:] + fb * b[heads:]) / total
        return carry

    lax.fori_loop(0, spans, combine, 0, unroll=8)
    back_to, backs_arrive, backs_leave = send_to_group(
        groups, lambda g: back.at[g], landed, back_send, back_recv
    )

    def answer(o):
        mine = combined[source[o]]
        back[o] = jnp.where(live[o] > 0, mine, jnp.zeros_like(mine))

    def answer_to(k, carry):
        answer(lax.rem(me + k, groups))
        back_to(k).start()
        return carry

    lax.fori_loop(1, groups, answer_to, 0)
    answer(me)
    local = pltpu.make_async_copy(back.at[me], landed.at[me], local_sem.at[3])
    local.start()
    local.wait()
    backs_arrive()
    left = lax.broadcasted_iota(jnp.int32, landed.shape[1:], 1) < CLEN

    def normalise(p, carry):
        both = jnp.where(left, landed[2 * p], landed[2 * p + 1])
        for h in range(heads):
            factor = jnp.exp(peaks[p, h : h + 1] - both[h : h + 1])
            pr = weights[p // blocks, p % blocks, :, h * HS : (h + 1) * HS] * factor
            probs[p, h] = pr.astype(BF16)
            grad_s[p, h] = (pr * (grad_p[p, h] - both[heads + h : heads + h + 1])).astype(BF16)
        return carry

    lax.fori_loop(0, groups // 2, normalise, 0, unroll=2)

    top = lax.broadcasted_iota(jnp.int32, (2 * CLEN, HS), 0) < CLEN

    def slot_view(buffer, g):
        start = pl.multiple_of(lax.rem(g // 2, 2) * CLEN, CLEN)
        column = pl.multiple_of(lax.rem(g, 2) * width, width)
        return buffer.at[g // 4, pl.ds(start, CLEN), pl.ds(column, width)]

    def answer_all(lefts, rights, scale, buffer):
        def one(p, carry):
            low, high = rows[0, 2 * p], rows[0, 2 * p + 1]
            start = pl.multiple_of(lax.rem(p, 2) * CLEN, CLEN)
            for h in range(heads):
                cols = pl.ds(h * HS, HS)
                right = jnp.concatenate([rights[low, :, cols], rights[high, :, cols]], 1)
                both = lax.dot_general(lefts[p, h], right, FIRST, preferred_element_type=F32)
                picked = (jnp.where(top, both[:, :HS], both[:, HS:]) * scale).astype(BF16)
                buffer[p // 2, pl.ds(start, CLEN), h * HS : (h + 1) * HS] = picked[:CLEN]
                buffer[p // 2, pl.ds(start, CLEN), width + h * HS : width + (h + 1) * HS] = picked[CLEN:]
            return carry

        lax.fori_loop(0, groups // 2, one, 0, unroll=4)

    half_lane = lax.broadcasted_iota(jnp.int32, (NLEN, 2 * CLEN), 1) // CLEN
    key_run[...] = jnp.zeros_like(key_run)
    value_run[...] = jnp.zeros_like(value_run)

    def accumulate(i, carry):
        slot = order[i]
        pair = slot // 2
        mine = half_lane == lax.rem(slot, 2)
        more = keep[i].astype(F32)
        for h in range(heads):
            cols = pl.ds(h * HS, HS)
            zero = jnp.zeros((NLEN, 2 * CLEN), BF16)
            p = jnp.where(mine, probs[pair, h], zero)
            s = jnp.where(mine, grad_s[pair, h], zero)
            q, g = slots[slot, 0, :, cols], slots[slot, 1, :, cols]
            k = key_run[:, cols] * more + jnp.dot(
                s, jnp.concatenate([q, q], 0), preferred_element_type=F32
            )
            v = value_run[:, cols] * more + jnp.dot(
                p, jnp.concatenate([g, g], 0), preferred_element_type=F32
            )
            key_run[:, cols] = k
            value_run[:, cols] = v
            outgoing[i, :, :, cols] = (k * SCALE).astype(BF16).reshape(2, CLEN, HS)
            value_sums[i, :, :, cols] = v.astype(BF16).reshape(2, CLEN, HS)
        return carry

    lax.fori_loop(0, groups, accumulate, 0, unroll=8)
    def gather(n):
        for j, sums in enumerate((outgoing, value_sums)):
            block = sums[final[n]].reshape(NLEN, width)
            far[n, :, j * width : (j + 1) * width] = jnp.where(
                filled[n] > 0, block, jnp.zeros_like(block)
            )


    def own_part(c, i):
        return lax.dot_general(
            far[c, :, :width], key_w[i], LAST, preferred_element_type=F32
        ) + lax.dot_general(far[c, :, width:], value_w[i], LAST, preferred_element_type=F32)

    def cross_part(c, i):
        some = pl.ds(i * in_phase, in_phase)
        shape = (in_phase * CLEN, width)
        return lax.dot_general(
            cross_grads[c, :, :width], cross_w[some, 0].reshape(shape), LAST, preferred_element_type=F32
        ) + lax.dot_general(
            cross_grads[c, :, width:], cross_w[some, 1].reshape(shape), LAST, preferred_element_type=F32
        )

    def sum_copy(lane, source, target, block, to):
        return pltpu.make_async_remote_copy(
            src_ref=source.at[block],
            dst_ref=target.at[block],
            send_sem=sum_send.at[lane],
            recv_sem=sum_recv.at[lane, block],
            device_id={"mp": to},
            device_id_type=MESH,
        )

    to_pair = own

    def cross_copy(c):
        return sum_copy(0, far, cross_grads, c, cross)

    def pair_copy(c):
        return sum_copy(1, to_pair, pair_sums, c, partner)

    def send_cross(c, carry):
        gather(c)
        cross_copy(c).start()
        return carry

    lax.fori_loop(0, blocks, send_cross, 0)
    answer_all(probs, values, 1.0, before)
    out_to, outs_arrive, outs_leave = send_to_group(
        groups, lambda g: slot_view(before, g), outs_in, answer_send, answer_recv
    )
    start_all(groups, out_to)
    local_out = pltpu.make_async_copy(slot_view(before, me), outs_in.at[me], local_sem.at[1])
    local_out.start()
    halves.wait_recv()

    def send_pair(c, carry):
        mine = own_part(c, pair_slot)
        cross_copy(c).wait_recv()
        to_pair[c] = (mine + cross_part(c, 1)).astype(BF16)
        pair_copy(c).start()
        mine = own_part(c, 0) + cross_part(c, 0)
        key_acc[c] = mine[:, :width]
        value_acc[c] = mine[:, width:]
        return carry

    lax.fori_loop(0, 2, send_pair, 0)
    answer_all(grad_s, keys, SCALE, after)
    grad_q_to, grad_qs_arrive, grad_qs_leave = send_to_group(
        groups, lambda g: slot_view(after, g), grad_qs_in, grad_q_send, grad_q_recv
    )
    start_all(groups, grad_q_to)
    local_grad_q = pltpu.make_async_copy(slot_view(after, me), grad_qs_in.at[me], load_sem.at[0])
    local_grad_q.start()
    lax.fori_loop(2, blocks, send_pair, 0)

    def add_pair(c, carry):
        pair_copy(c).wait_recv()
        other = pair_sums[c].astype(F32)
        grad_e[c, :, :width] = (key_acc[c] + other[:, :width]).astype(BF16)
        grad_e[c, :, width:] = (value_acc[c] + other[:, width:]).astype(BF16)
        return carry

    lax.fori_loop(0, blocks, add_pair, 0)
    local_out.wait()
    local_grad_q.wait()
    outs_arrive()
    grad_qs_arrive()
    outs_leave()
    grad_qs_leave()
    stats_leave()
    backs_leave()

    def finish_span(t, carry):
        a, b = reads[0, t], reads[1, t]
        for target, parts in ((attended, outs_in), (grad_q, grad_qs_in)):
            target[t] = (parts[a].astype(F32) + parts[b].astype(F32)).astype(BF16)
        return carry

    lax.fori_loop(0, spans, finish_span, 0)
    for lane in range(2):
        all_sent(lane, far, sum_send)
    for copy in (pieces, firsts, seconds, halves):
        copy.wait_send()


def params(collective_id=None, mib=56):
    return pltpu.CompilerParams(
        collective_id=collective_id,
        has_side_effects=collective_id is not None,
        vmem_limit_bytes=mib << 20,
    )


def body(queries, grad_out, encoded, key_weight, value_weight, send_rows, read_slots):
    groups = lax.axis_size(("phase", "dp"))
    ring = lax.axis_size("mp")
    in_phase = lax.axis_size("dp")
    blocks, _, features = encoded.shape
    width = key_weight.shape[1]
    heads = width // HS
    spans = read_slots.shape[0]
    hbm = pl.BlockSpec(memory_space=pl.ANY)
    vmem = pl.BlockSpec(memory_space=pltpu.VMEM)
    smem = pl.BlockSpec(memory_space=pltpu.SMEM)
    dma = pltpu.SemaphoreType.DMA
    half_pairs = groups // 2

    rows = send_rows.reshape(1, groups)
    reads = read_slots.T
    query_spans = queries.reshape(spans, CLEN, width)
    grad_spans = grad_out.reshape(spans, CLEN, width)
    key_parts = key_weight.reshape(ring, features, width)
    value_parts = value_weight.reshape(ring, features, width)
    block_shape = jax.ShapeDtypeStruct((blocks, NLEN, width), BF16)
    slot_shape = jax.ShapeDtypeStruct((groups, 2, CLEN, width), BF16)
    prob_shape = jax.ShapeDtypeStruct((half_pairs, heads, NLEN, 2 * CLEN), BF16)

    stat_shape = (groups, 2 * heads, 2 * CLEN)
    factor_shape = (groups, 2 * heads, 2 * CLEN)
    span_shape = jax.ShapeDtypeStruct((spans, CLEN, width), BF16)
    attended, grad_q, grad_e = pl.pallas_call(
        functools.partial(retro_kernel, groups),
        out_shape=(
            pltpu.VMEM(span_shape.shape, BF16),
            pltpu.VMEM(span_shape.shape, BF16),
            pltpu.VMEM(encoded.shape, BF16),
        ),
        in_specs=[smem, smem, hbm, hbm, hbm, hbm, hbm],
        out_specs=(vmem, vmem, vmem),
        scratch_shapes=[
            pltpu.SMEM((groups,), jnp.int32),
            pltpu.SMEM((groups,), jnp.int32),
            pltpu.SMEM((groups,), jnp.int32),
            pltpu.SMEM((groups,), jnp.int32),
            pltpu.SMEM((groups,), jnp.int32),
            pltpu.SMEM((blocks,), jnp.int32),
            pltpu.SMEM((blocks,), jnp.int32),
            pltpu.VMEM(span_shape.shape, BF16),
            pltpu.VMEM(span_shape.shape, BF16),
            pltpu.VMEM(slot_shape.shape, BF16),
            pltpu.VMEM(slot_shape.shape, BF16),
            pltpu.VMEM(encoded.shape, BF16),
            pltpu.VMEM(encoded.shape, BF16),
            pltpu.VMEM(encoded.shape, BF16),
            pltpu.VMEM(encoded.shape, BF16),
            pltpu.VMEM(key_parts.shape, BF16),
            pltpu.VMEM(key_parts.shape, BF16),
            pltpu.VMEM((2,) + block_shape.shape, F32),
            pltpu.VMEM(block_shape.shape, BF16),
            pltpu.VMEM(block_shape.shape, BF16),
            pltpu.VMEM(prob_shape.shape, BF16),
            pltpu.VMEM(prob_shape.shape, BF16),
            pltpu.VMEM(prob_shape.shape, F32),
            pltpu.VMEM((half_pairs,) + stat_shape[1:], F32),
            pltpu.VMEM((half_pairs,) + stat_shape[1:], F32),
            pltpu.VMEM(stat_shape, F32),
            pltpu.VMEM((spans,) + factor_shape[1:], F32),
            pltpu.VMEM(factor_shape, F32),
            pltpu.VMEM(factor_shape, F32),
            pltpu.VMEM((NLEN, width), F32),
            pltpu.VMEM((NLEN, width), F32),
            pltpu.VMEM(slot_shape.shape, BF16),
            pltpu.VMEM((groups, CLEN, width), BF16),
            pltpu.VMEM((groups, CLEN, width), BF16),
            pltpu.VMEM(encoded.shape, BF16),
            pltpu.VMEM(encoded.shape, BF16),
            pltpu.VMEM((2 * in_phase, 2, CLEN, width), BF16),
            dma((11,)),
            dma((3,)),
            dma((3, blocks)),
            dma,
            dma,
            dma((4,)),
            dma,
            dma,
            dma,
            dma,
            dma((2,)),
            dma((2, blocks)),
            dma,
            dma,
            dma,
            dma,
            dma((4,)),
            dma((4,)),
        ],
        compiler_params=params(0, 60),
        name="retro",
    )(rows, reads, query_spans, grad_spans, encoded, key_parts, value_parts)
    return (attended.reshape(queries.shape), grad_q.reshape(queries.shape), grad_e)


def solution(mesh):
    return jax.shard_map(
        body,
        mesh=mesh,
        in_specs=(
            P(("phase", "dp"), "mp"),
            P(("phase", "dp"), "mp"),
            P(("phase", "dp"), None, "mp"),
            P(None, "mp"),
            P(None, "mp"),
            P(("phase", "dp"), None, None),
            P(("phase", "dp"), None),
        ),
        out_specs=(
            P(("phase", "dp"), "mp"),
            P(("phase", "dp"), "mp"),
            P(("phase", "dp"), None, "mp"),
        ),
        check_vma=False,
    )
```
